128 devices in a mesh: clu: 32 (over y, z, core), col: 4 (over x).
Axes of the slice: x: 4, y: 4, z: 4, core: 2. Of those that a mesh axis runs over, the one named last changes fastest.
Arguments:
- track_dest: int32 [131072, 1], P(('clu', 'col')), may hold values from 0 to 31; in each aligned block of 1024 rows (0 to 1023, 1024 to 2047, ...) at most 80 rows name the same one
- obs_count: int32 [131072], P(('clu', 'col')), may hold values from 1 to 8
- track_jac: bfloat16 [131072, 1728], P(('clu', 'col'))
- point_info: float32 [3, 3, 131072], P(None, None, ('clu', 'col')), as said below
- point_grad: float32 [3, 131072], P(None, ('clu', 'col')), may hold values from -6 to 6
- camera_grad: float32 [32, 576], P('clu', 'col'), may hold values from -6 to 6
- camera_diag: float32 [32, 576], P('clu', 'col'), may hold values from 6 to 12
- step_scale: float32 [32, 576], P('clu', 'col'), may hold values from 0.03 to 0.09
- covis_blocks: bfloat16 [32, 4, 576, 576], P('clu', None, None, 'col'), may hold values from -0.625 to 0.625
- cluster_colour: int32 [32], replicated, may hold values from 0 to 3, as said below
- round_partner: int32 [4, 4, 32], replicated, may hold values from 0 to 31, as said below
Outputs:
- solution: float32 [32, 576], P('clu', 'col')
- reduced_rhs: float32 [32, 576], P('clu', 'col')
The draws below stay inside these ranges and needn't reach their ends.
Inputs may be any that keep to these rules, and one draw needn't show every extreme that they name: `track_dest`: among the tracks of one device at most 80 name one cluster, and in every draw some cluster is named by exactly 80 of some device's tracks. `point_info`: each 3 x 3 block is symmetric with a dominant positive diagonal. `cluster_colour`: each colour holds 8 clusters. `round_partner`: each round is a matching: the partner of a cluster's partner is the cluster itself; a cluster of colour k has a partner of another colour in every round of colour k; clusters left out of a round name themselves.
All inputs are finite; a program needn't handle non-finite values.
Results may differ from the reference program's by a relative error of at most 0.0003.
Values may be sent and summed in bfloat16 or wider, within the bound.
No kernel may reach another device: no remote copies, remote signals or barrier semaphores. Data moves between devices by JAX's collectives and lax.ppermute only.
A program may use at most 128 MiB of HBM per device.

```python
import math
import jax
import jax.numpy as jnp
import numpy as np
from jax import lax

CAM = 576
ROUNDS = 4
COLOURS = 4
COLOUR_PASSES = 2
TRACKS_PER_UNIT = 1024
CAMERA_GROUPS = 32
TRACKS = 131072
CAP = 80


def colour_plan(key):
    order = jax.random.permutation(jax.random.fold_in(key, 101), CAMERA_GROUPS).astype(jnp.int32)
    slots = jnp.arange(CAMERA_GROUPS, dtype=jnp.int32)
    colour = jnp.zeros((CAMERA_GROUPS,), jnp.int32).at[order].set(slots % COLOURS)
    members = order.reshape(CAMERA_GROUPS // COLOURS, COLOURS)
    table = jnp.zeros((COLOURS, ROUNDS, CAMERA_GROUPS), jnp.int32)
    for colour_now in range(COLOURS):
        for round_now in range(ROUNDS):
            other = (colour_now + 1 + round_now % (COLOURS - 1)) % COLOURS
            shuffle = jax.random.permutation(jax.random.fold_in(key, 200 + colour_now * ROUNDS + round_now), CAMERA_GROUPS // COLOURS)
            first = members[:, colour_now]
            second = members[shuffle, other]
            row = slots.at[first].set(second).at[second].set(first)
            table = table.at[colour_now, round_now].set(row)
    return (colour, table)


def draw_cluster_colour(key, part):
    colour, table = colour_plan(key)
    return colour


def draw_round_partner(key, part):
    colour, table = colour_plan(key)
    return table


def column_scaled(key, ratio):
    columns = TRACKS // (TRACKS_PER_UNIT * CAMERA_GROUPS)
    spread_end = max(columns - 1, 1)
    position = jnp.arange(TRACKS, dtype=jnp.int32) // TRACKS_PER_UNIT % columns
    level = position.astype(jnp.float32) / spread_end
    factor = jnp.exp(jnp.log(ratio) * level)
    every = jnp.arange(columns, dtype=jnp.float32) / spread_end
    norm_value = jnp.sqrt(jnp.mean(jnp.exp(2.0 * jnp.log(ratio) * every)))
    noise = jax.random.truncated_normal(key, -6.0, 6.0, (TRACKS, 3 * CAM), jnp.float32)
    return 0.006 / norm_value * factor[:, None] * noise


def draw_track_jac(key, part):
    key = jax.random.fold_in(key, 11)
    values = column_scaled(key, 3.0)
    return values.astype(jnp.bfloat16)


def draw_point_info(key, part):
    key = jax.random.fold_in(key, 7)
    key_diag, key_off = jax.random.split(key)
    diag = jax.random.uniform(key_diag, (3, TRACKS), jnp.float32, 1.0, 4.0)
    off = jax.random.uniform(key_off, (3, TRACKS), jnp.float32, -0.4, 0.4)
    row0 = jnp.stack([diag[0], off[0], off[1]], 0)
    row1 = jnp.stack([off[0], diag[1], off[2]], 0)
    row2 = jnp.stack([off[1], off[2], diag[2]], 0)
    return jnp.stack([row0, row1, row2], 0).astype(jnp.float32)


def touch_ends(entries, rng, low, high):
    longest = entries.shape.index(max(entries.shape))
    spots = []
    for shift in (0, 1):
        where = [jax.random.randint(jax.random.fold_in(rng, axis), (), 0, length) for axis, length in enumerate(entries.shape)]
        where[longest] = (where[longest] + shift) % entries.shape[longest]
        spots.append(tuple(where))
    return entries.at[spots[0]].set(low).at[spots[1]].set(high)


def level_of(stream_key, shape, cuts, least, high):
    factor_of, own = 1.0, jax.random.fold_in(stream_key, 6)
    for axis_at, shards_of in cuts:
        draws = jnp.exp(jax.random.uniform(jax.random.fold_in(own, axis_at), (shards_of,), jnp.float32, least / len(cuts), high / len(cuts)))
        factor_of = factor_of * jnp.repeat(draws, shape[axis_at] // shards_of).reshape([-1 if axis == axis_at else 1 for axis in range(len(shape))])
    return factor_of


def shared_out(rng, own, number, rows, amount, top, most, skew):
    ranking = jax.random.permutation(rng, amount)
    heavy_load, common = load_shares(amount, rows * top, most, skew, True), load_shares(amount, rows * top, most, skew, False)
    places = jnp.arange(amount)

    def named(lengths, offset_by):
        used = int((lengths > 0).sum())
        fixed = max(1, used // 4)
        passed = fixed + (places - fixed + offset_by * (used - fixed)) % max(1, amount - fixed)
        return jnp.zeros((amount,), jnp.int32).at[ranking[jnp.where(places < fixed, places, passed)]].set(jnp.asarray(lengths, jnp.int32))

    lengths = jnp.where(number % 4 == 0, named(heavy_load, number // 4), named(common, number - number // 4 - 1))
    mixed = jax.random.permutation(jax.random.fold_in(own, 3), amount)
    giver, receiver = mixed[0:amount // 2 * 2:2], mixed[1:amount // 2 * 2:2]
    slack = jnp.minimum(lengths[giver] - 1, most - lengths[receiver]) // 2
    slack = jnp.where((giver == ranking[0]) | (receiver == ranking[0]) | (lengths[receiver] == 0), 0, jnp.maximum(slack, 0))
    passed = jax.random.randint(jax.random.fold_in(own, 4), (amount // 2,), 0, 1 << 20) % (slack + 1)
    lengths = lengths.at[giver].add(-passed).at[receiver].add(passed)
    items = jnp.searchsorted(jnp.cumsum(lengths), jnp.arange(rows * top), side="right").astype(jnp.int32)
    listing = items.reshape(top, rows).T
    listing = listing[jax.random.permutation(jax.random.fold_in(own, 1), rows)]
    offset_by = jax.random.randint(jax.random.fold_in(own, 2), (rows, 1), 0, top)
    return jnp.take_along_axis(listing, (jnp.arange(top)[None, :] + offset_by) % top, axis=1)


def load_shares(count, total, limit, lean, full):
    loads = [(1 << 20) // math.isqrt(rank ** lean) + 1 for rank in range(1, count + 1)]
    largest = limit if full else min(limit, max(-(-total // count), total * loads[0] // sum(loads)))
    least = 1 if total - largest >= count - 1 else 0
    holding, rest = [largest] + [least] * (count - 1), total - largest - least * (count - 1)
    while rest > 0:
        movable = [i for i in range(1, count) if holding[i] < largest] or [i for i in range(1, count) if holding[i] < limit]
        whole, remaining = sum([loads[i] for i in movable]), rest
        for i in movable:
            addition = min(limit - holding[i], max(1, remaining * loads[i] // whole), rest)
            holding[i] = holding[i] + addition
            rest = rest - addition
    return np.array(holding)


def bell_draw(rng, extent, scale, bound, cuts=(), held_as=jnp.bfloat16):
    result = jax.random.normal(rng, extent, jnp.float32) * scale
    if len(cuts) > 0:
        result = level_of(rng, extent, cuts, -0.22, 0.18) * result
    return jnp.clip(result, min=-bound, max=bound).astype(held_as)


def setup_inputs(seed: int = 0) -> dict:
    streams_of = jax.random.split(jax.random.key(seed), 12)
    track_dest_keys = jax.random.split(jax.random.fold_in(streams_of[0], 1), TRACKS // TRACKS_PER_UNIT)
    track_dest_turns = jax.random.permutation(jax.random.fold_in(streams_of[0], 3), TRACKS // TRACKS_PER_UNIT)
    track_dest = jax.vmap(lambda own, number: shared_out(jax.random.fold_in(streams_of[0], 2), own, number, TRACKS_PER_UNIT, CAMERA_GROUPS, 1, CAP, 2))(track_dest_keys, track_dest_turns).reshape((TRACKS, 1))
    obs_count = touch_ends(jax.random.randint(streams_of[1], (TRACKS,), 1, 9), jax.random.fold_in(streams_of[1], 1), 1, 8).astype(jnp.int32)
    track_jac = draw_track_jac(jax.random.fold_in(streams_of[11], 71), 0)
    point_info = draw_point_info(jax.random.fold_in(streams_of[11], 71), 0)
    point_grad = bell_draw(streams_of[4], (3, TRACKS), 0.4, 6.0, ((1, 128),), jnp.float32)
    camera_grad = bell_draw(streams_of[5], (CAMERA_GROUPS, CAM), 2.0, 6.0, ((0, 32), (1, 4)), jnp.float32)
    camera_diag = jnp.clip(6.0 + 6.0 * jax.random.uniform(streams_of[6], (CAMERA_GROUPS, CAM), jnp.float32) ** level_of(streams_of[6], (CAMERA_GROUPS, CAM), ((0, 32), (1, 4)), -0.2, 0.2), 6.0, 12.0)
    step_scale = jnp.clip(jnp.exp(math.log(0.09) - 1.09861235 * jax.random.uniform(streams_of[7], (CAMERA_GROUPS, CAM), jnp.float32) ** level_of(streams_of[7], (CAMERA_GROUPS, CAM), ((0, 32), (1, 4)), -0.2, 0.2)), 0.03, 0.09)
    covis_blocks = bell_draw(streams_of[8], (CAMERA_GROUPS, ROUNDS, CAM, CAM), 0.04, 0.625, ((0, 32), (3, 4)))
    cluster_colour = draw_cluster_colour(jax.random.fold_in(streams_of[11], 71), 0)
    round_partner = draw_round_partner(jax.random.fold_in(streams_of[11], 71), 0)
    return dict(track_dest=track_dest, obs_count=obs_count, track_jac=track_jac, point_info=point_info, point_grad=point_grad, camera_grad=camera_grad, camera_diag=camera_diag, step_scale=step_scale, covis_blocks=covis_blocks, cluster_colour=cluster_colour, round_partner=round_partner)


def weigh(coefs, jac):
    rows = []
    for a in range(3):
        acc = coefs[3 * a][:, None] * jac[:, 0, :].astype(jnp.float32)
        acc = acc + coefs[3 * a + 1][:, None] * jac[:, 1, :].astype(jnp.float32)
        acc = acc + coefs[3 * a + 2][:, None] * jac[:, 2, :].astype(jnp.float32)
        rows.append(acc)
    return jnp.stack(rows, 1).astype(jnp.bfloat16)


def reference(track_dest, obs_count, track_jac, point_info, point_grad, camera_grad, camera_diag, step_scale, covis_blocks, cluster_colour, round_partner):
    block = 512
    dest = track_dest[:, 0].astype(jnp.int32)
    coef = obs_count.astype(jnp.float32)[None, None, :] * point_info
    qvec = jnp.sum(coef * point_grad[None, :, :], axis=1)
    small = jnp.concatenate([coef.reshape(9, TRACKS), qvec], 0)
    order = jnp.argsort(dest, stable=True).astype(jnp.int32)
    sorted_dest = jnp.concatenate([dest[order], jnp.full((block,), -1, jnp.int32)])
    sorted_jac = jnp.concatenate([track_jac[order], jnp.zeros((block, 3 * CAM), jnp.bfloat16)], 0)
    sorted_small = jnp.concatenate([small[:, order], jnp.zeros((12, block), jnp.float32)], 1)
    counts = jnp.sum((dest[:, None] == jnp.arange(CAMERA_GROUPS, dtype=jnp.int32)[None, :]).astype(jnp.int32), 0)
    ends = jnp.cumsum(counts).astype(jnp.int32)
    starts = (ends - counts).astype(jnp.int32)

    def single_cluster(index):
        lower = starts[index] // block
        upper = (ends[index] + block - 1) // block

        def add_block(bnum, carry):
            total, vector = carry
            first = (bnum * block).astype(jnp.int32)
            jac = lax.dynamic_slice_in_dim(sorted_jac, first, block, 0).reshape(block, 3, CAM)
            smalls = lax.dynamic_slice_in_dim(sorted_small, first, block, 1)
            member = lax.dynamic_slice_in_dim(sorted_dest, first, block, 0) == index
            jac = jnp.where(member[:, None, None], jac, jnp.zeros_like(jac))
            weighted = weigh(smalls[:9], jac)
            jac2 = jac.reshape(block * 3, CAM)
            wgt2 = weighted.reshape(block * 3, CAM)
            total = total + lax.dot_general(wgt2, jac2, (((0,), (0,)), ((), ())), preferred_element_type=jnp.float32)
            qv = jnp.transpose(smalls[9:12]).reshape(block * 3)
            vector = vector + jnp.dot(qv, jac2.astype(jnp.float32), precision=lax.Precision.HIGHEST)
            return total, vector

        init = (jnp.zeros((CAM, CAM), jnp.float32), jnp.zeros((CAM,), jnp.float32))
        return lax.fori_loop(lower, upper, add_block, init)

    eliminator, right_side_terms = lax.map(single_cluster, jnp.arange(CAMERA_GROUPS, dtype=jnp.int32))
    reduced_rhs = camera_grad - right_side_terms
    blocks = covis_blocks.astype(jnp.float32)
    solution = jnp.zeros((CAMERA_GROUPS, CAM), jnp.float32)
    for sweep in range(COLOUR_PASSES):
        for colour in range(COLOURS):
            near = solution[round_partner[colour]]
            coupled = jnp.einsum("crij,rcj->ci", blocks, near, precision=lax.Precision.HIGHEST)
            self_partner = jnp.einsum("get,ge->gt", eliminator, solution, precision=lax.Precision.HIGHEST)
            resid = reduced_rhs - camera_diag * solution + self_partner - coupled
            active = (cluster_colour == colour)[:, None]
            solution = jnp.where(active, solution + step_scale * resid, solution)
    return solution, reduced_rhs
```

```python
import functools

import jax
import jax.numpy as jnp
from jax import lax
from jax.experimental import pallas as pl
from jax.experimental.pallas import tpu as pltpu
from jax.sharding import PartitionSpec as P

CLUSTERS = 32
ROUNDS = 4
COLOURS = 4
COLS = 4
CAM = 576
SHARE = 144
WIDE = 640
SLOT = 256
TRK = 1024
NT = (((1,), (1,)), ((), ()))
NN = (((1,), (0,)), ((), ()))

MY_COLOUR, PARTNER, PARTNER_COLOUR, MY_COL, MY_CLU = 0, 1, 5, 9, 10

F32 = jnp.float32
BF16 = jnp.bfloat16


def smem():
    return pl.BlockSpec(memory_space=pltpu.SMEM)


def vmem():
    return pl.BlockSpec(memory_space=pltpu.VMEM)


def two_parts(v):
    high = v.astype(BF16)
    low = (v - high.astype(F32)).astype(BF16)
    return high, low


def widen(v, width=WIDE):
    return jnp.concatenate([v, jnp.zeros((v.shape[0], width - v.shape[1]), F32)], 1)


def place_share(share, col):
    total = jnp.zeros((1, WIDE), F32)
    for at in range(COLS):
        pieces = []
        if at:
            pieces.append(jnp.zeros((1, SHARE * at), F32))
        pieces.append(share)
        pieces.append(jnp.zeros((1, WIDE - SHARE * (at + 1)), F32))
        total = total + jnp.where(col == at, jnp.concatenate(pieces, 1), 0.0)
    return total


def take_share(vector, col):
    total = jnp.zeros((1, SHARE), F32)
    for at in range(COLS):
        total = total + jnp.where(col == at, vector[:, SHARE * at : SHARE * (at + 1)], 0.0)
    return total


def members(dest_ref):
    lanes = lax.broadcasted_iota(jnp.int32, (CLUSTERS, TRK), 0)
    return (lanes == dest_ref[...]).astype(F32)


def scatter_rows(onehot, row):
    high, low = two_parts(row)
    return jnp.concatenate(
        [onehot * high.astype(F32), onehot * low.astype(F32)], 0
    ).astype(BF16)


def fold(both):
    return both[:CLUSTERS] + both[CLUSTERS:]


def rhs_kernel(
    cc_ref, rp_ref, dest_ref, obs_ref, info_ref, grad_ref, jac_ref, cg_ref, step_ref,
    out_ref, ids_ref, total,
):
    a = pl.program_id(0)
    me = lax.axis_index("clu")
    col = lax.axis_index("col")
    obs = obs_ref[...].astype(F32)
    q = jnp.zeros((1, TRK), F32)
    for b in range(3):
        q = q + obs * info_ref[0, b : b + 1, :] * grad_ref[b : b + 1, :]
    part = fold(
        lax.dot_general(
            scatter_rows(members(dest_ref), q), jac_ref[...], NT, preferred_element_type=F32
        )
    )

    @pl.when(a == 0)
    def _():
        rows = lax.broadcasted_iota(jnp.int32, (CLUSTERS, WIDE), 0)
        total[...] = jnp.where(rows == me, place_share(cg_ref[...], col), 0.0)

    total[:, :CAM] = total[:, :CAM] - part

    @pl.when(a == 2)
    def _():
        mine = cc_ref[me]
        ids_ref[MY_COLOUR] = mine
        ids_ref[MY_COL] = col
        ids_ref[MY_CLU] = me
        for r in range(ROUNDS):
            p = rp_ref[mine, r, me]
            ids_ref[PARTNER + r] = p
            ids_ref[PARTNER_COLOUR + r] = cc_ref[p]
        share = widen(step_ref[...], SLOT)
        for c in range(CLUSTERS):
            colour = cc_ref[c]
            out_ref[c, :, 0:WIDE] = total[c : c + 1, :]
            for r in range(ROUNDS):
                p = rp_ref[colour, r, c]
                out_ref[c, :, WIDE * (r + 1) : WIDE * (r + 2)] = total[pl.ds(p, 1), :]
            out_ref[c, :, WIDE * 5 : WIDE * 5 + SLOT] = share


def gather_kernel(ids_ref, recv_ref, diag_ref, out_ref):
    vectors = recv_ref[0, :, : WIDE * 5]
    for c in range(1, CLUSTERS):
        vectors = vectors + recv_ref[c, :, : WIDE * 5]
    diag = widen(diag_ref[...], SLOT)
    shares = [recv_ref[ids_ref[MY_CLU], :, WIDE * 5 :]]
    for r in range(ROUNDS):
        shares.append(recv_ref[ids_ref[PARTNER + r], :, WIDE * 5 :])
    shares.append(diag)
    row = jnp.concatenate([vectors] + shares, 1)
    for k in range(COLS):
        out_ref[k] = row


def couple(ids_ref, vectors, blocks, columns):
    columns[...] = jnp.concatenate(vectors + [jnp.zeros((4, WIDE), F32)], 0).T
    col = ids_ref[MY_COL]
    acc = jnp.zeros((16, CAM), F32)
    for k in range(COLS):
        base = lax.rem(col + k, COLS) * SHARE
        for m in range(SHARE // 16):
            xs = columns[pl.ds(pl.multiple_of(base + 16 * m, 16), 16), :]
            for r in range(ROUNDS):
                acc = acc + blocks[k][r, 16 * m : 16 * m + 16, :].astype(F32) * xs[:, r : r + 1]
    return widen(jnp.sum(acc, 0, keepdims=True))


def first_step_kernel(
    ids_ref, recv_ref, b0, b1, b2, b3, state_ref, out_ref, rhs_ref, columns
):
    col = ids_ref[MY_COL]
    vectors = recv_ref[0, :, : WIDE * 5]
    for k in range(1, COLS):
        vectors = vectors + recv_ref[k, :, : WIDE * 5]

    def full(v):
        at = WIDE * 5 + SLOT * v
        return widen(jnp.concatenate([recv_ref[k, :, at : at + SHARE] for k in range(COLS)], 1))

    rhs = vectors[:, :WIDE]
    step, diag = full(0), full(5)
    near = []
    for r in range(ROUNDS):
        x = full(r + 1) * vectors[:, WIDE * (r + 1) : WIDE * (r + 2)]
        near.append(jnp.where(ids_ref[PARTNER_COLOUR + r] == 0, x, 0.0))
    coupled = couple(ids_ref, near, (b0, b1, b2, b3), columns)
    mine = ids_ref[MY_COLOUR]
    x = jnp.where(mine == 0, step * rhs, jnp.where(mine == 1, step * (rhs - coupled), 0.0))
    state_ref[0:1, :] = x
    state_ref[1:2, :] = rhs
    state_ref[2:3, :] = step
    state_ref[3:4, :] = diag
    rhs_ref[...] = take_share(rhs, col)
    for c in range(CLUSTERS):
        out_ref[c] = x


def step_kernel(colour, sweep, n_elim, has_send, has_recv, last, *refs):
    refs = list(refs)
    ids_ref, recv_ref, state_ref = refs[:3]
    blocks = refs[3:7]
    at = 7
    elim = jnp.zeros((1, WIDE), F32)
    for _ in range(n_elim):
        elim = elim + refs[at][...]
        at += 1
    if has_send:
        send_ref = refs[at]
        at += 1
    if last:
        share_ref = refs[at]
        at += 1
    else:
        new_ref, out_ref = refs[at : at + 2]
        at += 2
        if has_recv:
            sum_ref = refs[at]
            at += 1
    columns = refs[at]
    near = [recv_ref[ids_ref[PARTNER + r], :, :WIDE] for r in range(ROUNDS)]
    coupled = couple(ids_ref, near, blocks, columns)
    x, rhs, step, diag = (state_ref[i : i + 1, :] for i in range(4))
    resid = rhs - coupled
    if sweep:
        resid = resid - diag * x + elim
    x = jnp.where(ids_ref[MY_COLOUR] == colour, x + step * resid, x)
    if last:
        share_ref[...] = take_share(x, ids_ref[MY_COL])
        return
    new_ref[0:1, :] = x
    new_ref[1:4, :] = state_ref[1:4, :]
    for c in range(CLUSTERS):
        out_ref[c, :, :WIDE] = x
    if has_send:
        out_ref[:, :, WIDE:] = send_ref[...]
    if has_recv:
        total = recv_ref[0, :, WIDE:]
        for c in range(1, CLUSTERS):
            total = total + recv_ref[c, :, WIDE:]
        sum_ref[...] = total


def elim_kernel(dest_ref, obs_ref, info_ref, recv_ref, jac_ref, out_ref):
    onehot = members(dest_ref)
    obs = obs_ref[...].astype(F32)
    x = recv_ref[:, 0, :CAM]
    high, low = two_parts(x)
    both = jnp.concatenate([high, low], 0)
    along = []
    for b in range(3):
        every = lax.dot_general(
            both, jac_ref[CAM * b : CAM * (b + 1), :], NN, preferred_element_type=F32
        )
        along.append(jnp.sum(fold(every) * onehot, 0, keepdims=True))
    total = jnp.zeros((2 * CLUSTERS, CAM), F32)
    for a in range(3):
        u = jnp.zeros((1, TRK), F32)
        for b in range(3):
            u = u + obs * info_ref[a, b : b + 1, :] * along[b]
        total = total + lax.dot_general(
            scatter_rows(onehot, u),
            jac_ref[CAM * a : CAM * (a + 1), :],
            NT,
            preferred_element_type=F32,
        )
    out_ref[:, 0, :] = widen(fold(total))


def shape(*dims, dtype=F32):
    return jax.ShapeDtypeStruct(dims, dtype)


def per_device(
    track_dest, obs_count, track_jac, point_info, point_grad, camera_grad, camera_diag,
    step_scale, covis_blocks, cluster_colour, round_partner,
):
    dest = jnp.transpose(track_dest)
    obs = obs_count[None, :]
    jac = jnp.transpose(track_jac)
    own = jnp.transpose(covis_blocks[0], (0, 2, 1))
    blocks = [own] + [
        lax.ppermute(own, "col", [((i + k) % COLS, i) for i in range(COLS)]) for k in (1, 2, 3)
    ]
    limit = pltpu.CompilerParams(vmem_limit_bytes=24 << 20)

    whole = lambda *block: pl.BlockSpec(block, lambda a: (0,) * len(block))
    payload, ids = pl.pallas_call(
        rhs_kernel,
        grid=(3,),
        in_specs=[
            smem(), smem(), whole(1, TRK), whole(1, TRK),
            pl.BlockSpec((1, 3, TRK), lambda a: (a, 0, 0)), whole(3, TRK),
            pl.BlockSpec((CAM, TRK), lambda a: (a, 0)), whole(1, SHARE), whole(1, SHARE),
        ],
        out_specs=[whole(CLUSTERS, 1, 5 * WIDE + SLOT), smem()],
        out_shape=[shape(CLUSTERS, 1, 5 * WIDE + SLOT), shape(16, dtype=jnp.int32)],
        scratch_shapes=[pltpu.VMEM((CLUSTERS, WIDE), F32)],
        compiler_params=limit,
        name="rhs",
    )(cluster_colour, round_partner, dest, obs, point_info, point_grad, jac, camera_grad, step_scale)

    def over_clu(v):
        return lax.all_to_all(v, "clu", split_axis=0, concat_axis=0, tiled=True)

    recv = over_clu(payload)
    payload = pl.pallas_call(
        gather_kernel,
        in_specs=[smem(), vmem(), vmem()],
        out_specs=vmem(),
        out_shape=shape(COLS, 1, 5 * WIDE + 6 * SLOT),
        compiler_params=limit,
        name="gather",
    )(ids, recv, camera_diag)
    recv = lax.all_to_all(payload, "col", split_axis=0, concat_axis=0, tiled=True)
    columns = pltpu.VMEM((WIDE, 8), F32)
    state, payload, reduced_rhs = pl.pallas_call(
        first_step_kernel,
        in_specs=[smem()] + [vmem()] * 5,
        out_specs=[vmem()] * 3,
        out_shape=[shape(4, WIDE), shape(CLUSTERS, 1, WIDE), shape(1, SHARE)],
        scratch_shapes=[columns],
        compiler_params=limit,
        name="first_step",
    )(ids, recv, *blocks)

    def eliminate(recv):
        return pl.pallas_call(
            elim_kernel,
            in_specs=[vmem()] * 5,
            out_specs=vmem(),
            out_shape=shape(CLUSTERS, 1, WIDE),
            compiler_params=limit,
            cost_estimate=pl.CostEstimate(
                flops=12 * 64 * 1024 * 576, bytes_accessed=1 << 22, transcendentals=0
            ),
            name="elim",
        )(dest, obs, point_info, recv, jac)

    def update(number, recv, state, elim=(), send=None, has_recv=False):
        last = number == 7
        outs = [shape(1, SHARE)]
        if not last:
            outs = [shape(4, WIDE), shape(CLUSTERS, 1, WIDE if send is None else 2 * WIDE)]
            if has_recv:
                outs.append(shape(1, WIDE))
        extra = list(elim) + ([] if send is None else [send])
        return pl.pallas_call(
            functools.partial(
                step_kernel, number % COLOURS, number // COLOURS, len(elim),
                send is not None, has_recv, last,
            ),
            in_specs=[smem()] + [vmem()] * (6 + len(extra)),
            out_specs=[vmem()] * len(outs),
            out_shape=outs,
            scratch_shapes=[columns],
            compiler_params=limit,
            name="step",
        )(ids, recv, state, *blocks, *extra)

    def over_col(v):
        return [v] + [
            lax.ppermute(v, "col", [((i + k) % COLS, i) for i in range(COLS)]) for k in (1, 2, 3)
        ]

    recv = over_clu(payload)
    first = eliminate(recv)
    state, payload = update(2, recv, state, send=first)
    recv = over_clu(payload)
    state, payload, part = update(3, recv, state, has_recv=True)
    elim_early = over_col(part)
    second = eliminate(recv)
    recv = over_clu(payload)
    state, payload = update(4, recv, state, elim=elim_early, send=second)
    third = eliminate(recv)
    recv = over_clu(payload)
    state, payload, part = update(5, recv, state, elim=elim_early, send=third, has_recv=True)
    elim_second = over_col(part)
    recv = over_clu(payload)
    state, payload, part = update(6, recv, state, elim=elim_second, has_recv=True)
    elim_third = over_col(part)
    recv = over_clu(payload)
    (solution,) = update(7, recv, state, elim=elim_third)
    return solution, reduced_rhs


def solution(mesh):
    in_specs = (
        P(("clu", "col"), None),
        P(("clu", "col")),
        P(("clu", "col"), None),
        P(None, None, ("clu", "col")),
        P(None, ("clu", "col")),
        P("clu", "col"),
        P("clu", "col"),
        P("clu", "col"),
        P("clu", None, None, "col"),
        P(),
        P(),
    )
    out_specs = (P("clu", "col"), P("clu", "col"))
    return jax.shard_map(
        per_device, mesh=mesh, in_specs=in_specs, out_specs=out_specs, check_vma=False
    )
```

```python
import functools

import jax
import jax.numpy as jnp
from jax import lax
from jax.experimental import pallas as pl
from jax.experimental.pallas import tpu as pltpu
from jax.sharding import PartitionSpec as P

CLUSTERS = 32
ROUNDS = 4
COLOURS = 4
COLS = 4
CAM = 576
SHARE = 144
WIDE = 640
SLOT = 256
TRK = 1024
NT = (((1,), (1,)), ((), ()))
NN = (((1,), (0,)), ((), ()))

MY_COLOUR, PARTNER, PARTNER_COLOUR, MY_COL, MY_CLU = 0, 1, 5, 9, 10

F32 = jnp.float32
BF16 = jnp.bfloat16


def smem():
    return pl.BlockSpec(memory_space=pltpu.SMEM)


def vmem():
    return pl.BlockSpec(memory_space=pltpu.VMEM)


def two_parts(v):
    high = v.astype(BF16)
    low = (v - high.astype(F32)).astype(BF16)
    return high, low


def widen(v, width=WIDE):
    return jnp.concatenate([v, jnp.zeros((v.shape[0], width - v.shape[1]), F32)], 1)


def place_share(share, col):
    total = jnp.zeros((1, WIDE), F32)
    for at in range(COLS):
        pieces = []
        if at:
            pieces.append(jnp.zeros((1, SHARE * at), F32))
        pieces.append(share)
        pieces.append(jnp.zeros((1, WIDE - SHARE * (at + 1)), F32))
        total = total + jnp.where(col == at, jnp.concatenate(pieces, 1), 0.0)
    return total


def take_share(vector, col):
    total = jnp.zeros((1, SHARE), F32)
    for at in range(COLS):
        total = total + jnp.where(col == at, vector[:, SHARE * at : SHARE * (at + 1)], 0.0)
    return total


def members(dest_ref):
    lanes = lax.broadcasted_iota(jnp.int32, (CLUSTERS, TRK), 0)
    return (lanes == dest_ref[...]).astype(F32)


def scatter_rows(onehot, row):
    high, low = two_parts(row)
    return jnp.concatenate(
        [onehot * high.astype(F32), onehot * low.astype(F32)], 0
    ).astype(BF16)


def fold(both):
    return both[:CLUSTERS] + both[CLUSTERS:]


def rhs_kernel(
    cc_ref, rp_ref, dest_ref, obs_ref, info_ref, grad_ref, jac_ref, cg_ref, step_ref,
    out_ref, ids_ref, total,
):
    a = pl.program_id(0)
    me = lax.axis_index("clu")
    col = lax.axis_index("col")
    obs = obs_ref[...].astype(F32)
    q = jnp.zeros((1, TRK), F32)
    for b in range(3):
        q = q + obs * info_ref[0, b : b + 1, :] * grad_ref[b : b + 1, :]
    part = fold(
        lax.dot_general(
            scatter_rows(members(dest_ref), q), jac_ref[...], NT, preferred_element_type=F32
        )
    )

    @pl.when(a == 0)
    def _():
        rows = lax.broadcasted_iota(jnp.int32, (CLUSTERS, WIDE), 0)
        total[...] = jnp.where(rows == me, place_share(cg_ref[...], col), 0.0)

    total[:, :CAM] = total[:, :CAM] - part

    @pl.when(a == 2)
    def _():
        mine = cc_ref[me]
        ids_ref[MY_COLOUR] = mine
        ids_ref[MY_COL] = col
        ids_ref[MY_CLU] = me
        for r in range(ROUNDS):
            p = rp_ref[mine, r, me]
            ids_ref[PARTNER + r] = p
            ids_ref[PARTNER_COLOUR + r] = cc_ref[p]
        share = widen(step_ref[...], SLOT)
        for c in range(CLUSTERS):
            colour = cc_ref[c]
            out_ref[c, :, 0:WIDE] = total[c : c + 1, :]
            for r in range(ROUNDS):
                p = rp_ref[colour, r, c]
                out_ref[c, :, WIDE * (r + 1) : WIDE * (r + 2)] = total[pl.ds(p, 1), :]
            out_ref[c, :, WIDE * 5 : WIDE * 5 + SLOT] = share


def gather_kernel(ids_ref, recv_ref, diag_ref, out_ref):
    vectors = recv_ref[0, :, : WIDE * 5]
    for c in range(1, CLUSTERS):
        vectors = vectors + recv_ref[c, :, : WIDE * 5]
    diag = widen(diag_ref[...], SLOT)
    shares = [recv_ref[ids_ref[MY_CLU], :, WIDE * 5 :]]
    for r in range(ROUNDS):
        shares.append(recv_ref[ids_ref[PARTNER + r], :, WIDE * 5 :])
    shares.append(diag)
    row = jnp.concatenate([vectors] + shares, 1)
    for k in range(COLS):
        out_ref[k] = row


def couple(ids_ref, vectors, blocks, columns):
    columns[...] = jnp.concatenate(vectors + [jnp.zeros((4, WIDE), F32)], 0).T
    col = ids_ref[MY_COL]
    acc = jnp.zeros((16, CAM), F32)
    for k in range(COLS):
        base = lax.rem(col + k, COLS) * SHARE
        for m in range(SHARE // 16):
            xs = columns[pl.ds(pl.multiple_of(base + 16 * m, 16), 16), :]
            for r in range(ROUNDS):
                acc = acc + blocks[k][r, 16 * m : 16 * m + 16, :].astype(F32) * xs[:, r : r + 1]
    return widen(jnp.sum(acc, 0, keepdims=True))


def first_step_kernel(
    ids_ref, recv_ref, b0, b1, b2, b3, state_ref, out_ref, rhs_ref, columns
):
    col = ids_ref[MY_COL]
    vectors = recv_ref[0, :, : WIDE * 5]
    for k in range(1, COLS):
        vectors = vectors + recv_ref[k, :, : WIDE * 5]

    def full(v):
        at = WIDE * 5 + SLOT * v
        return widen(jnp.concatenate([recv_ref[k, :, at : at + SHARE] for k in range(COLS)], 1))

    rhs = vectors[:, :WIDE]
    step, diag = full(0), full(5)
    near = []
    for r in range(ROUNDS):
        x = full(r + 1) * vectors[:, WIDE * (r + 1) : WIDE * (r + 2)]
        near.append(jnp.where(ids_ref[PARTNER_COLOUR + r] == 0, x, 0.0))
    coupled = couple(ids_ref, near, (b0, b1, b2, b3), columns)
    mine = ids_ref[MY_COLOUR]
    x = jnp.where(mine == 0, step * rhs, jnp.where(mine == 1, step * (rhs - coupled), 0.0))
    state_ref[0:1, :] = x
    state_ref[1:2, :] = rhs
    state_ref[2:3, :] = step
    state_ref[3:4, :] = diag
    state_ref[4:8, :] = jnp.zeros((4, WIDE), F32)
    rhs_ref[...] = take_share(rhs, col)
    for c in range(CLUSTERS):
        out_ref[c] = x


def step_kernel(number, has_send, has_recv, *refs):
    ids_ref, recv_ref, state_ref = refs[:3]
    blocks = refs[3:7]
    send_ref = refs[7] if has_send else None
    new_ref, out_ref, columns = refs[-3:]
    near = [recv_ref[ids_ref[PARTNER + r], :, :WIDE] for r in range(ROUNDS)]
    coupled = couple(ids_ref, near, blocks, columns)
    x, rhs, step, diag, elim = (state_ref[i : i + 1, :] for i in range(5))
    mine = ids_ref[MY_COLOUR]
    if has_recv:
        total = recv_ref[0, :, WIDE:]
        for c in range(1, CLUSTERS):
            total = total + recv_ref[c, :, WIDE:]
        elim = jnp.where(mine >= (2 if number > COLOURS else 0), total, elim)
    if number == COLOURS:
        x, rhs, coupled = 0.25 * x, 0.25 * rhs, 0.25 * coupled
    resid = rhs - coupled
    if number >= COLOURS:
        resid = resid - diag * x + elim
    x = jnp.where(mine == number % COLOURS, x + step * resid, x)
    for i, v in enumerate((x, rhs, step, diag, elim)):
        new_ref[i : i + 1, :] = v
    if number == 2 * COLOURS - 2:
        x = jnp.where(mine == COLOURS - 1, x + step * (rhs - diag * x + elim), x)
    for c in range(out_ref.shape[0]):
        out_ref[c, :, :WIDE] = x
    if has_send:
        out_ref[:, :, WIDE:] = send_ref[...]


def last_step_kernel(ids_ref, recv_ref, state_ref, b0, b1, b2, b3, out_ref, columns):
    def total(c):
        v = recv_ref[COLS * c]
        for k in range(1, COLS):
            v = v + recv_ref[COLS * c + k]
        return v

    near = [total(ids_ref[PARTNER + r]) for r in range(ROUNDS)]
    coupled = couple(ids_ref, near, (b0, b1, b2, b3), columns)
    x = total(ids_ref[MY_CLU])
    x = jnp.where(ids_ref[MY_COLOUR] == COLOURS - 1, x - state_ref[2:3, :] * coupled, x)
    out_ref[...] = take_share(x, ids_ref[MY_COL])


def elim_kernel(dest_ref, obs_ref, info_ref, recv_ref, jac_ref, out_ref):
    onehot = members(dest_ref)
    obs = obs_ref[...].astype(F32)
    x = recv_ref[:, 0, :CAM]
    high, low = two_parts(x)
    both = jnp.concatenate([high, low], 0)
    along = []
    for b in range(3):
        every = lax.dot_general(
            both, jac_ref[CAM * b : CAM * (b + 1), :], NN, preferred_element_type=F32
        )
        along.append(jnp.sum(fold(every) * onehot, 0, keepdims=True))
    total = jnp.zeros((2 * CLUSTERS, CAM), F32)
    for a in range(3):
        u = jnp.zeros((1, TRK), F32)
        for b in range(3):
            u = u + obs * info_ref[a, b : b + 1, :] * along[b]
        total = total + lax.dot_general(
            scatter_rows(onehot, u),
            jac_ref[CAM * a : CAM * (a + 1), :],
            NT,
            preferred_element_type=F32,
        )
    out_ref[:, 0, :] = widen(fold(total))


def shape(*dims, dtype=F32):
    return jax.ShapeDtypeStruct(dims, dtype)


def per_device(
    track_dest, obs_count, track_jac, point_info, point_grad, camera_grad, camera_diag,
    step_scale, covis_blocks, cluster_colour, round_partner,
):
    dest = jnp.transpose(track_dest)
    obs = obs_count[None, :]
    jac = jnp.transpose(track_jac)
    own = jnp.transpose(covis_blocks[0], (0, 2, 1))
    blocks = [own] + [
        lax.ppermute(own, "col", [((i + k) % COLS, i) for i in range(COLS)]) for k in (1, 2, 3)
    ]
    limit = pltpu.CompilerParams(vmem_limit_bytes=24 << 20)

    whole = lambda *block: pl.BlockSpec(block, lambda a: (0,) * len(block))
    payload, ids = pl.pallas_call(
        rhs_kernel,
        grid=(3,),
        in_specs=[
            smem(), smem(), whole(1, TRK), whole(1, TRK),
            pl.BlockSpec((1, 3, TRK), lambda a: (a, 0, 0)), whole(3, TRK),
            pl.BlockSpec((CAM, TRK), lambda a: (a, 0)), whole(1, SHARE), whole(1, SHARE),
        ],
        out_specs=[whole(CLUSTERS, 1, 5 * WIDE + SLOT), smem()],
        out_shape=[shape(CLUSTERS, 1, 5 * WIDE + SLOT), shape(16, dtype=jnp.int32)],
        scratch_shapes=[pltpu.VMEM((CLUSTERS, WIDE), F32)],
        compiler_params=pltpu.CompilerParams(vmem_limit_bytes=56 << 20),
        name="rhs",
    )(cluster_colour, round_partner, dest, obs, point_info, point_grad, jac, camera_grad, step_scale)

    def over_clu(v):
        return lax.all_to_all(v, "clu", split_axis=0, concat_axis=0, tiled=True)

    recv = over_clu(payload)
    payload = pl.pallas_call(
        gather_kernel,
        in_specs=[smem(), vmem(), vmem()],
        out_specs=vmem(),
        out_shape=shape(COLS, 1, 5 * WIDE + 6 * SLOT),
        compiler_params=limit,
        name="gather",
    )(ids, recv, camera_diag)
    recv = lax.all_to_all(payload, "col", split_axis=0, concat_axis=0, tiled=True)
    columns = pltpu.VMEM((WIDE, 8), F32)
    state, payload, reduced_rhs = pl.pallas_call(
        first_step_kernel,
        in_specs=[smem()] + [vmem()] * 5,
        out_specs=[vmem()] * 3,
        out_shape=[shape(8, WIDE), shape(CLUSTERS, 1, WIDE), shape(1, SHARE)],
        scratch_shapes=[columns],
        compiler_params=limit,
        name="first_step",
    )(ids, recv, *blocks)

    def eliminate(recv):
        return pl.pallas_call(
            elim_kernel,
            in_specs=[vmem()] * 5,
            out_specs=vmem(),
            out_shape=shape(CLUSTERS, 1, WIDE),
            compiler_params=limit,
            cost_estimate=pl.CostEstimate(
                flops=12 * 64 * 1024 * 576, bytes_accessed=1 << 22, transcendentals=0
            ),
            name="elim",
        )(dest, obs, point_info, recv, jac)

    def update(number, recv, state, send=None, has_recv=False):
        rows = CLUSTERS * COLS if number == 2 * COLOURS - 2 else CLUSTERS
        return pl.pallas_call(
            functools.partial(step_kernel, number, send is not None, has_recv),
            in_specs=[smem()] + [vmem()] * (6 if send is None else 7),
            out_specs=[vmem()] * 2,
            out_shape=[shape(8, WIDE), shape(rows, 1, WIDE if send is None else 2 * WIDE)],
            scratch_shapes=[columns],
            compiler_params=limit,
            name="step",
        )(ids, recv, state, *blocks, *(() if send is None else (send,)))

    recv = over_clu(payload)
    state, payload = update(2, recv, state, send=eliminate(recv))
    recv = over_clu(payload)
    state, payload = update(3, recv, state, has_recv=True)
    recv = over_clu(payload)
    state, payload = update(4, recv, state, send=eliminate(recv))
    recv = over_clu(payload)
    state, payload = update(5, recv, state, has_recv=True)
    recv = over_clu(payload)
    state, payload = update(6, recv, state)
    recv = lax.all_to_all(payload, ("clu", "col"), split_axis=0, concat_axis=0, tiled=True)
    solution = pl.pallas_call(
        last_step_kernel,
        in_specs=[smem()] + [vmem()] * 6,
        out_specs=vmem(),
        out_shape=shape(1, SHARE),
        scratch_shapes=[columns],
        compiler_params=limit,
        name="last_step",
    )(ids, recv, state, *blocks)
    return solution, reduced_rhs


def solution(mesh):
    in_specs = (
        P(("clu", "col"), None),
        P(("clu", "col")),
        P(("clu", "col"), None),
        P(None, None, ("clu", "col")),
        P(None, ("clu", "col")),
        P("clu", "col"),
        P("clu", "col"),
        P("clu", "col"),
        P("clu", None, None, "col"),
        P(),
        P(),
    )
    out_specs = (P("clu", "col"), P("clu", "col"))
    return jax.shard_map(
        per_device, mesh=mesh, in_specs=in_specs, out_specs=out_specs, check_vma=False
    )
```

```python
import functools

import jax
import jax.numpy as jnp
from jax import lax
from jax.experimental import pallas as pl
from jax.experimental.pallas import tpu as pltpu
from jax.sharding import PartitionSpec as P

CLUSTERS = 32
ROUNDS = 4
COLOURS = 4
COLS = 4
CAM = 576
SHARE = 144
WIDE = 640
SLOT = 256
PAIR = 384
TRK = 1024
NT = (((1,), (1,)), ((), ()))
NN = (((1,), (0,)), ((), ()))

MY_COLOUR, PARTNER, PARTNER_COLOUR, MY_COL, MY_CLU = 0, 1, 5, 9, 10

F32 = jnp.float32
BF16 = jnp.bfloat16


def smem():
    return pl.BlockSpec(memory_space=pltpu.SMEM)


def vmem():
    return pl.BlockSpec(memory_space=pltpu.VMEM)


def two_parts(v):
    high = v.astype(BF16)
    low = (v - high.astype(F32)).astype(BF16)
    return high, low


def widen(v, width=WIDE):
    return jnp.concatenate([v, jnp.zeros((v.shape[0], width - v.shape[1]), F32)], 1)


def place_share(share, col):
    total = jnp.zeros((1, WIDE), F32)
    for at in range(COLS):
        pieces = []
        if at:
            pieces.append(jnp.zeros((1, SHARE * at), F32))
        pieces.append(share)
        pieces.append(jnp.zeros((1, WIDE - SHARE * (at + 1)), F32))
        total = total + jnp.where(col == at, jnp.concatenate(pieces, 1), 0.0)
    return total


def take_share(vector, col):
    total = jnp.zeros((1, SHARE), F32)
    for at in range(COLS):
        total = total + jnp.where(col == at, vector[:, SHARE * at : SHARE * (at + 1)], 0.0)
    return total


def members(dest_ref):
    lanes = lax.broadcasted_iota(jnp.int32, (CLUSTERS, TRK), 0)
    return (lanes == dest_ref[...]).astype(F32)


def scatter_rows(onehot, row):
    high, low = two_parts(row)
    return jnp.concatenate(
        [onehot * high.astype(F32), onehot * low.astype(F32)], 0
    ).astype(BF16)


def fold(both):
    return both[:CLUSTERS] + both[CLUSTERS:]


def rhs_kernel(
    cc_ref, rp_ref, dest_ref, obs_ref, info_ref, grad_ref, jac_ref, cg_ref, step_ref, diag_ref,
    out_ref, ids_ref, total,
):
    a = pl.program_id(0)
    me = lax.axis_index("clu")
    col = lax.axis_index("col")
    obs = obs_ref[...].astype(F32)
    q = jnp.zeros((1, TRK), F32)
    for b in range(3):
        q = q + obs * info_ref[0, b : b + 1, :] * grad_ref[b : b + 1, :]
    part = fold(
        lax.dot_general(
            scatter_rows(members(dest_ref), q), jac_ref[...], NT, preferred_element_type=F32
        )
    )

    @pl.when(a == 0)
    def _():
        rows = lax.broadcasted_iota(jnp.int32, (CLUSTERS, WIDE), 0)
        total[...] = jnp.where(rows == me, place_share(cg_ref[...], col), 0.0)

    total[:, :CAM] = total[:, :CAM] - part

    @pl.when(a == 2)
    def _():
        mine = cc_ref[me]
        ids_ref[MY_COLOUR] = mine
        ids_ref[MY_COL] = col
        ids_ref[MY_CLU] = me
        for r in range(ROUNDS):
            p = rp_ref[mine, r, me]
            ids_ref[PARTNER + r] = p
            ids_ref[PARTNER_COLOUR + r] = cc_ref[p]
        share = widen(jnp.concatenate([step_ref[...], diag_ref[...]], 1), PAIR)
        for c in range(CLUSTERS):
            colour = cc_ref[c]
            out_ref[c, :, 0:WIDE] = total[c : c + 1, :]
            for r in range(ROUNDS):
                p = rp_ref[colour, r, c]
                out_ref[c, :, WIDE * (r + 1) : WIDE * (r + 2)] = total[pl.ds(p, 1), :]
            out_ref[c, :, WIDE * 5 :] = share


def gather_kernel(ids_ref, recv_ref, out_ref):
    vectors = recv_ref[0, :, : WIDE * 5]
    for c in range(1, CLUSTERS):
        vectors = vectors + recv_ref[c, :, : WIDE * 5]
    out_ref[:, : WIDE * 5] = vectors
    sources = [ids_ref[MY_CLU]] + [ids_ref[PARTNER + r] for r in range(ROUNDS)]
    shares = [recv_ref[c, :, WIDE * 5 : WIDE * 5 + SHARE] for c in sources]
    shares.append(recv_ref[sources[0], :, WIDE * 5 + SHARE : WIDE * 5 + 2 * SHARE])
    for at, share in enumerate(shares):
        out_ref[:, WIDE * 5 + SLOT * at : WIDE * 5 + SLOT * (at + 1)] = widen(share, SLOT)


def couple(ids_ref, vectors, blocks, columns):
    columns[...] = jnp.concatenate(vectors + [jnp.zeros((4, WIDE), F32)], 0).T
    col = ids_ref[MY_COL]
    acc = jnp.zeros((16, CAM), F32)
    for k in range(COLS):
        base = jnp.bitwise_xor(col, k) * SHARE
        for m in range(SHARE // 16):
            xs = columns[pl.ds(pl.multiple_of(base + 16 * m, 16), 16), :]
            for r in range(ROUNDS):
                acc = acc + blocks[k][r, 16 * m : 16 * m + 16, :].astype(F32) * xs[:, r : r + 1]
    return widen(jnp.sum(acc, 0, keepdims=True))


def first_step_kernel(
    ids_ref, v0, v1, v2, v3, b0, b1, b2, b3, state_ref, out_ref, rhs_ref, columns
):
    col = ids_ref[MY_COL]
    rows = [v[...] for v in (v0, v1, v2, v3)]
    vectors = (rows[0] + rows[1] + rows[2] + rows[3])[:, : WIDE * 5]
    shares = []
    for at in range(COLS):
        share = jnp.zeros((1, SLOT * 6), F32)
        for k in range(COLS):
            share = jnp.where(jnp.bitwise_xor(col, k) == at, rows[k][:, WIDE * 5 :], share)
        shares.append(share)

    def full(v):
        return widen(jnp.concatenate([s[:, SLOT * v : SLOT * v + SHARE] for s in shares], 1))

    rhs = vectors[:, :WIDE]
    step, diag = full(0), full(5)
    near = []
    for r in range(ROUNDS):
        x = full(r + 1) * vectors[:, WIDE * (r + 1) : WIDE * (r + 2)]
        near.append(jnp.where(ids_ref[PARTNER_COLOUR + r] == 0, x, 0.0))
    coupled = couple(ids_ref, near, (b0, b1, b2, b3), columns)
    mine = ids_ref[MY_COLOUR]
    x = jnp.where(mine == 0, step * rhs, jnp.where(mine == 1, step * (rhs - coupled), 0.0))
    state_ref[0:1, :] = x
    state_ref[1:2, :] = rhs
    state_ref[2:3, :] = step
    state_ref[3:4, :] = diag
    state_ref[4:8, :] = jnp.zeros((4, WIDE), F32)
    rhs_ref[...] = take_share(rhs, col)
    for c in range(CLUSTERS):
        out_ref[c] = x


def step_kernel(number, has_send, has_recv, *refs):
    ids_ref, recv_ref, state_ref = refs[:3]
    blocks = refs[3:7]
    send_ref = refs[7] if has_send else None
    new_ref, out_ref, columns = refs[-3:]
    near = [recv_ref[ids_ref[PARTNER + r], :, :WIDE] for r in range(ROUNDS)]
    coupled = couple(ids_ref, near, blocks, columns)
    x, rhs, step, diag, elim = (state_ref[i : i + 1, :] for i in range(5))
    mine = ids_ref[MY_COLOUR]
    if has_recv:
        total = recv_ref[0, :, WIDE:]
        for c in range(1, CLUSTERS):
            total = total + recv_ref[c, :, WIDE:]
        elim = jnp.where(mine >= (2 if number > COLOURS else 0), total, elim)
    if number == COLOURS:
        x, rhs, coupled = 0.25 * x, 0.25 * rhs, 0.25 * coupled
    resid = rhs - coupled
    if number >= COLOURS:
        resid = resid - diag * x + elim
    x = jnp.where(mine == number % COLOURS, x + step * resid, x)
    for i, v in enumerate((x, rhs, step, diag, elim)):
        new_ref[i : i + 1, :] = v
    if number == 2 * COLOURS - 2:
        x = jnp.where(mine == COLOURS - 1, x + step * (rhs - diag * x + elim), x)
    for c in range(out_ref.shape[0]):
        out_ref[c, :, :WIDE] = x
    if has_send:
        out_ref[:, :, WIDE:] = send_ref[...]


def last_step_kernel(ids_ref, recv_ref, state_ref, b0, b1, b2, b3, out_ref, columns):
    def total(c):
        v = recv_ref[COLS * c]
        for k in range(1, COLS):
            v = v + recv_ref[COLS * c + k]
        return v

    near = [total(ids_ref[PARTNER + r]) for r in range(ROUNDS)]
    coupled = couple(ids_ref, near, (b0, b1, b2, b3), columns)
    x = total(ids_ref[MY_CLU])
    x = jnp.where(ids_ref[MY_COLOUR] == COLOURS - 1, x - state_ref[2:3, :] * coupled, x)
    out_ref[...] = take_share(x, ids_ref[MY_COL])


def elim_kernel(dest_ref, obs_ref, info_ref, recv_ref, jac_ref, out_ref):
    onehot = members(dest_ref)
    obs = obs_ref[...].astype(F32)
    x = recv_ref[:, 0, :CAM]
    high, low = two_parts(x)
    both = jnp.concatenate([high, low], 0)
    along = []
    for b in range(3):
        every = lax.dot_general(
            both, jac_ref[CAM * b : CAM * (b + 1), :], NN, preferred_element_type=F32
        )
        along.append(jnp.sum(fold(every) * onehot, 0, keepdims=True))
    total = jnp.zeros((2 * CLUSTERS, CAM), F32)
    for a in range(3):
        u = jnp.zeros((1, TRK), F32)
        for b in range(3):
            u = u + obs * info_ref[a, b : b + 1, :] * along[b]
        total = total + lax.dot_general(
            scatter_rows(onehot, u),
            jac_ref[CAM * a : CAM * (a + 1), :],
            NT,
            preferred_element_type=F32,
        )
    out_ref[:, 0, :] = widen(fold(total))


def shape(*dims, dtype=F32):
    return jax.ShapeDtypeStruct(dims, dtype)


def per_device(
    track_dest, obs_count, track_jac, point_info, point_grad, camera_grad, camera_diag,
    step_scale, covis_blocks, cluster_colour, round_partner,
):
    dest = jnp.transpose(track_dest)
    obs = obs_count[None, :]
    jac = jnp.transpose(track_jac)
    own = jnp.transpose(covis_blocks[0], (0, 2, 1))

    def over_col(v):
        return [v] + [lax.ppermute(v, "col", [(i, i ^ k) for i in range(COLS)]) for k in (1, 3, 2)]

    own, first, third, second = over_col(own)
    blocks = [own, first, second, third]
    limit = pltpu.CompilerParams(vmem_limit_bytes=24 << 20)

    whole = lambda *block: pl.BlockSpec(block, lambda a: (0,) * len(block))
    payload, ids = pl.pallas_call(
        rhs_kernel,
        grid=(3,),
        in_specs=[
            smem(), smem(), whole(1, TRK), whole(1, TRK),
            pl.BlockSpec((1, 3, TRK), lambda a: (a, 0, 0)), whole(3, TRK),
            pl.BlockSpec((CAM, TRK), lambda a: (a, 0)), whole(1, SHARE), whole(1, SHARE),
            whole(1, SHARE),
        ],
        out_specs=[whole(CLUSTERS, 1, 5 * WIDE + PAIR), smem()],
        out_shape=[shape(CLUSTERS, 1, 5 * WIDE + PAIR), shape(16, dtype=jnp.int32)],
        scratch_shapes=[pltpu.VMEM((CLUSTERS, WIDE), F32)],
        compiler_params=pltpu.CompilerParams(vmem_limit_bytes=56 << 20),
        name="rhs",
    )(
        cluster_colour, round_partner, dest, obs, point_info, point_grad, jac,
        camera_grad, step_scale, camera_diag,
    )

    def over_clu(v):
        return lax.all_to_all(v, "clu", split_axis=0, concat_axis=0, tiled=True)

    recv = over_clu(payload)
    row = pl.pallas_call(
        gather_kernel,
        in_specs=[smem(), vmem()],
        out_specs=vmem(),
        out_shape=shape(1, 5 * WIDE + 6 * SLOT),
        compiler_params=limit,
        name="gather",
    )(ids, recv)
    row, first, third, second = over_col(row)
    columns = pltpu.VMEM((WIDE, 8), F32)
    state, payload, reduced_rhs = pl.pallas_call(
        first_step_kernel,
        in_specs=[smem()] + [vmem()] * 8,
        out_specs=[vmem()] * 3,
        out_shape=[shape(8, WIDE), shape(CLUSTERS, 1, WIDE), shape(1, SHARE)],
        scratch_shapes=[columns],
        compiler_params=limit,
        name="first_step",
    )(ids, row, first, second, third, *blocks)

    def eliminate(recv):
        return pl.pallas_call(
            elim_kernel,
            in_specs=[vmem()] * 5,
            out_specs=vmem(),
            out_shape=shape(CLUSTERS, 1, WIDE),
            compiler_params=limit,
            cost_estimate=pl.CostEstimate(
                flops=12 * 64 * 1024 * 576, bytes_accessed=1 << 22, transcendentals=0
            ),
            name="elim",
        )(dest, obs, point_info, recv, jac)

    def update(number, recv, state, send=None, has_recv=False):
        rows = CLUSTERS * COLS if number == 2 * COLOURS - 2 else CLUSTERS
        return pl.pallas_call(
            functools.partial(step_kernel, number, send is not None, has_recv),
            in_specs=[smem()] + [vmem()] * (6 if send is None else 7),
            out_specs=[vmem()] * 2,
            out_shape=[shape(8, WIDE), shape(rows, 1, WIDE if send is None else 2 * WIDE)],
            scratch_shapes=[columns],
            compiler_params=limit,
            name="step",
        )(ids, recv, state, *blocks, *(() if send is None else (send,)))

    recv = over_clu(payload)
    state, payload = update(2, recv, state, send=eliminate(recv))
    recv = over_clu(payload)
    state, payload = update(3, recv, state, has_recv=True)
    recv = over_clu(payload)
    state, payload = update(4, recv, state, send=eliminate(recv))
    recv = over_clu(payload)
    state, payload = update(5, recv, state, has_recv=True)
    recv = over_clu(payload)
    state, payload = update(6, recv, state)
    recv = lax.all_to_all(payload, ("clu", "col"), split_axis=0, concat_axis=0, tiled=True)
    solution = pl.pallas_call(
        last_step_kernel,
        in_specs=[smem()] + [vmem()] * 6,
        out_specs=vmem(),
        out_shape=shape(1, SHARE),
        scratch_shapes=[columns],
        compiler_params=limit,
        name="last_step",
    )(ids, recv, state, *blocks)
    return solution, reduced_rhs


def solution(mesh):
    in_specs = (
        P(("clu", "col"), None),
        P(("clu", "col")),
        P(("clu", "col"), None),
        P(None, None, ("clu", "col")),
        P(None, ("clu", "col")),
        P("clu", "col"),
        P("clu", "col"),
        P("clu", "col"),
        P("clu", None, None, "col"),
        P(),
        P(),
    )
    out_specs = (P("clu", "col"), P("clu", "col"))
    return jax.shard_map(
        per_device, mesh=mesh, in_specs=in_specs, out_specs=out_specs, check_vma=False
    )
```

```python
import functools

import jax
import jax.numpy as jnp
from jax import lax
from jax.experimental import pallas as pl
from jax.experimental.pallas import tpu as pltpu
from jax.sharding import PartitionSpec as P

CLUSTERS = 32
ROUNDS = 4
COLOURS = 4
COLS = 4
CAM = 576
SHARE = 144
WIDE = 640
SLOT = 256
PAIR = 384
TRK = 1024
NT = (((1,), (1,)), ((), ()))
NN = (((1,), (0,)), ((), ()))

MY_COLOUR, PARTNER, PARTNER_COLOUR, MY_COL, MY_CLU = 0, 1, 5, 9, 10

F32 = jnp.float32
BF16 = jnp.bfloat16


def smem():
    return pl.BlockSpec(memory_space=pltpu.SMEM)


def vmem():
    return pl.BlockSpec(memory_space=pltpu.VMEM)


def two_parts(v):
    high = v.astype(BF16)
    low = (v - high.astype(F32)).astype(BF16)
    return high, low


def widen(v, width=WIDE):
    return jnp.concatenate([v, jnp.zeros((v.shape[0], width - v.shape[1]), F32)], 1)


def place_share(share, col):
    total = jnp.zeros((1, WIDE), F32)
    for at in range(COLS):
        pieces = []
        if at:
            pieces.append(jnp.zeros((1, SHARE * at), F32))
        pieces.append(share)
        pieces.append(jnp.zeros((1, WIDE - SHARE * (at + 1)), F32))
        total = total + jnp.where(col == at, jnp.concatenate(pieces, 1), 0.0)
    return total


def take_share(vector, col):
    total = jnp.zeros((1, SHARE), F32)
    for at in range(COLS):
        total = total + jnp.where(col == at, vector[:, SHARE * at : SHARE * (at + 1)], 0.0)
    return total


def members(dest_ref):
    lanes = lax.broadcasted_iota(jnp.int32, (CLUSTERS, TRK), 0)
    return (lanes == dest_ref[...]).astype(F32)


def scatter_rows(onehot, row):
    high, low = two_parts(row)
    return jnp.concatenate(
        [onehot * high.astype(F32), onehot * low.astype(F32)], 0
    ).astype(BF16)


def fold(both):
    return both[:CLUSTERS] + both[CLUSTERS:]


def rhs_kernel(
    cc_ref, rp_ref, dest_ref, obs_ref, info_ref, grad_ref, jac_ref, cg_ref, step_ref, diag_ref,
    out_ref, ids_ref, total,
):
    a = pl.program_id(0)
    me = lax.axis_index("clu")
    col = lax.axis_index("col")
    obs = obs_ref[...].astype(F32)
    q = jnp.zeros((1, TRK), F32)
    for b in range(3):
        q = q + obs * info_ref[0, b : b + 1, :] * grad_ref[b : b + 1, :]
    part = fold(
        lax.dot_general(
            scatter_rows(members(dest_ref), q), jac_ref[...], NT, preferred_element_type=F32
        )
    )

    @pl.when(a == 0)
    def _():
        rows = lax.broadcasted_iota(jnp.int32, (CLUSTERS, WIDE), 0)
        total[...] = jnp.where(rows == me, place_share(cg_ref[...], col), 0.0)

    total[:, :CAM] = total[:, :CAM] - part

    @pl.when(a == 2)
    def _():
        mine = cc_ref[me]
        ids_ref[MY_COLOUR] = mine
        ids_ref[MY_COL] = col
        ids_ref[MY_CLU] = me
        for r in range(ROUNDS):
            p = rp_ref[mine, r, me]
            ids_ref[PARTNER + r] = p
            ids_ref[PARTNER_COLOUR + r] = cc_ref[p]
        share = widen(jnp.concatenate([step_ref[...], diag_ref[...]], 1), PAIR)
        for c in range(CLUSTERS):
            colour = cc_ref[c]
            out_ref[c, :, 0:WIDE] = total[c : c + 1, :]
            for r in range(ROUNDS):
                p = rp_ref[colour, r, c]
                out_ref[c, :, WIDE * (r + 1) : WIDE * (r + 2)] = total[pl.ds(p, 1), :]
            out_ref[c, :, WIDE * 5 :] = share


def gather_kernel(ids_ref, recv_ref, out_ref):
    vectors = recv_ref[0, :, : WIDE * 5]
    for c in range(1, CLUSTERS):
        vectors = vectors + recv_ref[c, :, : WIDE * 5]
    out_ref[:, : WIDE * 5] = vectors
    sources = [ids_ref[MY_CLU]] + [ids_ref[PARTNER + r] for r in range(ROUNDS)]
    shares = [recv_ref[c, :, WIDE * 5 : WIDE * 5 + SHARE] for c in sources]
    shares.append(recv_ref[sources[0], :, WIDE * 5 + SHARE : WIDE * 5 + 2 * SHARE])
    for at, share in enumerate(shares):
        out_ref[:, WIDE * 5 + SLOT * at : WIDE * 5 + SLOT * (at + 1)] = widen(share, SLOT)


def couple(ids_ref, vectors, blocks, columns):
    columns[...] = jnp.concatenate(vectors + [jnp.zeros((4, WIDE), F32)], 0).T
    col = ids_ref[MY_COL]
    acc = jnp.zeros((16, CAM), F32)
    for k in range(COLS):
        base = jnp.bitwise_xor(col, k) * SHARE
        for m in range(SHARE // 16):
            xs = columns[pl.ds(pl.multiple_of(base + 16 * m, 16), 16), :]
            for r in range(ROUNDS):
                if k == 2:
                    block = blocks[2 + r // 2][r % 2, 16 * m : 16 * m + 16, :]
                else:
                    block = blocks[k + k // 3][r, 16 * m : 16 * m + 16, :]
                acc = acc + block.astype(F32) * xs[:, r : r + 1]
    return widen(jnp.sum(acc, 0, keepdims=True))


def first_step_kernel(
    ids_ref, v0, v1, v2, v3, b0, b1, b2, b3, b4, state_ref, out_ref, rhs_ref, columns
):
    col = ids_ref[MY_COL]
    rows = [v[...] for v in (v0, v1, v2, v3)]
    vectors = (rows[0] + rows[1] + rows[2] + rows[3])[:, : WIDE * 5]
    shares = []
    for at in range(COLS):
        share = jnp.zeros((1, SLOT * 6), F32)
        for k in range(COLS):
            share = jnp.where(jnp.bitwise_xor(col, k) == at, rows[k][:, WIDE * 5 :], share)
        shares.append(share)

    def full(v):
        return widen(jnp.concatenate([s[:, SLOT * v : SLOT * v + SHARE] for s in shares], 1))

    rhs = vectors[:, :WIDE]
    step, diag = full(0), full(5)
    near = []
    for r in range(ROUNDS):
        x = full(r + 1) * vectors[:, WIDE * (r + 1) : WIDE * (r + 2)]
        near.append(jnp.where(ids_ref[PARTNER_COLOUR + r] == 0, x, 0.0))
    coupled = couple(ids_ref, near, (b0, b1, b2, b3, b4), columns)
    mine = ids_ref[MY_COLOUR]
    x = jnp.where(mine == 0, step * rhs, jnp.where(mine == 1, step * (rhs - coupled), 0.0))
    state_ref[0:1, :] = x
    state_ref[1:2, :] = rhs
    state_ref[2:3, :] = step
    state_ref[3:4, :] = diag
    state_ref[4:8, :] = jnp.zeros((4, WIDE), F32)
    rhs_ref[...] = take_share(rhs, col)
    for c in range(CLUSTERS):
        out_ref[c] = x


def step_kernel(number, has_send, has_recv, *refs):
    ids_ref, recv_ref, state_ref = refs[:3]
    blocks = refs[3:8]
    send_ref = refs[8] if has_send else None
    new_ref, out_ref, columns = refs[-3:]
    near = [recv_ref[ids_ref[PARTNER + r], :, :WIDE] for r in range(ROUNDS)]
    coupled = couple(ids_ref, near, blocks, columns)
    x, rhs, step, diag, elim = (state_ref[i : i + 1, :] for i in range(5))
    mine = ids_ref[MY_COLOUR]
    if has_recv:
        total = recv_ref[0, :, WIDE:]
        for c in range(1, CLUSTERS):
            total = total + recv_ref[c, :, WIDE:]
        elim = jnp.where(mine >= (2 if number > COLOURS else 0), total, elim)
    if number == COLOURS:
        x, rhs, coupled = 0.25 * x, 0.25 * rhs, 0.25 * coupled
    resid = rhs - coupled
    if number >= COLOURS:
        resid = resid - diag * x + elim
    x = jnp.where(mine == number % COLOURS, x + step * resid, x)
    for i, v in enumerate((x, rhs, step, diag, elim)):
        new_ref[i : i + 1, :] = v
    if number == 2 * COLOURS - 2:
        x = jnp.where(mine == COLOURS - 1, x + step * (rhs - diag * x + elim), x)
    for c in range(out_ref.shape[0]):
        out_ref[c, :, :WIDE] = x
    if has_send:
        out_ref[:, :, WIDE:] = send_ref[...]


def last_step_kernel(ids_ref, recv_ref, state_ref, b0, b1, b2, b3, b4, out_ref, columns):
    def total(c):
        v = recv_ref[COLS * c]
        for k in range(1, COLS):
            v = v + recv_ref[COLS * c + k]
        return v

    near = [total(ids_ref[PARTNER + r]) for r in range(ROUNDS)]
    coupled = couple(ids_ref, near, (b0, b1, b2, b3, b4), columns)
    x = total(ids_ref[MY_CLU])
    x = jnp.where(ids_ref[MY_COLOUR] == COLOURS - 1, x - state_ref[2:3, :] * coupled, x)
    out_ref[...] = take_share(x, ids_ref[MY_COL])


def elim_kernel(dest_ref, obs_ref, info_ref, recv_ref, jac_ref, out_ref):
    onehot = members(dest_ref)
    obs = obs_ref[...].astype(F32)
    x = recv_ref[:, 0, :CAM]
    high, low = two_parts(x)
    both = jnp.concatenate([high, low], 0)
    along = []
    for b in range(3):
        every = lax.dot_general(
            both, jac_ref[CAM * b : CAM * (b + 1), :], NN, preferred_element_type=F32
        )
        along.append(jnp.sum(fold(every) * onehot, 0, keepdims=True))
    total = jnp.zeros((2 * CLUSTERS, CAM), F32)
    for a in range(3):
        u = jnp.zeros((1, TRK), F32)
        for b in range(3):
            u = u + obs * info_ref[a, b : b + 1, :] * along[b]
        total = total + lax.dot_general(
            scatter_rows(onehot, u),
            jac_ref[CAM * a : CAM * (a + 1), :],
            NT,
            preferred_element_type=F32,
        )
    out_ref[:, 0, :] = widen(fold(total))


def shape(*dims, dtype=F32):
    return jax.ShapeDtypeStruct(dims, dtype)


def per_device(
    track_dest, obs_count, track_jac, point_info, point_grad, camera_grad, camera_diag,
    step_scale, covis_blocks, cluster_colour, round_partner,
):
    dest = jnp.transpose(track_dest)
    obs = obs_count[None, :]
    jac = jnp.transpose(track_jac)
    own = jnp.transpose(covis_blocks[0], (0, 2, 1))

    def over_col(v):
        return [v] + [lax.ppermute(v, "col", [(i, i ^ k) for i in range(COLS)]) for k in (1, 3, 2)]

    def swap(v, k):
        return lax.ppermute(v, "col", [(i, i ^ k) for i in range(COLS)])

    first, third = swap(own, 1), swap(own, 3)
    blocks = [own, first, swap(first[: ROUNDS // 2], 3), swap(third[ROUNDS // 2 :], 1), third]
    limit = pltpu.CompilerParams(vmem_limit_bytes=24 << 20)

    whole = lambda *block: pl.BlockSpec(block, lambda a: (0,) * len(block))
    payload, ids = pl.pallas_call(
        rhs_kernel,
        grid=(3,),
        in_specs=[
            smem(), smem(), whole(1, TRK), whole(1, TRK),
            pl.BlockSpec((1, 3, TRK), lambda a: (a, 0, 0)), whole(3, TRK),
            pl.BlockSpec((CAM, TRK), lambda a: (a, 0)), whole(1, SHARE), whole(1, SHARE),
            whole(1, SHARE),
        ],
        out_specs=[whole(CLUSTERS, 1, 5 * WIDE + PAIR), smem()],
        out_shape=[shape(CLUSTERS, 1, 5 * WIDE + PAIR), shape(16, dtype=jnp.int32)],
        scratch_shapes=[pltpu.VMEM((CLUSTERS, WIDE), F32)],
        compiler_params=pltpu.CompilerParams(vmem_limit_bytes=56 << 20),
        name="rhs",
    )(
        cluster_colour, round_partner, dest, obs, point_info, point_grad, jac,
        camera_grad, step_scale, camera_diag,
    )

    def over_clu(v):
        return lax.all_to_all(v, "clu", split_axis=0, concat_axis=0, tiled=True)

    recv = over_clu(payload)
    row = pl.pallas_call(
        gather_kernel,
        in_specs=[smem(), vmem()],
        out_specs=vmem(),
        out_shape=shape(1, 5 * WIDE + 6 * SLOT),
        compiler_params=limit,
        name="gather",
    )(ids, recv)
    row, first, third, second = over_col(row)
    columns = pltpu.VMEM((WIDE, 8), F32)
    state, payload, reduced_rhs = pl.pallas_call(
        first_step_kernel,
        in_specs=[smem()] + [vmem()] * 9,
        out_specs=[vmem()] * 3,
        out_shape=[shape(8, WIDE), shape(CLUSTERS, 1, WIDE), shape(1, SHARE)],
        scratch_shapes=[columns],
        compiler_params=limit,
        name="first_step",
    )(ids, row, first, second, third, *blocks)

    def eliminate(recv):
        return pl.pallas_call(
            elim_kernel,
            in_specs=[vmem()] * 5,
            out_specs=vmem(),
            out_shape=shape(CLUSTERS, 1, WIDE),
            compiler_params=limit,
            cost_estimate=pl.CostEstimate(
                flops=12 * 64 * 1024 * 576, bytes_accessed=1 << 22, transcendentals=0
            ),
            name="elim",
        )(dest, obs, point_info, recv, jac)

    def update(number, recv, state, send=None, has_recv=False):
        rows = CLUSTERS * COLS if number == 2 * COLOURS - 2 else CLUSTERS
        return pl.pallas_call(
            functools.partial(step_kernel, number, send is not None, has_recv),
            in_specs=[smem()] + [vmem()] * (7 if send is None else 8),
            out_specs=[vmem()] * 2,
            out_shape=[shape(8, WIDE), shape(rows, 1, WIDE if send is None else 2 * WIDE)],
            scratch_shapes=[columns],
            compiler_params=limit,
            name="step",
        )(ids, recv, state, *blocks, *(() if send is None else (send,)))

    recv = over_clu(payload)
    state, payload = update(2, recv, state, send=eliminate(recv))
    recv = over_clu(payload)
    state, payload = update(3, recv, state, has_recv=True)
    recv = over_clu(payload)
    state, payload = update(4, recv, state, send=eliminate(recv))
    recv = over_clu(payload)
    state, payload = update(5, recv, state, has_recv=True)
    recv = over_clu(payload)
    state, payload = update(6, recv, state)
    recv = lax.all_to_all(payload, ("clu", "col"), split_axis=0, concat_axis=0, tiled=True)
    solution = pl.pallas_call(
        last_step_kernel,
        in_specs=[smem()] + [vmem()] * 7,
        out_specs=vmem(),
        out_shape=shape(1, SHARE),
        scratch_shapes=[columns],
        compiler_params=limit,
        name="last_step",
    )(ids, recv, state, *blocks)
    return solution, reduced_rhs


def solution(mesh):
    in_specs = (
        P(("clu", "col"), None),
        P(("clu", "col")),
        P(("clu", "col"), None),
        P(None, None, ("clu", "col")),
        P(None, ("clu", "col")),
        P("clu", "col"),
        P("clu", "col"),
        P("clu", "col"),
        P("clu", None, None, "col"),
        P(),
        P(),
    )
    out_specs = (P("clu", "col"), P("clu", "col"))
    return jax.shard_map(
        per_device, mesh=mesh, in_specs=in_specs, out_specs=out_specs, check_vma=False
    )
```

```python
import functools

import jax
import jax.numpy as jnp
from jax import lax
from jax.experimental import pallas as pl
from jax.experimental.pallas import tpu as pltpu
from jax.sharding import PartitionSpec as P

CLUSTERS = 32
ROUNDS = 4
COLOURS = 4
COLS = 4
CAM = 576
SHARE = 144
WIDE = 640
SLOT = 256
PAIR = 384
TRK = 1024
NT = (((1,), (1,)), ((), ()))
NN = (((1,), (0,)), ((), ()))

MY_COLOUR, PARTNER, PARTNER_COLOUR, MY_COL, MY_CLU = 0, 1, 5, 9, 10

F32 = jnp.float32
BF16 = jnp.bfloat16


def smem():
    return pl.BlockSpec(memory_space=pltpu.SMEM)


def vmem():
    return pl.BlockSpec(memory_space=pltpu.VMEM)


def two_parts(v):
    high = v.astype(BF16)
    low = (v - high.astype(F32)).astype(BF16)
    return high, low


def widen(v, width=WIDE):
    return jnp.concatenate([v, jnp.zeros((v.shape[0], width - v.shape[1]), F32)], 1)


def place_share(share, col):
    total = jnp.zeros((1, WIDE), F32)
    for at in range(COLS):
        pieces = []
        if at:
            pieces.append(jnp.zeros((1, SHARE * at), F32))
        pieces.append(share)
        pieces.append(jnp.zeros((1, WIDE - SHARE * (at + 1)), F32))
        total = total + jnp.where(col == at, jnp.concatenate(pieces, 1), 0.0)
    return total


def take_share(vector, col):
    total = jnp.zeros((1, SHARE), F32)
    for at in range(COLS):
        total = total + jnp.where(col == at, vector[:, SHARE * at : SHARE * (at + 1)], 0.0)
    return total


def members(dest_ref):
    lanes = lax.broadcasted_iota(jnp.int32, (CLUSTERS, TRK), 0)
    return (lanes == dest_ref[...]).astype(F32)


def scatter_rows(onehot, row):
    high, low = two_parts(row)
    return jnp.concatenate(
        [onehot * high.astype(F32), onehot * low.astype(F32)], 0
    ).astype(BF16)


def fold(both):
    return both[:CLUSTERS] + both[CLUSTERS:]


def rhs_kernel(
    cc_ref, rp_ref, dest_ref, obs_ref, info_ref, grad_ref, jac_ref, cg_ref, step_ref, diag_ref,
    out_ref, ids_ref, total,
):
    a = pl.program_id(0)
    me = lax.axis_index("clu")
    col = lax.axis_index("col")
    obs = obs_ref[...].astype(F32)
    q = jnp.zeros((1, TRK), F32)
    for b in range(3):
        q = q + obs * info_ref[0, b : b + 1, :] * grad_ref[b : b + 1, :]
    part = fold(
        lax.dot_general(
            scatter_rows(members(dest_ref), q), jac_ref[...], NT, preferred_element_type=F32
        )
    )

    @pl.when(a == 0)
    def _():
        rows = lax.broadcasted_iota(jnp.int32, (CLUSTERS, WIDE), 0)
        total[...] = jnp.where(rows == me, place_share(cg_ref[...], col), 0.0)

    total[:, :CAM] = total[:, :CAM] - part

    @pl.when(a == 2)
    def _():
        mine = cc_ref[me]
        ids_ref[MY_COLOUR] = mine
        ids_ref[MY_COL] = col
        ids_ref[MY_CLU] = me
        for r in range(ROUNDS):
            p = rp_ref[mine, r, me]
            ids_ref[PARTNER + r] = p
            ids_ref[PARTNER_COLOUR + r] = cc_ref[p]
        share = widen(jnp.concatenate([step_ref[...], diag_ref[...]], 1), PAIR)
        for c in range(CLUSTERS):
            colour = cc_ref[c]
            out_ref[c, :, 0:WIDE] = total[c : c + 1, :]
            for r in range(ROUNDS):
                p = rp_ref[colour, r, c]
                out_ref[c, :, WIDE * (r + 1) : WIDE * (r + 2)] = total[pl.ds(p, 1), :]
            out_ref[c, :, WIDE * 5 :] = share


def gather_kernel(ids_ref, recv_ref, out_ref):
    vectors = recv_ref[0, :, : WIDE * 5]
    for c in range(1, CLUSTERS):
        vectors = vectors + recv_ref[c, :, : WIDE * 5]
    out_ref[:, : WIDE * 5] = vectors
    sources = [ids_ref[MY_CLU]] + [ids_ref[PARTNER + r] for r in range(ROUNDS)]
    shares = [recv_ref[c, :, WIDE * 5 : WIDE * 5 + SHARE] for c in sources]
    shares.append(recv_ref[sources[0], :, WIDE * 5 + SHARE : WIDE * 5 + 2 * SHARE])
    for at, share in enumerate(shares):
        out_ref[:, WIDE * 5 + SLOT * at : WIDE * 5 + SLOT * (at + 1)] = widen(share, SLOT)


def block_of(blocks, k, r):
    if k == 2:
        return blocks[2 + r // 2], r % 2
    return blocks[k + k // 3], r


def couple(ids_ref, vectors, blocks, columns, wanted, keep):
    columns[...] = jnp.concatenate(vectors + [jnp.zeros((4, WIDE), F32)], 0).T
    col = ids_ref[MY_COL]
    for r in range(ROUNDS):

        @pl.when(wanted(r))
        def _():
            acc = jnp.zeros((16, CAM), F32)
            for k in range(COLS):
                base = jnp.bitwise_xor(col, k) * SHARE
                ref, at = block_of(blocks, k, r)
                for m in range(SHARE // 16):
                    xs = columns[pl.ds(pl.multiple_of(base + 16 * m, 16), 16), r : r + 1]
                    acc = acc + ref[at, 16 * m : 16 * m + 16, :].astype(F32) * xs
            keep[r : r + 1, :] = widen(jnp.sum(acc, 0, keepdims=True))


def first_step_kernel(
    ids_ref, v0, v1, v2, v3, b0, b1, b2, b3, b4, state_ref, out_ref, rhs_ref, columns
):
    col = ids_ref[MY_COL]
    rows = [v[...] for v in (v0, v1, v2, v3)]
    vectors = (rows[0] + rows[1] + rows[2] + rows[3])[:, : WIDE * 5]
    shares = []
    for at in range(COLS):
        share = jnp.zeros((1, SLOT * 6), F32)
        for k in range(COLS):
            share = jnp.where(jnp.bitwise_xor(col, k) == at, rows[k][:, WIDE * 5 :], share)
        shares.append(share)

    def full(v):
        return widen(jnp.concatenate([s[:, SLOT * v : SLOT * v + SHARE] for s in shares], 1))

    rhs = vectors[:, :WIDE]
    step, diag = full(0), full(5)
    near = [full(r + 1) * vectors[:, WIDE * (r + 1) : WIDE * (r + 2)] for r in range(ROUNDS)]
    keep = state_ref.at[8:16]
    keep[...] = jnp.zeros((8, WIDE), F32)
    couple(
        ids_ref, near, (b0, b1, b2, b3, b4), columns,
        lambda r: ids_ref[PARTNER_COLOUR + r] == 0, keep,
    )
    coupled = jnp.sum(keep[...], 0, keepdims=True)
    mine = ids_ref[MY_COLOUR]
    x = jnp.where(mine == 0, step * rhs, jnp.where(mine == 1, step * (rhs - coupled), 0.0))
    state_ref[0:1, :] = x
    state_ref[1:2, :] = rhs
    state_ref[2:3, :] = step
    state_ref[3:4, :] = diag
    state_ref[4:8, :] = jnp.zeros((4, WIDE), F32)
    rhs_ref[...] = take_share(rhs, col)
    for c in range(CLUSTERS):
        out_ref[c] = x


def step_kernel(number, has_recv, *refs):
    ids_ref, recv_ref, state_ref = refs[:3]
    blocks = refs[3:8]
    tracks = refs[8:-3]
    new_ref, out_ref, columns = refs[-3:]
    fresh = (number - 1) % COLOURS
    near = [recv_ref[ids_ref[PARTNER + r], :, :WIDE] for r in range(ROUNDS)]
    keep = new_ref.at[8:16]
    keep[...] = state_ref[8:16, :]
    couple(
        ids_ref, near, blocks, columns, lambda r: ids_ref[PARTNER_COLOUR + r] == fresh, keep
    )
    x, rhs, step, diag, elim = (state_ref[i : i + 1, :] for i in range(5))
    mine = ids_ref[MY_COLOUR]
    if has_recv:
        total = recv_ref[0, :, WIDE:]
        for c in range(1, CLUSTERS):
            total = total + recv_ref[c, :, WIDE:]
        elim = jnp.where(mine >= (2 if number > COLOURS else 0), total, elim)
    if number == COLOURS:
        x, rhs = 0.25 * x, 0.25 * rhs
        keep[...] = 0.25 * keep[...]
    resid = rhs - jnp.sum(keep[...], 0, keepdims=True)
    if number >= COLOURS:
        resid = resid - diag * x + elim
    x = jnp.where(mine == number % COLOURS, x + step * resid, x)
    for i, v in enumerate((x, rhs, step, diag, elim)):
        new_ref[i : i + 1, :] = v
    if number == 2 * COLOURS - 2:
        resid = rhs - diag * x + elim
        for r in range(ROUNDS):
            done = ids_ref[PARTNER_COLOUR + r] != number % COLOURS
            resid = resid - jnp.where(done, keep[r : r + 1, :], 0.0)
        x = jnp.where(mine == COLOURS - 1, x + step * resid, x)
    for c in range(out_ref.shape[0]):
        out_ref[c, :, :WIDE] = x
    if tracks:
        eliminate(recv_ref, out_ref, *tracks)


def last_step_kernel(ids_ref, recv_ref, state_ref, b0, b1, b2, b3, b4, out_ref, columns, keep):
    def total(c):
        v = recv_ref[COLS * c]
        for k in range(1, COLS):
            v = v + recv_ref[COLS * c + k]
        return v

    near = [total(ids_ref[PARTNER + r]) for r in range(ROUNDS)]
    mine = ids_ref[MY_COLOUR]
    last = COLOURS - 1
    keep[...] = jnp.zeros((8, WIDE), F32)

    def wanted(r):
        return jnp.logical_and(mine == last, ids_ref[PARTNER_COLOUR + r] == last - 1)

    couple(ids_ref, near, (b0, b1, b2, b3, b4), columns, wanted, keep)
    x = total(ids_ref[MY_CLU]) - state_ref[2:3, :] * jnp.sum(keep[...], 0, keepdims=True)
    out_ref[...] = take_share(x, ids_ref[MY_COL])


def eliminate(recv_ref, out_ref, dest_ref, obs_ref, info_ref, jac_ref):
    onehot = members(dest_ref)
    obs = obs_ref[...].astype(F32)
    high, low = two_parts(recv_ref[:, 0, :CAM])
    both = jnp.concatenate([high, low], 0)
    along = []
    for b in range(3):
        every = lax.dot_general(
            both, jac_ref[CAM * b : CAM * (b + 1), :], NN, preferred_element_type=F32
        )
        along.append(jnp.sum(fold(every) * onehot, 0, keepdims=True))
    total = jnp.zeros((2 * CLUSTERS, CAM), F32)
    for a in range(3):
        u = jnp.zeros((1, TRK), F32)
        for b in range(3):
            u = u + obs * info_ref[a, b : b + 1, :] * along[b]
        total = total + lax.dot_general(
            scatter_rows(onehot, u),
            jac_ref[CAM * a : CAM * (a + 1), :],
            NT,
            preferred_element_type=F32,
        )
    out_ref[:, 0, WIDE:] = widen(fold(total))


def shape(*dims, dtype=F32):
    return jax.ShapeDtypeStruct(dims, dtype)


def per_device(
    track_dest, obs_count, track_jac, point_info, point_grad, camera_grad, camera_diag,
    step_scale, covis_blocks, cluster_colour, round_partner,
):
    dest = jnp.transpose(track_dest)
    obs = obs_count[None, :]
    jac = jnp.transpose(track_jac)
    own = jnp.transpose(covis_blocks[0], (0, 2, 1))

    def over_col(v):
        return [v] + [lax.ppermute(v, "col", [(i, i ^ k) for i in range(COLS)]) for k in (1, 3, 2)]

    def swap(v, k):
        return lax.ppermute(v, "col", [(i, i ^ k) for i in range(COLS)])

    first, third = swap(own, 1), swap(own, 3)
    blocks = [own, first, swap(first[: ROUNDS // 2], 3), swap(third[ROUNDS // 2 :], 1), third]
    limit = pltpu.CompilerParams(vmem_limit_bytes=24 << 20)

    whole = lambda *block: pl.BlockSpec(block, lambda a: (0,) * len(block))
    payload, ids = pl.pallas_call(
        rhs_kernel,
        grid=(3,),
        in_specs=[
            smem(), smem(), whole(1, TRK), whole(1, TRK),
            pl.BlockSpec((1, 3, TRK), lambda a: (a, 0, 0)), whole(3, TRK),
            pl.BlockSpec((CAM, TRK), lambda a: (a, 0)), whole(1, SHARE), whole(1, SHARE),
            whole(1, SHARE),
        ],
        out_specs=[whole(CLUSTERS, 1, 5 * WIDE + PAIR), smem()],
        out_shape=[shape(CLUSTERS, 1, 5 * WIDE + PAIR), shape(16, dtype=jnp.int32)],
        scratch_shapes=[pltpu.VMEM((CLUSTERS, WIDE), F32)],
        compiler_params=pltpu.CompilerParams(vmem_limit_bytes=56 << 20),
        name="rhs",
    )(
        cluster_colour, round_partner, dest, obs, point_info, point_grad, jac,
        camera_grad, step_scale, camera_diag,
    )

    def over_clu(v):
        return lax.all_to_all(v, "clu", split_axis=0, concat_axis=0, tiled=True)

    recv = over_clu(payload)
    row = pl.pallas_call(
        gather_kernel,
        in_specs=[smem(), vmem()],
        out_specs=vmem(),
        out_shape=shape(1, 5 * WIDE + 6 * SLOT),
        compiler_params=limit,
        name="gather",
    )(ids, recv)
    row, first, third, second = over_col(row)
    columns = pltpu.VMEM((WIDE, 8), F32)
    state, payload, reduced_rhs = pl.pallas_call(
        first_step_kernel,
        in_specs=[smem()] + [vmem()] * 9,
        out_specs=[vmem()] * 3,
        out_shape=[shape(16, WIDE), shape(CLUSTERS, 1, WIDE), shape(1, SHARE)],
        scratch_shapes=[columns],
        compiler_params=limit,
        name="first_step",
    )(ids, row, first, second, third, *blocks)

    def update(number, recv, state, has_send=False, has_recv=False):
        rows = CLUSTERS * COLS if number == 2 * COLOURS - 2 else CLUSTERS
        extra = (dest, obs, point_info, jac) if has_send else ()
        return pl.pallas_call(
            functools.partial(step_kernel, number, has_recv),
            in_specs=[smem()] + [vmem()] * (7 + len(extra)),
            out_specs=[vmem()] * 2,
            out_shape=[shape(16, WIDE), shape(rows, 1, 2 * WIDE if has_send else WIDE)],
            scratch_shapes=[columns],
            compiler_params=limit,
            name="step",
        )(ids, recv, state, *blocks, *extra)

    recv = over_clu(payload)
    state, payload = update(2, recv, state, has_send=True)
    recv = over_clu(payload)
    state, payload = update(3, recv, state, has_recv=True)
    recv = over_clu(payload)
    state, payload = update(4, recv, state, has_send=True)
    recv = over_clu(payload)
    state, payload = update(5, recv, state, has_recv=True)
    recv = over_clu(payload)
    state, payload = update(6, recv, state)
    recv = lax.all_to_all(payload, ("clu", "col"), split_axis=0, concat_axis=0, tiled=True)
    solution = pl.pallas_call(
        last_step_kernel,
        in_specs=[smem()] + [vmem()] * 7,
        out_specs=vmem(),
        out_shape=shape(1, SHARE),
        scratch_shapes=[columns, pltpu.VMEM((8, WIDE), F32)],
        compiler_params=limit,
        name="last_step",
    )(ids, recv, state, *blocks)
    return solution, reduced_rhs


def solution(mesh):
    in_specs = (
        P(("clu", "col"), None),
        P(("clu", "col")),
        P(("clu", "col"), None),
        P(None, None, ("clu", "col")),
        P(None, ("clu", "col")),
        P("clu", "col"),
        P("clu", "col"),
        P("clu", "col"),
        P("clu", None, None, "col"),
        P(),
        P(),
    )
    out_specs = (P("clu", "col"), P("clu", "col"))
    return jax.shard_map(
        per_device, mesh=mesh, in_specs=in_specs, out_specs=out_specs, check_vma=False
    )
```

```python
import functools

import jax
import jax.numpy as jnp
from jax import lax
from jax.experimental import pallas as pl
from jax.experimental.pallas import tpu as pltpu
from jax.sharding import PartitionSpec as P

CLUSTERS = 32
ROUNDS = 4
COLOURS = 4
COLS = 4
CAM = 576
SHARE = 144
WIDE = 640
SLOT = 256
PAIR = 384
TABLE = 2 * SHARE
TRK = 1024
NT = (((1,), (1,)), ((), ()))
NN = (((1,), (0,)), ((), ()))

MY_COLOUR, PARTNER, PARTNER_COLOUR = 0, 1, 5
LANES = 128

F32 = jnp.float32
BF16 = jnp.bfloat16


def smem():
    return pl.BlockSpec(memory_space=pltpu.SMEM)


def vmem():
    return pl.BlockSpec(memory_space=pltpu.VMEM)


def two_parts(v):
    high = v.astype(BF16)
    low = (v - high.astype(F32)).astype(BF16)
    return high, low


def widen(v, width=WIDE):
    return jnp.concatenate([v, jnp.zeros((v.shape[0], width - v.shape[1]), F32)], 1)


def place_share(share, col):
    total = jnp.zeros((1, WIDE), F32)
    for at in range(COLS):
        pieces = []
        if at:
            pieces.append(jnp.zeros((1, SHARE * at), F32))
        pieces.append(share)
        pieces.append(jnp.zeros((1, WIDE - SHARE * (at + 1)), F32))
        total = total + jnp.where(col == at, jnp.concatenate(pieces, 1), 0.0)
    return total


def take_share(vector, col):
    total = jnp.zeros((1, SHARE), F32)
    for at in range(COLS):
        total = total + jnp.where(col == at, vector[:, SHARE * at : SHARE * (at + 1)], 0.0)
    return total


def members(dest_ref):
    lanes = lax.broadcasted_iota(jnp.int32, (CLUSTERS, TRK), 0)
    return (lanes == dest_ref[...]).astype(F32)


def scatter_rows(onehot, row):
    high, low = two_parts(row)
    return jnp.concatenate(
        [onehot * high.astype(F32), onehot * low.astype(F32)], 0
    ).astype(BF16)


def fold(both):
    return both[:CLUSTERS] + both[CLUSTERS:]


def rhs_kernel(
    cc_ref, rp_ref, dest_ref, obs_ref, info_ref, grad_ref, jac_ref, cg_ref, step_ref, diag_ref,
    out_ref, total,
):
    a = pl.program_id(0)
    me = lax.axis_index("clu")
    col = lax.axis_index("col")
    obs = obs_ref[...].astype(F32)
    q = jnp.zeros((1, TRK), F32)
    for b in range(3):
        q = q + obs * info_ref[0, b : b + 1, :] * grad_ref[b : b + 1, :]
    part = fold(
        lax.dot_general(
            scatter_rows(members(dest_ref), q), jac_ref[...], NT, preferred_element_type=F32
        )
    )

    @pl.when(a == 0)
    def _():
        rows = lax.broadcasted_iota(jnp.int32, (CLUSTERS, WIDE), 0)
        total[...] = jnp.where(rows == me, place_share(cg_ref[...], col), 0.0)

    total[:, :CAM] = total[:, :CAM] - part

    @pl.when(a == 2)
    def _():
        share = widen(jnp.concatenate([step_ref[...], diag_ref[...]], 1), PAIR)
        lanes = lax.broadcasted_iota(jnp.int32, (1, PAIR), 1) - TABLE
        for c in range(CLUSTERS):
            colour = cc_ref[c]
            row = jnp.where(lanes == MY_COLOUR, colour.astype(F32), share)
            out_ref[c, :, 0:WIDE] = total[c : c + 1, :]
            for r in range(ROUNDS):
                p = rp_ref[colour, r, c]
                out_ref[c, :, WIDE * (r + 1) : WIDE * (r + 2)] = total[pl.ds(p, 1), :]
                row = jnp.where(lanes == PARTNER + r, p.astype(F32), row)
                row = jnp.where(lanes == PARTNER_COLOUR + r, cc_ref[p].astype(F32), row)
            out_ref[c, :, WIDE * 5 :] = row


def gather_kernel(recv_ref, ready_ref, out_ref, ids_ref):
    del ready_ref
    vectors = recv_ref[0, :, : WIDE * 5]
    for c in range(1, CLUSTERS):
        vectors = vectors + recv_ref[c, :, : WIDE * 5]
    out_ref[:, : WIDE * 5] = vectors
    table = recv_ref[0, :, WIDE * 5 + TABLE :].astype(jnp.int32)
    ids_ref[...] = jnp.concatenate(
        [table, jnp.zeros((1, LANES - table.shape[1]), jnp.int32)], 1
    )
    sources = [lax.axis_index("clu")] + [ids_ref[0, PARTNER + r] for r in range(ROUNDS)]
    shares = [recv_ref[c, :, WIDE * 5 : WIDE * 5 + SHARE] for c in sources]
    shares.append(recv_ref[sources[0], :, WIDE * 5 + SHARE : WIDE * 5 + 2 * SHARE])
    for at, share in enumerate(shares):
        out_ref[:, WIDE * 5 + SLOT * at : WIDE * 5 + SLOT * (at + 1)] = widen(share, SLOT)


def couple(vectors, blocks_ref):
    row = jnp.concatenate(vectors, 1)
    high = row.astype(BF16).astype(F32)
    middle = (row - high).astype(BF16).astype(F32)
    low = row - high - middle
    parts = jnp.concatenate([high, middle, low, jnp.zeros((13, ROUNDS * WIDE), F32)], 0)
    out = jnp.dot(
        parts.astype(BF16),
        blocks_ref[...].reshape(ROUNDS * WIDE, CAM),
        preferred_element_type=F32,
    )
    return widen(jnp.sum(out, 0, keepdims=True))


def lay_out(pieces, blocks_ref, sems):
    col, core = lax.axis_index("col"), lax.rem(lax.axis_index("clu"), 2)
    copies = []
    for i, (piece, away) in enumerate(zip(pieces, (0, 1 + 2 * core, 2, 3 - 2 * core))):
        at = pl.multiple_of(jnp.bitwise_xor(col, away) * SHARE, 16)
        copies.append(
            pltpu.make_async_copy(piece, blocks_ref.at[:, pl.ds(at, SHARE), :], sems.at[i])
        )
        copies[i].start()
    return copies


def first_step_kernel(
    ids_ref, v0, v1, v2, v3, b0, b1, b2, b3, state_ref, out_ref, rhs_ref, blocks_ref, sems
):
    copies = lay_out((b0, b1, b2, b3), blocks_ref, sems)
    blocks_ref[:, CAM:, :] = jnp.zeros((ROUNDS, WIDE - CAM, CAM), BF16)
    col = lax.axis_index("col")
    rows = [v[...] for v in (v0, v1, v2, v3)]
    vectors = (rows[0] + rows[1] + rows[2] + rows[3])[:, : WIDE * 5]
    shares = []
    for at in range(COLS):
        share = jnp.zeros((1, SLOT * 6), F32)
        for k in range(COLS):
            share = jnp.where(jnp.bitwise_xor(col, k) == at, rows[k][:, WIDE * 5 :], share)
        shares.append(share)

    def full(v):
        return widen(jnp.concatenate([s[:, SLOT * v : SLOT * v + SHARE] for s in shares], 1))

    rhs = vectors[:, :WIDE]
    step, diag = full(0), full(5)
    near = []
    for r in range(ROUNDS):
        x = full(r + 1) * vectors[:, WIDE * (r + 1) : WIDE * (r + 2)]
        near.append(jnp.where(ids_ref[0, PARTNER_COLOUR + r] == 0, x, 0.0))
    for copy in copies:
        copy.wait()
    coupled = couple(near, blocks_ref)
    mine = ids_ref[0, MY_COLOUR]
    x = jnp.where(mine == 0, step * rhs, jnp.where(mine == 1, step * (rhs - coupled), 0.0))
    state_ref[0:1, :] = x
    state_ref[1:2, :] = rhs
    state_ref[2:3, :] = step
    state_ref[3:4, :] = diag
    state_ref[4:8, :] = jnp.zeros((4, WIDE), F32)
    rhs_ref[...] = take_share(rhs, col)
    for c in range(CLUSTERS):
        out_ref[c] = x


def step_kernel(number, has_recv, *refs):
    ids_ref, recv_ref, state_ref, blocks_ref = refs[:4]
    tracks = refs[4:-2]
    new_ref, out_ref = refs[-2:]
    near = [recv_ref[ids_ref[0, PARTNER + r], :, :WIDE] for r in range(ROUNDS)]
    coupled = couple(near, blocks_ref)
    x, rhs, step, diag, elim = (state_ref[i : i + 1, :] for i in range(5))
    mine = ids_ref[0, MY_COLOUR]
    if has_recv:
        total = recv_ref[0, :, WIDE:]
        for c in range(1, CLUSTERS):
            total = total + recv_ref[c, :, WIDE:]
        elim = jnp.where(mine >= (2 if number > COLOURS else 0), total, elim)
    if number == COLOURS:
        x, rhs, coupled = 0.25 * x, 0.25 * rhs, 0.25 * coupled
    resid = rhs - coupled
    if number >= COLOURS:
        resid = resid - diag * x + elim
    x = jnp.where(mine == number % COLOURS, x + step * resid, x)
    for i, v in enumerate((x, rhs, step, diag, elim)):
        new_ref[i : i + 1, :] = v
    if number == 2 * COLOURS - 2:
        x = jnp.where(mine == COLOURS - 1, x + step * (rhs - diag * x + elim), x)
    for c in range(out_ref.shape[0]):
        out_ref[c, :, :WIDE] = x
    if tracks:
        eliminate(recv_ref, out_ref, *tracks)


def last_step_kernel(ids_ref, recv_ref, state_ref, blocks_ref, out_ref):
    def total(c):
        v = recv_ref[COLS * c]
        for k in range(1, COLS):
            v = v + recv_ref[COLS * c + k]
        return v

    coupled = couple([total(ids_ref[0, PARTNER + r]) for r in range(ROUNDS)], blocks_ref)
    x = total(lax.axis_index("clu"))
    x = jnp.where(ids_ref[0, MY_COLOUR] == COLOURS - 1, x - state_ref[2:3, :] * coupled, x)
    out_ref[...] = take_share(x, lax.axis_index("col"))


def eliminate(recv_ref, out_ref, dest_ref, obs_ref, info_ref, jac_ref):
    onehot = members(dest_ref)
    obs = obs_ref[...].astype(F32)
    high, low = two_parts(recv_ref[:, 0, :CAM])
    both = jnp.concatenate([high, low], 0)
    along = []
    for b in range(3):
        every = lax.dot_general(
            both, jac_ref[CAM * b : CAM * (b + 1), :], NN, preferred_element_type=F32
        )
        along.append(jnp.sum(fold(every) * onehot, 0, keepdims=True))
    total = jnp.zeros((2 * CLUSTERS, CAM), F32)
    for a in range(3):
        u = jnp.zeros((1, TRK), F32)
        for b in range(3):
            u = u + obs * info_ref[a, b : b + 1, :] * along[b]
        total = total + lax.dot_general(
            scatter_rows(onehot, u),
            jac_ref[CAM * a : CAM * (a + 1), :],
            NT,
            preferred_element_type=F32,
        )
    out_ref[:, 0, WIDE:] = widen(fold(total))


def shape(*dims, dtype=F32):
    return jax.ShapeDtypeStruct(dims, dtype)


def per_device(
    track_dest, obs_count, track_jac, point_info, point_grad, camera_grad, camera_diag,
    step_scale, covis_blocks, cluster_colour, round_partner,
):
    dest = jnp.transpose(track_dest)
    obs = obs_count[None, :]
    jac = jnp.transpose(track_jac)
    own = jnp.transpose(covis_blocks[0], (0, 2, 1))

    def over_col(v):
        return [v] + [lax.ppermute(v, "col", [(i, i ^ k) for i in range(COLS)]) for k in (1, 3, 2)]

    def swap(v, even, odd):
        pairs = []
        for c in range(CLUSTERS):
            for i in range(COLS):
                pairs.append((COLS * c + i, COLS * c + (i ^ (odd if c % 2 else even))))
        return lax.ppermute(v, ("clu", "col"), pairs)

    near, other = swap(own, 1, 3), swap(own, 3, 1)
    limit = pltpu.CompilerParams(vmem_limit_bytes=24 << 20)
    large = pltpu.CompilerParams(vmem_limit_bytes=56 << 20)

    whole = lambda *block: pl.BlockSpec(block, lambda a: (0,) * len(block))
    payload = pl.pallas_call(
        rhs_kernel,
        grid=(3,),
        in_specs=[
            smem(), smem(), whole(1, TRK), whole(1, TRK),
            pl.BlockSpec((1, 3, TRK), lambda a: (a, 0, 0)), whole(3, TRK),
            pl.BlockSpec((CAM, TRK), lambda a: (a, 0)), whole(1, SHARE), whole(1, SHARE),
            whole(1, SHARE),
        ],
        out_specs=whole(CLUSTERS, 1, 5 * WIDE + PAIR),
        out_shape=shape(CLUSTERS, 1, 5 * WIDE + PAIR),
        scratch_shapes=[pltpu.VMEM((CLUSTERS, WIDE), F32)],
        compiler_params=large,
        name="rhs",
    )(
        cluster_colour, round_partner, dest, obs, point_info, point_grad, jac,
        camera_grad, step_scale, camera_diag,
    )

    pieces = [own, near, swap(near, 3, 1), other]

    def over_clu(v):
        return lax.all_to_all(v, "clu", split_axis=0, concat_axis=0, tiled=True)

    recv = over_clu(payload)
    row, ids = pl.pallas_call(
        gather_kernel,
        in_specs=[vmem(), pl.BlockSpec(memory_space=pl.ANY)],
        out_specs=[vmem()] * 2,
        out_shape=[shape(1, 5 * WIDE + 6 * SLOT), shape(1, LANES, dtype=jnp.int32)],
        compiler_params=limit,
        cost_estimate=pl.CostEstimate(
            flops=6 * 10**9, bytes_accessed=1 << 19, transcendentals=0
        ),
        name="gather",
    )(recv, other)
    row, first, third, second = over_col(row)
    state, payload, reduced_rhs, blocks = pl.pallas_call(
        first_step_kernel,
        in_specs=[vmem()] * 5 + [pl.BlockSpec(memory_space=pl.ANY)] * 4,
        out_specs=[vmem()] * 4,
        out_shape=[
            shape(8, WIDE), shape(CLUSTERS, 1, WIDE), shape(1, SHARE),
            shape(ROUNDS, WIDE, CAM, dtype=BF16),
        ],
        scratch_shapes=[pltpu.SemaphoreType.DMA((COLS,))],
        compiler_params=limit,
        name="first_step",
    )(ids, row, first, second, third, *pieces)

    def update(number, recv, state, has_send=False, has_recv=False):
        rows = CLUSTERS * COLS if number == 2 * COLOURS - 2 else CLUSTERS
        extra = (dest, obs, point_info, jac) if has_send else ()
        return pl.pallas_call(
            functools.partial(step_kernel, number, has_recv),
            in_specs=[vmem()] * (4 + len(extra)),
            out_specs=[vmem()] * 2,
            out_shape=[shape(8, WIDE), shape(rows, 1, 2 * WIDE if has_send else WIDE)],
            compiler_params=limit,
            name="step",
        )(ids, recv, state, blocks, *extra)

    recv = over_clu(payload)
    state, payload = update(2, recv, state, has_send=True)
    recv = over_clu(payload)
    state, payload = update(3, recv, state, has_recv=True)
    recv = over_clu(payload)
    state, payload = update(4, recv, state, has_send=True)
    recv = over_clu(payload)
    state, payload = update(5, recv, state, has_recv=True)
    recv = over_clu(payload)
    state, payload = update(6, recv, state)
    recv = lax.all_to_all(payload, ("clu", "col"), split_axis=0, concat_axis=0, tiled=True)
    solution = pl.pallas_call(
        last_step_kernel,
        in_specs=[vmem()] * 4,
        out_specs=vmem(),
        out_shape=shape(1, SHARE),
        compiler_params=limit,
        name="last_step",
    )(ids, recv, state, blocks)
    return solution, reduced_rhs


def solution(mesh):
    in_specs = (
        P(("clu", "col"), None),
        P(("clu", "col")),
        P(("clu", "col"), None),
        P(None, None, ("clu", "col")),
        P(None, ("clu", "col")),
        P("clu", "col"),
        P("clu", "col"),
        P("clu", "col"),
        P("clu", None, None, "col"),
        P(),
        P(),
    )
    out_specs = (P("clu", "col"), P("clu", "col"))
    return jax.shard_map(
        per_device, mesh=mesh, in_specs=in_specs, out_specs=out_specs, check_vma=False
    )
```

```python
import functools

import jax
import jax.numpy as jnp
from jax import lax
from jax.experimental import pallas as pl
from jax.experimental.pallas import tpu as pltpu
from jax.sharding import PartitionSpec as P

CLUSTERS = 32
ROUNDS = 4
COLOURS = 4
COLS = 4
CAM = 576
SHARE = 144
WIDE = 640
SLOT = 256
PAIR = 384
TABLE = 2 * SHARE
TRK = 1024
NT = (((1,), (1,)), ((), ()))
NN = (((1,), (0,)), ((), ()))

MY_COLOUR, PARTNER, PARTNER_COLOUR = 0, 1, 5
LANES = 128

F32 = jnp.float32
BF16 = jnp.bfloat16


def smem():
    return pl.BlockSpec(memory_space=pltpu.SMEM)


def vmem():
    return pl.BlockSpec(memory_space=pltpu.VMEM)


def two_parts(v):
    high = v.astype(BF16)
    low = (v - high.astype(F32)).astype(BF16)
    return high, low


def widen(v, width=WIDE):
    return jnp.concatenate([v, jnp.zeros((v.shape[0], width - v.shape[1]), F32)], 1)


def place_share(share, col):
    total = jnp.zeros((1, WIDE), F32)
    for at in range(COLS):
        pieces = []
        if at:
            pieces.append(jnp.zeros((1, SHARE * at), F32))
        pieces.append(share)
        pieces.append(jnp.zeros((1, WIDE - SHARE * (at + 1)), F32))
        total = total + jnp.where(col == at, jnp.concatenate(pieces, 1), 0.0)
    return total


def take_share(vector, col):
    total = jnp.zeros((1, SHARE), F32)
    for at in range(COLS):
        total = total + jnp.where(col == at, vector[:, SHARE * at : SHARE * (at + 1)], 0.0)
    return total


def members(dest_ref):
    lanes = lax.broadcasted_iota(jnp.int32, (CLUSTERS, TRK), 0)
    return (lanes == dest_ref[...]).astype(F32)


def scatter_rows(onehot, row):
    high, low = two_parts(row)
    return jnp.concatenate(
        [onehot * high.astype(F32), onehot * low.astype(F32)], 0
    ).astype(BF16)


def fold(both):
    return both[:CLUSTERS] + both[CLUSTERS:]


def rhs_kernel(
    cc_hbm, rp_hbm, dest_hbm, obs_hbm, info_hbm, grad_hbm, cg_hbm, step_hbm, diag_hbm, jac_hbm,
    own_hbm, out_ref, again_hbm,
    cc_ref, rp_ref, dest_ref, obs_ref, info_ref, grad_ref, cg_ref, step_ref, diag_ref, jac_ref,
    total, block_ref, sems,
):
    sources = [dest_hbm, obs_hbm, info_hbm, grad_hbm, cg_hbm, step_hbm, diag_hbm, cc_hbm, rp_hbm]
    targets = [dest_ref, obs_ref, info_ref, grad_ref, cg_ref, step_ref, diag_ref, cc_ref, rp_ref]
    for a in range(3):
        sources.append(jac_hbm.at[CAM * a : CAM * (a + 1), :])
        targets.append(jac_ref.at[a])
    sources.append(own_hbm)
    targets.append(block_ref)
    copies = [
        pltpu.make_async_copy(source, target, sems.at[i])
        for i, (source, target) in enumerate(zip(sources, targets))
    ]
    for copy in copies:
        copy.start()
    me = lax.axis_index("clu")
    col = lax.axis_index("col")
    for copy in copies[:7]:
        copy.wait()
    onehot = members(dest_ref)
    obs = obs_ref[...].astype(F32)
    part = jnp.zeros((2 * CLUSTERS, CAM), F32)
    for a in range(3):
        q = jnp.zeros((1, TRK), F32)
        for b in range(3):
            q = q + obs * info_ref[a, b : b + 1, :] * grad_ref[b : b + 1, :]
        spread = scatter_rows(onehot, q)
        copies[9 + a].wait()
        part = part + lax.dot_general(spread, jac_ref[a], NT, preferred_element_type=F32)
    rows = lax.broadcasted_iota(jnp.int32, (CLUSTERS, WIDE), 0)
    total[...] = jnp.where(rows == me, place_share(cg_ref[...], col), 0.0) - widen(fold(part))
    copies[7].wait()
    copies[8].wait()
    copies[12].wait()
    back = pltpu.make_async_copy(block_ref, again_hbm, sems.at[13])
    back.start()
    share = widen(jnp.concatenate([step_ref[...], diag_ref[...]], 1), PAIR)
    ends = PAIR - LANES
    lanes = lax.broadcasted_iota(jnp.int32, (1, LANES), 1) + (ends - TABLE)
    for c in range(CLUSTERS):
        colour = cc_ref[c]
        row = jnp.where(lanes == MY_COLOUR, colour.astype(F32), share[:, ends:])
        out_ref[c, :, 0:WIDE] = total[c : c + 1, :]
        for r in range(ROUNDS):
            p = rp_ref[colour, r, c]
            out_ref[c, :, WIDE * (r + 1) : WIDE * (r + 2)] = total[pl.ds(p, 1), :]
            row = jnp.where(lanes == PARTNER + r, p.astype(F32), row)
            row = jnp.where(lanes == PARTNER_COLOUR + r, cc_ref[p].astype(F32), row)
        out_ref[c, :, WIDE * 5 : WIDE * 5 + ends] = share[:, :ends]
        out_ref[c, :, WIDE * 5 + ends :] = row
    back.wait()


def gather_kernel(recv_ref, ready_ref, out_ref, ids_ref):
    del ready_ref
    vectors = recv_ref[0, :, : WIDE * 5]
    for c in range(1, CLUSTERS):
        vectors = vectors + recv_ref[c, :, : WIDE * 5]
    out_ref[:, : WIDE * 5] = vectors
    table = recv_ref[0, :, WIDE * 5 + TABLE :].astype(jnp.int32)
    ids_ref[...] = jnp.concatenate(
        [table, jnp.zeros((1, LANES - table.shape[1]), jnp.int32)], 1
    )
    sources = [lax.axis_index("clu")] + [ids_ref[0, PARTNER + r] for r in range(ROUNDS)]
    shares = [recv_ref[c, :, WIDE * 5 : WIDE * 5 + SHARE] for c in sources]
    shares.append(recv_ref[sources[0], :, WIDE * 5 + SHARE : WIDE * 5 + 2 * SHARE])
    for at, share in enumerate(shares):
        out_ref[:, WIDE * 5 + SLOT * at : WIDE * 5 + SLOT * (at + 1)] = widen(share, SLOT)


def couple(vectors, blocks_ref):
    row = jnp.concatenate(vectors, 1)
    high = row.astype(BF16).astype(F32)
    middle = (row - high).astype(BF16).astype(F32)
    low = row - high - middle
    parts = jnp.concatenate([high, middle, low, jnp.zeros((13, ROUNDS * WIDE), F32)], 0)
    out = jnp.dot(
        parts.astype(BF16),
        blocks_ref[...].reshape(ROUNDS * WIDE, CAM),
        preferred_element_type=F32,
    )
    return widen(jnp.sum(out, 0, keepdims=True))


def lay_out(pieces, blocks_ref, sems):
    col, core = lax.axis_index("col"), lax.rem(lax.axis_index("clu"), 2)
    copies = []
    for i, (piece, away) in enumerate(zip(pieces, (0, 1 + 2 * core, 2, 3 - 2 * core))):
        at = pl.multiple_of(jnp.bitwise_xor(col, away) * SHARE, 16)
        copies.append(
            pltpu.make_async_copy(piece, blocks_ref.at[:, pl.ds(at, SHARE), :], sems.at[i])
        )
        copies[i].start()
    return copies


def first_step_kernel(
    ids_ref, v0, v1, v2, v3, b0, b1, b2, b3, state_ref, out_ref, rhs_ref, blocks_ref, sems
):
    copies = lay_out((b0, b1, b2, b3), blocks_ref, sems)
    blocks_ref[:, CAM:, :] = jnp.zeros((ROUNDS, WIDE - CAM, CAM), BF16)
    col = lax.axis_index("col")
    rows = [v[...] for v in (v0, v1, v2, v3)]
    vectors = (rows[0] + rows[1] + rows[2] + rows[3])[:, : WIDE * 5]
    shares = []
    for at in range(COLS):
        share = jnp.zeros((1, SLOT * 6), F32)
        for k in range(COLS):
            share = jnp.where(jnp.bitwise_xor(col, k) == at, rows[k][:, WIDE * 5 :], share)
        shares.append(share)

    def full(v):
        return widen(jnp.concatenate([s[:, SLOT * v : SLOT * v + SHARE] for s in shares], 1))

    rhs = vectors[:, :WIDE]
    step, diag = full(0), full(5)
    near = []
    for r in range(ROUNDS):
        x = full(r + 1) * vectors[:, WIDE * (r + 1) : WIDE * (r + 2)]
        near.append(jnp.where(ids_ref[0, PARTNER_COLOUR + r] == 0, x, 0.0))
    for copy in copies:
        copy.wait()
    coupled = couple(near, blocks_ref)
    mine = ids_ref[0, MY_COLOUR]
    x = jnp.where(mine == 0, step * rhs, jnp.where(mine == 1, step * (rhs - coupled), 0.0))
    state_ref[0:1, :] = x
    state_ref[1:2, :] = rhs
    state_ref[2:3, :] = step
    state_ref[3:4, :] = diag
    state_ref[4:8, :] = jnp.zeros((4, WIDE), F32)
    rhs_ref[...] = take_share(rhs, col)
    for c in range(CLUSTERS):
        out_ref[c] = x


def step_kernel(number, has_recv, *refs):
    ids_ref, recv_ref, state_ref, blocks_ref = refs[:4]
    tracks = refs[4:-2]
    new_ref, out_ref = refs[-2:]
    near = [recv_ref[ids_ref[0, PARTNER + r], :, :WIDE] for r in range(ROUNDS)]
    coupled = couple(near, blocks_ref)
    x, rhs, step, diag, elim = (state_ref[i : i + 1, :] for i in range(5))
    mine = ids_ref[0, MY_COLOUR]
    if has_recv:
        total = recv_ref[0, :, WIDE:]
        for c in range(1, CLUSTERS):
            total = total + recv_ref[c, :, WIDE:]
        elim = jnp.where(mine >= (2 if number > COLOURS else 0), total, elim)
    if number == COLOURS:
        x, rhs, coupled = 0.25 * x, 0.25 * rhs, 0.25 * coupled
    resid = rhs - coupled
    if number >= COLOURS:
        resid = resid - diag * x + elim
    x = jnp.where(mine == number % COLOURS, x + step * resid, x)
    for i, v in enumerate((x, rhs, step, diag, elim)):
        new_ref[i : i + 1, :] = v
    if number == 2 * COLOURS - 2:
        x = jnp.where(mine == COLOURS - 1, x + step * (rhs - diag * x + elim), x)
    for c in range(out_ref.shape[0]):
        out_ref[c, :, :WIDE] = x
    if tracks:
        eliminate(recv_ref, out_ref, *tracks)


def last_step_kernel(ids_ref, recv_ref, state_ref, blocks_ref, out_ref):
    def total(c):
        v = recv_ref[COLS * c]
        for k in range(1, COLS):
            v = v + recv_ref[COLS * c + k]
        return v

    coupled = couple([total(ids_ref[0, PARTNER + r]) for r in range(ROUNDS)], blocks_ref)
    x = total(lax.axis_index("clu"))
    x = jnp.where(ids_ref[0, MY_COLOUR] == COLOURS - 1, x - state_ref[2:3, :] * coupled, x)
    out_ref[...] = take_share(x, lax.axis_index("col"))


def eliminate(recv_ref, out_ref, dest_ref, obs_ref, info_ref, jac_ref):
    onehot = members(dest_ref)
    obs = obs_ref[...].astype(F32)
    high, low = two_parts(recv_ref[:, 0, :CAM])
    both = jnp.concatenate([high, low], 0)
    along = []
    for b in range(3):
        every = lax.dot_general(
            both, jac_ref[CAM * b : CAM * (b + 1), :], NN, preferred_element_type=F32
        )
        along.append(jnp.sum(fold(every) * onehot, 0, keepdims=True))
    total = jnp.zeros((2 * CLUSTERS, CAM), F32)
    for a in range(3):
        u = jnp.zeros((1, TRK), F32)
        for b in range(3):
            u = u + obs * info_ref[a, b : b + 1, :] * along[b]
        total = total + lax.dot_general(
            scatter_rows(onehot, u),
            jac_ref[CAM * a : CAM * (a + 1), :],
            NT,
            preferred_element_type=F32,
        )
    out_ref[:, 0, WIDE:] = widen(fold(total))


def shape(*dims, dtype=F32):
    return jax.ShapeDtypeStruct(dims, dtype)


def per_device(
    track_dest, obs_count, track_jac, point_info, point_grad, camera_grad, camera_diag,
    step_scale, covis_blocks, cluster_colour, round_partner,
):
    dest = jnp.transpose(track_dest)
    obs = obs_count[None, :]
    jac = jnp.transpose(track_jac)
    own = jnp.transpose(covis_blocks[0], (0, 2, 1))

    def over_col(v):
        return [v] + [lax.ppermute(v, "col", [(i, i ^ k) for i in range(COLS)]) for k in (1, 3, 2)]

    def swap(v, even, odd):
        pairs = []
        for c in range(CLUSTERS):
            for i in range(COLS):
                pairs.append((COLS * c + i, COLS * c + (i ^ (odd if c % 2 else even))))
        return lax.ppermute(v, ("clu", "col"), pairs)

    near = swap(own, 1, 3)
    limit = pltpu.CompilerParams(vmem_limit_bytes=24 << 20)
    large = pltpu.CompilerParams(vmem_limit_bytes=56 << 20)

    payload, again = pl.pallas_call(
        rhs_kernel,
        in_specs=[pl.BlockSpec(memory_space=pl.ANY)] * 11,
        out_specs=[vmem(), pl.BlockSpec(memory_space=pl.ANY)],
        out_shape=[
            shape(CLUSTERS, 1, 5 * WIDE + PAIR), shape(ROUNDS, SHARE, CAM, dtype=BF16),
        ],
        scratch_shapes=[
            pltpu.SMEM((CLUSTERS,), jnp.int32),
            pltpu.SMEM((COLOURS, ROUNDS, CLUSTERS), jnp.int32),
            pltpu.VMEM((1, TRK), jnp.int32),
            pltpu.VMEM((1, TRK), jnp.int32),
            pltpu.VMEM((3, 3, TRK), F32),
            pltpu.VMEM((3, TRK), F32),
            pltpu.VMEM((1, SHARE), F32),
            pltpu.VMEM((1, SHARE), F32),
            pltpu.VMEM((1, SHARE), F32),
            pltpu.VMEM((3, CAM, TRK), BF16),
            pltpu.VMEM((CLUSTERS, WIDE), F32),
            pltpu.VMEM((ROUNDS, SHARE, CAM), BF16),
            pltpu.SemaphoreType.DMA((14,)),
        ],
        compiler_params=large,
        name="rhs",
    )(
        cluster_colour, round_partner, dest, obs, point_info, point_grad,
        camera_grad, step_scale, camera_diag, jac, own,
    )
    other = swap(again, 3, 1)
    pieces = [own, near, swap(near, 3, 1), other]

    def over_clu(v):
        return lax.all_to_all(v, "clu", split_axis=0, concat_axis=0, tiled=True)

    recv = over_clu(payload)
    row, ids = pl.pallas_call(
        gather_kernel,
        in_specs=[vmem(), pl.BlockSpec(memory_space=pl.ANY)],
        out_specs=[vmem()] * 2,
        out_shape=[shape(1, 5 * WIDE + 6 * SLOT), shape(1, LANES, dtype=jnp.int32)],
        compiler_params=limit,
        cost_estimate=pl.CostEstimate(
            flops=6 * 10**9, bytes_accessed=1 << 19, transcendentals=0
        ),
        name="gather",
    )(recv, other)
    row, first, third, second = over_col(row)
    state, payload, reduced_rhs, blocks = pl.pallas_call(
        first_step_kernel,
        in_specs=[vmem()] * 5 + [pl.BlockSpec(memory_space=pl.ANY)] * 4,
        out_specs=[vmem()] * 4,
        out_shape=[
            shape(8, WIDE), shape(CLUSTERS, 1, WIDE), shape(1, SHARE),
            shape(ROUNDS, WIDE, CAM, dtype=BF16),
        ],
        scratch_shapes=[pltpu.SemaphoreType.DMA((COLS,))],
        compiler_params=limit,
        name="first_step",
    )(ids, row, first, second, third, *pieces)

    def update(number, recv, state, has_send=False, has_recv=False):
        rows = CLUSTERS * COLS if number == 2 * COLOURS - 2 else CLUSTERS
        extra = (dest, obs, point_info, jac) if has_send else ()
        return pl.pallas_call(
            functools.partial(step_kernel, number, has_recv),
            in_specs=[vmem()] * (4 + len(extra)),
            out_specs=[vmem()] * 2,
            out_shape=[shape(8, WIDE), shape(rows, 1, 2 * WIDE if has_send else WIDE)],
            compiler_params=limit,
            name="step",
        )(ids, recv, state, blocks, *extra)

    recv = over_clu(payload)
    state, payload = update(2, recv, state, has_send=True)
    recv = over_clu(payload)
    state, payload = update(3, recv, state, has_recv=True)
    recv = over_clu(payload)
    state, payload = update(4, recv, state, has_send=True)
    recv = over_clu(payload)
    state, payload = update(5, recv, state, has_recv=True)
    recv = over_clu(payload)
    state, payload = update(6, recv, state)
    recv = lax.all_to_all(payload, ("clu", "col"), split_axis=0, concat_axis=0, tiled=True)
    solution = pl.pallas_call(
        last_step_kernel,
        in_specs=[vmem()] * 4,
        out_specs=vmem(),
        out_shape=shape(1, SHARE),
        compiler_params=limit,
        name="last_step",
    )(ids, recv, state, blocks)
    return solution, reduced_rhs


def solution(mesh):
    in_specs = (
        P(("clu", "col"), None),
        P(("clu", "col")),
        P(("clu", "col"), None),
        P(None, None, ("clu", "col")),
        P(None, ("clu", "col")),
        P("clu", "col"),
        P("clu", "col"),
        P("clu", "col"),
        P("clu", None, None, "col"),
        P(),
        P(),
    )
    out_specs = (P("clu", "col"), P("clu", "col"))
    return jax.shard_map(
        per_device, mesh=mesh, in_specs=in_specs, out_specs=out_specs, check_vma=False
    )
```

```python
import functools

import jax
import jax.numpy as jnp
from jax import lax
from jax.experimental import pallas as pl
from jax.experimental.pallas import tpu as pltpu
from jax.sharding import PartitionSpec as P

CLUSTERS = 32
ROUNDS = 4
COLOURS = 4
COLS = 4
CAM = 576
SHARE = 144
WIDE = 640
SLOT = 256
SPARE = WIDE - CAM
TABLE = 2 * SHARE
GROUP = 8
TRK = 1024
NT = (((1,), (1,)), ((), ()))
NN = (((1,), (0,)), ((), ()))

MY_COLOUR, PARTNER, PARTNER_COLOUR = 0, 1, 5
LANES = 128

F32 = jnp.float32
BF16 = jnp.bfloat16


def smem():
    return pl.BlockSpec(memory_space=pltpu.SMEM)


def vmem():
    return pl.BlockSpec(memory_space=pltpu.VMEM)


def two_parts(v):
    high = v.astype(BF16)
    low = (v - high.astype(F32)).astype(BF16)
    return high, low


def widen(v, width=WIDE):
    return jnp.concatenate([v, jnp.zeros((v.shape[0], width - v.shape[1]), F32)], 1)


def place_share(share, col):
    total = jnp.zeros((1, WIDE), F32)
    for at in range(COLS):
        pieces = []
        if at:
            pieces.append(jnp.zeros((1, SHARE * at), F32))
        pieces.append(share)
        pieces.append(jnp.zeros((1, WIDE - SHARE * (at + 1)), F32))
        total = total + jnp.where(col == at, jnp.concatenate(pieces, 1), 0.0)
    return total


def take_share(vector, col):
    total = jnp.zeros((1, SHARE), F32)
    for at in range(COLS):
        total = total + jnp.where(col == at, vector[:, SHARE * at : SHARE * (at + 1)], 0.0)
    return total


def members(dest_ref):
    lanes = lax.broadcasted_iota(jnp.int32, (CLUSTERS, TRK), 0)
    return (lanes == dest_ref[...]).astype(F32)


def scatter_rows(onehot, row):
    high, low = two_parts(row)
    return jnp.concatenate(
        [onehot * high.astype(F32), onehot * low.astype(F32)], 0
    ).astype(BF16)


def fold(both):
    return both[:CLUSTERS] + both[CLUSTERS:]


def rhs_kernel(
    cc_hbm, rp_hbm, dest_hbm, obs_hbm, info_hbm, grad_hbm, cg_hbm, step_hbm, diag_hbm, jac_hbm,
    own_hbm, out_hbm, again_hbm,
    cc_ref, rp_ref, dest_ref, obs_ref, info_ref, grad_ref, cg_ref, step_ref, diag_ref, jac_ref,
    total, block_ref, out_ref, sems,
):
    sources = [dest_hbm, obs_hbm, info_hbm, grad_hbm, cg_hbm, step_hbm, diag_hbm, cc_hbm, rp_hbm]
    targets = [dest_ref, obs_ref, info_ref, grad_ref, cg_ref, step_ref, diag_ref, cc_ref, rp_ref]
    for a in range(3):
        sources.append(jac_hbm.at[CAM * a : CAM * (a + 1), :])
        targets.append(jac_ref.at[a])
    sources.append(own_hbm)
    targets.append(block_ref)
    copies = [
        pltpu.make_async_copy(source, target, sems.at[i])
        for i, (source, target) in enumerate(zip(sources, targets))
    ]
    for copy in copies:
        copy.start()
    me = lax.axis_index("clu")
    col = lax.axis_index("col")
    for copy in copies[:7]:
        copy.wait()
    onehot = members(dest_ref)
    obs = obs_ref[...].astype(F32)
    part = jnp.zeros((2 * CLUSTERS, CAM), F32)
    for a in range(3):
        q = jnp.zeros((1, TRK), F32)
        for b in range(3):
            q = q + obs * info_ref[a, b : b + 1, :] * grad_ref[b : b + 1, :]
        spread = scatter_rows(onehot, q)
        copies[9 + a].wait()
        part = part + lax.dot_general(spread, jac_ref[a], NT, preferred_element_type=F32)
    rows = lax.broadcasted_iota(jnp.int32, (CLUSTERS, WIDE), 0)
    total[...] = jnp.where(rows == me, place_share(cg_ref[...], col), 0.0) - widen(fold(part))
    copies[7].wait()
    copies[8].wait()
    copies[12].wait()
    back = pltpu.make_async_copy(block_ref, again_hbm, sems.at[13])
    back.start()
    spare = jnp.concatenate(
        [step_ref[...], diag_ref[...], jnp.zeros((1, 5 * SPARE - 2 * SHARE), F32)], 1
    )
    empty = jnp.zeros((1, CAM), F32)
    tails = [
        jnp.concatenate([empty, spare[:, SPARE * v : SPARE * (v + 1)]], 1) for v in range(5)
    ]
    lanes = lax.broadcasted_iota(jnp.int32, (1, WIDE), 1) - (CAM + TABLE % SPARE)
    outs = []
    for c in range(CLUSTERS):
        colour = cc_ref[c]
        sources = [c] + [rp_ref[colour, r, c] for r in range(ROUNDS)]
        last = jnp.where(lanes == MY_COLOUR, colour.astype(F32), tails[4])
        for r, p in enumerate(sources[1:]):
            last = jnp.where(lanes == PARTNER + r, p.astype(F32), last)
            last = jnp.where(lanes == PARTNER_COLOUR + r, cc_ref[p].astype(F32), last)
        for v, p in enumerate(sources):
            tail = last if v == 4 else tails[v]
            out_ref[c, :, WIDE * v : WIDE * (v + 1)] = total[pl.ds(p, 1), :] + tail
        if c % GROUP == GROUP - 1:
            rows = pl.ds(c + 1 - GROUP, GROUP)
            outs.append(
                pltpu.make_async_copy(
                    out_ref.at[rows], out_hbm.at[rows], sems.at[14 + c // GROUP]
                )
            )
            outs[-1].start()
    for copy in outs:
        copy.wait()
    back.wait()


def gather_kernel(recv_ref, ready_ref, out_ref, ids_ref):
    del ready_ref
    vectors = recv_ref[0]
    for c in range(1, CLUSTERS):
        vectors = vectors + recv_ref[c]
    out_ref[:, : WIDE * 5] = vectors

    def spare(c):
        return jnp.concatenate(
            [recv_ref[c, :, WIDE * (v + 1) - SPARE : WIDE * (v + 1)] for v in range(5)], 1
        )

    me = lax.axis_index("clu")
    mine = spare(me)
    table = mine[:, TABLE:].astype(jnp.int32)
    ids_ref[...] = jnp.concatenate(
        [table, jnp.zeros((1, LANES - table.shape[1]), jnp.int32)], 1
    )
    shares = [mine[:, :SHARE]]
    shares += [spare(ids_ref[0, PARTNER + r])[:, :SHARE] for r in range(ROUNDS)]
    shares.append(mine[:, SHARE:TABLE])
    for at, share in enumerate(shares):
        out_ref[:, WIDE * 5 + SLOT * at : WIDE * 5 + SLOT * (at + 1)] = widen(share, SLOT)


def couple(vectors, blocks_ref):
    row = jnp.concatenate(vectors, 1)
    high = row.astype(BF16).astype(F32)
    middle = (row - high).astype(BF16).astype(F32)
    low = row - high - middle
    parts = jnp.concatenate([high, middle, low, jnp.zeros((13, ROUNDS * WIDE), F32)], 0)
    out = jnp.dot(
        parts.astype(BF16),
        blocks_ref[...].reshape(ROUNDS * WIDE, CAM),
        preferred_element_type=F32,
    )
    return widen(jnp.sum(out, 0, keepdims=True))


def lay_out_kernel(*refs):
    pieces, blocks_ref, sems = refs[:COLS], refs[COLS], refs[COLS + 1]
    col, core = lax.axis_index("col"), lax.rem(lax.axis_index("clu"), 2)
    copies = []
    for i, (piece, away) in enumerate(zip(pieces, (0, 1 + 2 * core, 2, 3 - 2 * core))):
        at = pl.multiple_of(jnp.bitwise_xor(col, away) * SHARE, 16)
        copies.append(
            pltpu.make_async_copy(piece, blocks_ref.at[:, pl.ds(at, SHARE), :], sems.at[i])
        )
        copies[i].start()
    blocks_ref[:, CAM:, :] = jnp.zeros((ROUNDS, WIDE - CAM, CAM), BF16)
    for copy in copies:
        copy.wait()


def first_step_kernel(
    ids_ref, v0, v1, v2, v3, blocks_ref, state_ref, out_ref, rhs_ref
):
    col = lax.axis_index("col")
    rows = [v[...] for v in (v0, v1, v2, v3)]
    vectors = (rows[0] + rows[1] + rows[2] + rows[3])[:, : WIDE * 5]
    shares = []
    for at in range(COLS):
        share = jnp.zeros((1, SLOT * 6), F32)
        for k in range(COLS):
            share = jnp.where(jnp.bitwise_xor(col, k) == at, rows[k][:, WIDE * 5 :], share)
        shares.append(share)

    def full(v):
        return widen(jnp.concatenate([s[:, SLOT * v : SLOT * v + SHARE] for s in shares], 1))

    rhs = vectors[:, :WIDE]
    step, diag = full(0), full(5)
    near = []
    for r in range(ROUNDS):
        x = full(r + 1) * vectors[:, WIDE * (r + 1) : WIDE * (r + 2)]
        near.append(jnp.where(ids_ref[0, PARTNER_COLOUR + r] == 0, x, 0.0))
    coupled = couple(near, blocks_ref)
    mine = ids_ref[0, MY_COLOUR]
    x = jnp.where(mine == 0, step * rhs, jnp.where(mine == 1, step * (rhs - coupled), 0.0))
    state_ref[0:1, :] = x
    state_ref[1:2, :] = rhs
    state_ref[2:3, :] = step
    state_ref[3:4, :] = diag
    state_ref[4:8, :] = jnp.zeros((4, WIDE), F32)
    rhs_ref[...] = take_share(rhs, col)
    for c in range(CLUSTERS):
        out_ref[c] = x


def step_kernel(number, has_recv, *refs):
    ids_ref, recv_ref, state_ref, blocks_ref = refs[:4]
    tracks = refs[4:-2]
    new_ref, out_ref = refs[-2:]
    near = [recv_ref[ids_ref[0, PARTNER + r], :, :WIDE] for r in range(ROUNDS)]
    coupled = couple(near, blocks_ref)
    x, rhs, step, diag, elim = (state_ref[i : i + 1, :] for i in range(5))
    mine = ids_ref[0, MY_COLOUR]
    if has_recv:
        total = recv_ref[0, :, WIDE:]
        for c in range(1, CLUSTERS):
            total = total + recv_ref[c, :, WIDE:]
        elim = jnp.where(mine >= (2 if number > COLOURS else 0), total, elim)
    if number == COLOURS:
        x, rhs, coupled = 0.25 * x, 0.25 * rhs, 0.25 * coupled
    resid = rhs - coupled
    if number >= COLOURS:
        resid = resid - diag * x + elim
    x = jnp.where(mine == number % COLOURS, x + step * resid, x)
    for i, v in enumerate((x, rhs, step, diag, elim)):
        new_ref[i : i + 1, :] = v
    if number == 2 * COLOURS - 2:
        x = jnp.where(mine == COLOURS - 1, x + step * (rhs - diag * x + elim), x)
    for c in range(out_ref.shape[0]):
        out_ref[c, :, :WIDE] = x
    if tracks:
        eliminate(recv_ref, out_ref, *tracks)


def last_step_kernel(ids_ref, recv_ref, state_ref, blocks_ref, out_ref):
    def total(c):
        v = recv_ref[COLS * c]
        for k in range(1, COLS):
            v = v + recv_ref[COLS * c + k]
        return v

    coupled = couple([total(ids_ref[0, PARTNER + r]) for r in range(ROUNDS)], blocks_ref)
    x = total(lax.axis_index("clu"))
    x = jnp.where(ids_ref[0, MY_COLOUR] == COLOURS - 1, x - state_ref[2:3, :] * coupled, x)
    out_ref[...] = take_share(x, lax.axis_index("col"))


def eliminate(recv_ref, out_ref, dest_ref, obs_ref, info_ref, jac_ref):
    onehot = members(dest_ref)
    obs = obs_ref[...].astype(F32)
    high, low = two_parts(recv_ref[:, 0, :CAM])
    both = jnp.concatenate([high, low], 0)
    along = []
    for b in range(3):
        every = lax.dot_general(
            both, jac_ref[CAM * b : CAM * (b + 1), :], NN, preferred_element_type=F32
        )
        along.append(jnp.sum(fold(every) * onehot, 0, keepdims=True))
    total = jnp.zeros((2 * CLUSTERS, CAM), F32)
    for a in range(3):
        u = jnp.zeros((1, TRK), F32)
        for b in range(3):
            u = u + obs * info_ref[a, b : b + 1, :] * along[b]
        total = total + lax.dot_general(
            scatter_rows(onehot, u),
            jac_ref[CAM * a : CAM * (a + 1), :],
            NT,
            preferred_element_type=F32,
        )
    out_ref[:, 0, WIDE:] = widen(fold(total))


def shape(*dims, dtype=F32):
    return jax.ShapeDtypeStruct(dims, dtype)


def per_device(
    track_dest, obs_count, track_jac, point_info, point_grad, camera_grad, camera_diag,
    step_scale, covis_blocks, cluster_colour, round_partner,
):
    dest = jnp.transpose(track_dest)
    obs = obs_count[None, :]
    jac = jnp.transpose(track_jac)
    own = jnp.transpose(covis_blocks[0], (0, 2, 1))

    def over_col(v):
        return [v] + [lax.ppermute(v, "col", [(i, i ^ k) for i in range(COLS)]) for k in (1, 3, 2)]

    def swap(v, even, odd):
        pairs = []
        for c in range(CLUSTERS):
            for i in range(COLS):
                pairs.append((COLS * c + i, COLS * c + (i ^ (odd if c % 2 else even))))
        return lax.ppermute(v, ("clu", "col"), pairs)

    near = swap(own, 1, 3)
    limit = pltpu.CompilerParams(vmem_limit_bytes=24 << 20)
    large = pltpu.CompilerParams(vmem_limit_bytes=56 << 20)

    payload, again = pl.pallas_call(
        rhs_kernel,
        in_specs=[pl.BlockSpec(memory_space=pl.ANY)] * 11,
        out_specs=[pl.BlockSpec(memory_space=pl.ANY)] * 2,
        out_shape=[
            shape(CLUSTERS, 1, 5 * WIDE), shape(ROUNDS, SHARE, CAM, dtype=BF16),
        ],
        scratch_shapes=[
            pltpu.SMEM((CLUSTERS,), jnp.int32),
            pltpu.SMEM((COLOURS, ROUNDS, CLUSTERS), jnp.int32),
            pltpu.VMEM((1, TRK), jnp.int32),
            pltpu.VMEM((1, TRK), jnp.int32),
            pltpu.VMEM((3, 3, TRK), F32),
            pltpu.VMEM((3, TRK), F32),
            pltpu.VMEM((1, SHARE), F32),
            pltpu.VMEM((1, SHARE), F32),
            pltpu.VMEM((1, SHARE), F32),
            pltpu.VMEM((3, CAM, TRK), BF16),
            pltpu.VMEM((CLUSTERS, WIDE), F32),
            pltpu.VMEM((ROUNDS, SHARE, CAM), BF16),
            pltpu.VMEM((CLUSTERS, 1, 5 * WIDE), F32),
            pltpu.SemaphoreType.DMA((14 + CLUSTERS // GROUP,)),
        ],
        compiler_params=large,
        name="rhs",
    )(
        cluster_colour, round_partner, dest, obs, point_info, point_grad,
        camera_grad, step_scale, camera_diag, jac, own,
    )
    other = swap(again, 3, 1)
    pieces = [own, near, swap(near, 3, 1), other]

    def over_clu(v):
        return lax.all_to_all(v, "clu", split_axis=0, concat_axis=0, tiled=True)

    recv = over_clu(payload)
    row, ids = pl.pallas_call(
        gather_kernel,
        in_specs=[vmem(), pl.BlockSpec(memory_space=pl.ANY)],
        out_specs=[vmem()] * 2,
        out_shape=[shape(1, 5 * WIDE + 6 * SLOT), shape(1, LANES, dtype=jnp.int32)],
        compiler_params=limit,
        cost_estimate=pl.CostEstimate(
            flops=6 * 10**9, bytes_accessed=1 << 19, transcendentals=0
        ),
        name="gather",
    )(recv, other)
    row, first, third, second = over_col(row)
    blocks = pl.pallas_call(
        lay_out_kernel,
        in_specs=[pl.BlockSpec(memory_space=pl.ANY)] * COLS,
        out_specs=vmem(),
        out_shape=shape(ROUNDS, WIDE, CAM, dtype=BF16),
        scratch_shapes=[pltpu.SemaphoreType.DMA((COLS,))],
        compiler_params=limit,
        name="lay_out",
    )(*pieces)
    state, payload, reduced_rhs = pl.pallas_call(
        first_step_kernel,
        in_specs=[vmem()] * 6,
        out_specs=[vmem()] * 3,
        out_shape=[shape(8, WIDE), shape(CLUSTERS, 1, WIDE), shape(1, SHARE)],
        compiler_params=limit,
        name="first_step",
    )(ids, row, first, second, third, blocks)

    def update(number, recv, state, has_send=False, has_recv=False):
        rows = CLUSTERS * COLS if number == 2 * COLOURS - 2 else CLUSTERS
        extra = (dest, obs, point_info, jac) if has_send else ()
        return pl.pallas_call(
            functools.partial(step_kernel, number, has_recv),
            in_specs=[vmem()] * (4 + len(extra)),
            out_specs=[vmem()] * 2,
            out_shape=[shape(8, WIDE), shape(rows, 1, 2 * WIDE if has_send else WIDE)],
            compiler_params=limit,
            name="step",
        )(ids, recv, state, blocks, *extra)

    recv = over_clu(payload)
    state, payload = update(2, recv, state, has_send=True)
    recv = over_clu(payload)
    state, payload = update(3, recv, state, has_recv=True)
    recv = over_clu(payload)
    state, payload = update(4, recv, state, has_send=True)
    recv = over_clu(payload)
    state, payload = update(5, recv, state, has_recv=True)
    recv = over_clu(payload)
    state, payload = update(6, recv, state)
    recv = lax.all_to_all(payload, ("clu", "col"), split_axis=0, concat_axis=0, tiled=True)
    solution = pl.pallas_call(
        last_step_kernel,
        in_specs=[vmem()] * 4,
        out_specs=vmem(),
        out_shape=shape(1, SHARE),
        compiler_params=limit,
        name="last_step",
    )(ids, recv, state, blocks)
    return solution, reduced_rhs


def solution(mesh):
    in_specs = (
        P(("clu", "col"), None),
        P(("clu", "col")),
        P(("clu", "col"), None),
        P(None, None, ("clu", "col")),
        P(None, ("clu", "col")),
        P("clu", "col"),
        P("clu", "col"),
        P("clu", "col"),
        P("clu", None, None, "col"),
        P(),
        P(),
    )
    out_specs = (P("clu", "col"), P("clu", "col"))
    return jax.shard_map(
        per_device, mesh=mesh, in_specs=in_specs, out_specs=out_specs, check_vma=False
    )
```

```python
import functools

import jax
import jax.numpy as jnp
from jax import lax
from jax.experimental import pallas as pl
from jax.experimental.pallas import tpu as pltpu
from jax.sharding import PartitionSpec as P

CLUSTERS = 32
ROUNDS = 4
COLOURS = 4
COLS = 4
CAM = 576
SHARE = 144
WIDE = 640
SLOT = 256
SPARE = WIDE - CAM
TABLE = 2 * SHARE
GROUP = 8
TRK = 1024
NT = (((1,), (1,)), ((), ()))
NN = (((1,), (0,)), ((), ()))

MY_COLOUR, PARTNER, PARTNER_COLOUR = 0, 1, 5
LANES = 128

F32 = jnp.float32
BF16 = jnp.bfloat16


def smem():
    return pl.BlockSpec(memory_space=pltpu.SMEM)


def vmem():
    return pl.BlockSpec(memory_space=pltpu.VMEM)


def two_parts(v):
    high = v.astype(BF16)
    low = (v - high.astype(F32)).astype(BF16)
    return high, low


def widen(v, width=WIDE):
    return jnp.concatenate([v, jnp.zeros((v.shape[0], width - v.shape[1]), F32)], 1)


def place_share(share, col):
    total = jnp.zeros((1, WIDE), F32)
    for at in range(COLS):
        pieces = []
        if at:
            pieces.append(jnp.zeros((1, SHARE * at), F32))
        pieces.append(share)
        pieces.append(jnp.zeros((1, WIDE - SHARE * (at + 1)), F32))
        total = total + jnp.where(col == at, jnp.concatenate(pieces, 1), 0.0)
    return total


def take_share(vector, col):
    total = jnp.zeros((1, SHARE), F32)
    for at in range(COLS):
        total = total + jnp.where(col == at, vector[:, SHARE * at : SHARE * (at + 1)], 0.0)
    return total


def members(dest_ref):
    lanes = lax.broadcasted_iota(jnp.int32, (CLUSTERS, TRK), 0)
    return (lanes == dest_ref[...]).astype(F32)


def scatter_rows(onehot, row):
    high, low = two_parts(row)
    return jnp.concatenate(
        [onehot * high.astype(F32), onehot * low.astype(F32)], 0
    ).astype(BF16)


def fold(both):
    return both[:CLUSTERS] + both[CLUSTERS:]


def rhs_kernel(
    cc_hbm, rp_hbm, dest_hbm, obs_hbm, info_hbm, grad_hbm, cg_hbm, step_hbm, diag_hbm, jac_hbm,
    own_hbm, out_hbm, again_hbm,
    cc_ref, rp_ref, dest_ref, obs_ref, info_ref, grad_ref, cg_ref, step_ref, diag_ref, jac_ref,
    total, block_ref, out_ref, sems,
):
    sources = [dest_hbm, obs_hbm, info_hbm, grad_hbm, cg_hbm, step_hbm, diag_hbm, cc_hbm, rp_hbm]
    targets = [dest_ref, obs_ref, info_ref, grad_ref, cg_ref, step_ref, diag_ref, cc_ref, rp_ref]
    for a in range(3):
        sources.append(jac_hbm.at[CAM * a : CAM * (a + 1), :])
        targets.append(jac_ref.at[a])
    sources.append(own_hbm)
    targets.append(block_ref)
    copies = [
        pltpu.make_async_copy(source, target, sems.at[i])
        for i, (source, target) in enumerate(zip(sources, targets))
    ]
    for copy in copies:
        copy.start()
    me = lax.axis_index("clu")
    col = lax.axis_index("col")
    for copy in copies[:7]:
        copy.wait()
    onehot = members(dest_ref)
    obs = obs_ref[...].astype(F32)
    part = jnp.zeros((2 * CLUSTERS, CAM), F32)
    for a in range(3):
        q = jnp.zeros((1, TRK), F32)
        for b in range(3):
            q = q + obs * info_ref[a, b : b + 1, :] * grad_ref[b : b + 1, :]
        spread = scatter_rows(onehot, q)
        copies[9 + a].wait()
        part = part + lax.dot_general(spread, jac_ref[a], NT, preferred_element_type=F32)
    rows = lax.broadcasted_iota(jnp.int32, (CLUSTERS, WIDE), 0)
    total[...] = jnp.where(rows == me, place_share(cg_ref[...], col), 0.0) - widen(fold(part))
    copies[7].wait()
    copies[8].wait()
    copies[12].wait()
    back = pltpu.make_async_copy(block_ref, again_hbm, sems.at[13])
    back.start()
    spare = jnp.concatenate(
        [step_ref[...], diag_ref[...], jnp.zeros((1, 5 * SPARE - 2 * SHARE), F32)], 1
    )
    empty = jnp.zeros((1, CAM), F32)
    tails = [
        jnp.concatenate([empty, spare[:, SPARE * v : SPARE * (v + 1)]], 1) for v in range(5)
    ]
    lanes = lax.broadcasted_iota(jnp.int32, (1, WIDE), 1) - (CAM + TABLE % SPARE)
    outs = []
    for c in range(CLUSTERS):
        colour = cc_ref[c]
        sources = [c] + [rp_ref[colour, r, c] for r in range(ROUNDS)]
        last = jnp.where(lanes == MY_COLOUR, colour.astype(F32), tails[4])
        for r, p in enumerate(sources[1:]):
            last = jnp.where(lanes == PARTNER + r, p.astype(F32), last)
            last = jnp.where(lanes == PARTNER_COLOUR + r, cc_ref[p].astype(F32), last)
        for v, p in enumerate(sources):
            tail = last if v == 4 else tails[v]
            out_ref[c, :, WIDE * v : WIDE * (v + 1)] = total[pl.ds(p, 1), :] + tail
        if c % GROUP == GROUP - 1:
            rows = pl.ds(c + 1 - GROUP, GROUP)
            outs.append(
                pltpu.make_async_copy(
                    out_ref.at[rows], out_hbm.at[rows], sems.at[14 + c // GROUP]
                )
            )
            outs[-1].start()
    for copy in outs:
        copy.wait()
    back.wait()


def gather_kernel(recv_ref, ready_ref, out_ref, ids_ref):
    del ready_ref
    vectors = recv_ref[0]
    for c in range(1, CLUSTERS):
        vectors = vectors + recv_ref[c]
    out_ref[:, : WIDE * 5] = vectors

    def spare(c):
        return jnp.concatenate(
            [recv_ref[c, :, WIDE * (v + 1) - SPARE : WIDE * (v + 1)] for v in range(5)], 1
        )

    me = lax.axis_index("clu")
    mine = spare(me)
    table = mine[:, TABLE:].astype(jnp.int32)
    ids_ref[...] = jnp.concatenate(
        [table, jnp.zeros((1, LANES - table.shape[1]), jnp.int32)], 1
    )
    shares = [mine[:, :SHARE]]
    shares += [spare(ids_ref[0, PARTNER + r])[:, :SHARE] for r in range(ROUNDS)]
    shares.append(mine[:, SHARE:TABLE])
    for at, share in enumerate(shares):
        out_ref[:, WIDE * 5 + SLOT * at : WIDE * 5 + SLOT * (at + 1)] = widen(share, SLOT)


def three_parts(vectors):
    row = jnp.concatenate(vectors, 1)
    high = row.astype(BF16).astype(F32)
    middle = (row - high).astype(BF16).astype(F32)
    low = row - high - middle
    parts = [high, middle, low, jnp.zeros((13, ROUNDS * WIDE), F32)]
    return jnp.concatenate(parts, 0).astype(BF16)


def couple(vectors, blocks_ref, begin=0, end=CAM):
    blocks = blocks_ref[:, :, begin:end].reshape(ROUNDS * WIDE, end - begin)
    out = jnp.dot(three_parts(vectors), blocks, preferred_element_type=F32)
    return jnp.sum(out, 0, keepdims=True)


def lay_out_kernel(*refs):
    pieces, blocks_ref, sems = refs[:COLS], refs[COLS], refs[COLS + 1]
    col, core = lax.axis_index("col"), lax.rem(lax.axis_index("clu"), 2)
    copies = []
    for i, (piece, away) in enumerate(zip(pieces, (0, 1 + 2 * core, 2, 3 - 2 * core))):
        at = pl.multiple_of(jnp.bitwise_xor(col, away) * SHARE, 16)
        copies.append(
            pltpu.make_async_copy(piece, blocks_ref.at[:, pl.ds(at, SHARE), :], sems.at[i])
        )
        copies[i].start()
    blocks_ref[:, CAM:, :] = jnp.zeros((ROUNDS, WIDE - CAM, CAM), BF16)
    for copy in copies:
        copy.wait()


def first_step_kernel(
    ids_ref, v0, v1, v2, v3, blocks_ref, state_ref, out_ref, rhs_ref
):
    col = lax.axis_index("col")
    rows = [v[...] for v in (v0, v1, v2, v3)]
    vectors = (rows[0] + rows[1] + rows[2] + rows[3])[:, : WIDE * 5]
    shares = []
    for at in range(COLS):
        share = jnp.zeros((1, SLOT * 6), F32)
        for k in range(COLS):
            share = jnp.where(jnp.bitwise_xor(col, k) == at, rows[k][:, WIDE * 5 :], share)
        shares.append(share)

    def full(v):
        return widen(jnp.concatenate([s[:, SLOT * v : SLOT * v + SHARE] for s in shares], 1))

    rhs = vectors[:, :WIDE]
    step, diag = full(0), full(5)
    near = []
    for r in range(ROUNDS):
        x = full(r + 1) * vectors[:, WIDE * (r + 1) : WIDE * (r + 2)]
        near.append(jnp.where(ids_ref[0, PARTNER_COLOUR + r] == 0, x, 0.0))
    coupled = widen(couple(near, blocks_ref))
    mine = ids_ref[0, MY_COLOUR]
    x = jnp.where(mine == 0, step * rhs, jnp.where(mine == 1, step * (rhs - coupled), 0.0))
    state_ref[0:1, :] = x
    state_ref[1:2, :] = rhs
    state_ref[2:3, :] = step
    state_ref[3:4, :] = diag
    state_ref[4:8, :] = jnp.zeros((4, WIDE), F32)
    rhs_ref[...] = take_share(rhs, col)
    for c in range(CLUSTERS):
        out_ref[c] = x


def step_kernel(number, has_recv, *refs):
    ids_ref, recv_ref, state_ref, blocks_ref = refs[:4]
    tracks = refs[4:-2]
    new_ref, out_ref = refs[-2:]
    near = [recv_ref[ids_ref[0, PARTNER + r], :, :WIDE] for r in range(ROUNDS)]
    coupled = widen(couple(near, blocks_ref))
    x, rhs, step, diag, elim = (state_ref[i : i + 1, :] for i in range(5))
    mine = ids_ref[0, MY_COLOUR]
    if has_recv:
        total = recv_ref[0, :, WIDE:]
        for c in range(1, CLUSTERS):
            total = total + recv_ref[c, :, WIDE:]
        elim = jnp.where(mine >= (2 if number > COLOURS else 0), total, elim)
    if number == COLOURS:
        x, rhs, coupled = 0.25 * x, 0.25 * rhs, 0.25 * coupled
    resid = rhs - coupled
    if number >= COLOURS:
        resid = resid - diag * x + elim
    x = jnp.where(mine == number % COLOURS, x + step * resid, x)
    for i, v in enumerate((x, rhs, step, diag, elim)):
        new_ref[i : i + 1, :] = v
    if number == 2 * COLOURS - 2:
        x = jnp.where(mine == COLOURS - 1, x + step * (rhs - diag * x + elim), x)
    for c in range(out_ref.shape[0]):
        out_ref[c, :, :WIDE] = x
    if tracks:
        eliminate(recv_ref, out_ref, *tracks)


def last_step_kernel(ids_ref, recv_ref, state_ref, blocks_ref, out_ref):
    def total(c):
        v = recv_ref[COLS * c]
        for k in range(1, COLS):
            v = v + recv_ref[COLS * c + k]
        return v

    near = [total(ids_ref[0, PARTNER + r]) for r in range(ROUNDS)]
    x = total(lax.axis_index("clu"))
    col = lax.axis_index("col")
    for at in range(COLS):

        @pl.when(col == at)
        def _():
            begin = SHARE * at // LANES * LANES
            end = min(begin + 2 * LANES, CAM)
            coupled = couple(near, blocks_ref, begin, end)
            share = slice(SHARE * at - begin, SHARE * (at + 1) - begin)
            new = x[:, begin:end] - state_ref[2:3, begin:end] * coupled
            new = jnp.where(ids_ref[0, MY_COLOUR] == COLOURS - 1, new, x[:, begin:end])
            out_ref[...] = new[:, share]


def eliminate(recv_ref, out_ref, dest_ref, obs_ref, info_ref, jac_ref):
    onehot = members(dest_ref)
    obs = obs_ref[...].astype(F32)
    high, low = two_parts(recv_ref[:, 0, :CAM])
    both = jnp.concatenate([high, low], 0)
    along = []
    for b in range(3):
        every = lax.dot_general(
            both, jac_ref[CAM * b : CAM * (b + 1), :], NN, preferred_element_type=F32
        )
        along.append(jnp.sum(fold(every) * onehot, 0, keepdims=True))
    total = jnp.zeros((2 * CLUSTERS, CAM), F32)
    for a in range(3):
        u = jnp.zeros((1, TRK), F32)
        for b in range(3):
            u = u + obs * info_ref[a, b : b + 1, :] * along[b]
        total = total + lax.dot_general(
            scatter_rows(onehot, u),
            jac_ref[CAM * a : CAM * (a + 1), :],
            NT,
            preferred_element_type=F32,
        )
    out_ref[:, 0, WIDE:] = widen(fold(total))


def shape(*dims, dtype=F32):
    return jax.ShapeDtypeStruct(dims, dtype)


def per_device(
    track_dest, obs_count, track_jac, point_info, point_grad, camera_grad, camera_diag,
    step_scale, covis_blocks, cluster_colour, round_partner,
):
    dest = jnp.transpose(track_dest)
    obs = obs_count[None, :]
    jac = jnp.transpose(track_jac)
    own = jnp.transpose(covis_blocks[0], (0, 2, 1))

    def over_col(v):
        return [v] + [lax.ppermute(v, "col", [(i, i ^ k) for i in range(COLS)]) for k in (1, 3, 2)]

    def swap(v, even, odd):
        pairs = []
        for c in range(CLUSTERS):
            for i in range(COLS):
                pairs.append((COLS * c + i, COLS * c + (i ^ (odd if c % 2 else even))))
        return lax.ppermute(v, ("clu", "col"), pairs)

    near = swap(own, 1, 3)
    limit = pltpu.CompilerParams(vmem_limit_bytes=24 << 20)
    large = pltpu.CompilerParams(vmem_limit_bytes=56 << 20)

    payload, again = pl.pallas_call(
        rhs_kernel,
        in_specs=[pl.BlockSpec(memory_space=pl.ANY)] * 11,
        out_specs=[pl.BlockSpec(memory_space=pl.ANY)] * 2,
        out_shape=[
            shape(CLUSTERS, 1, 5 * WIDE), shape(ROUNDS, SHARE, CAM, dtype=BF16),
        ],
        scratch_shapes=[
            pltpu.SMEM((CLUSTERS,), jnp.int32),
            pltpu.SMEM((COLOURS, ROUNDS, CLUSTERS), jnp.int32),
            pltpu.VMEM((1, TRK), jnp.int32),
            pltpu.VMEM((1, TRK), jnp.int32),
            pltpu.VMEM((3, 3, TRK), F32),
            pltpu.VMEM((3, TRK), F32),
            pltpu.VMEM((1, SHARE), F32),
            pltpu.VMEM((1, SHARE), F32),
            pltpu.VMEM((1, SHARE), F32),
            pltpu.VMEM((3, CAM, TRK), BF16),
            pltpu.VMEM((CLUSTERS, WIDE), F32),
            pltpu.VMEM((ROUNDS, SHARE, CAM), BF16),
            pltpu.VMEM((CLUSTERS, 1, 5 * WIDE), F32),
            pltpu.SemaphoreType.DMA((14 + CLUSTERS // GROUP,)),
        ],
        compiler_params=large,
        name="rhs",
    )(
        cluster_colour, round_partner, dest, obs, point_info, point_grad,
        camera_grad, step_scale, camera_diag, jac, own,
    )
    other = swap(again, 3, 1)
    pieces = [own, near, swap(near, 3, 1), other]

    def over_clu(v):
        return lax.all_to_all(v, "clu", split_axis=0, concat_axis=0, tiled=True)

    recv = over_clu(payload)
    row, ids = pl.pallas_call(
        gather_kernel,
        in_specs=[vmem(), pl.BlockSpec(memory_space=pl.ANY)],
        out_specs=[vmem()] * 2,
        out_shape=[shape(1, 5 * WIDE + 6 * SLOT), shape(1, LANES, dtype=jnp.int32)],
        compiler_params=limit,
        cost_estimate=pl.CostEstimate(
            flops=6 * 10**9, bytes_accessed=1 << 19, transcendentals=0
        ),
        name="gather",
    )(recv, other)
    row, first, third, second = over_col(row)
    blocks = pl.pallas_call(
        lay_out_kernel,
        in_specs=[pl.BlockSpec(memory_space=pl.ANY)] * COLS,
        out_specs=vmem(),
        out_shape=shape(ROUNDS, WIDE, CAM, dtype=BF16),
        scratch_shapes=[pltpu.SemaphoreType.DMA((COLS,))],
        compiler_params=limit,
        name="lay_out",
    )(*pieces)
    state, payload, reduced_rhs = pl.pallas_call(
        first_step_kernel,
        in_specs=[vmem()] * 6,
        out_specs=[vmem()] * 3,
        out_shape=[shape(8, WIDE), shape(CLUSTERS, 1, WIDE), shape(1, SHARE)],
        compiler_params=limit,
        name="first_step",
    )(ids, row, first, second, third, blocks)

    def update(number, recv, state, has_send=False, has_recv=False):
        rows = CLUSTERS * COLS if number == 2 * COLOURS - 2 else CLUSTERS
        extra = (dest, obs, point_info, jac) if has_send else ()
        return pl.pallas_call(
            functools.partial(step_kernel, number, has_recv),
            in_specs=[vmem()] * (4 + len(extra)),
            out_specs=[vmem()] * 2,
            out_shape=[shape(8, WIDE), shape(rows, 1, 2 * WIDE if has_send else WIDE)],
            compiler_params=limit,
            name="step",
        )(ids, recv, state, blocks, *extra)

    recv = over_clu(payload)
    state, payload = update(2, recv, state, has_send=True)
    recv = over_clu(payload)
    state, payload = update(3, recv, state, has_recv=True)
    recv = over_clu(payload)
    state, payload = update(4, recv, state, has_send=True)
    recv = over_clu(payload)
    state, payload = update(5, recv, state, has_recv=True)
    recv = over_clu(payload)
    state, payload = update(6, recv, state)
    recv = lax.all_to_all(payload, ("clu", "col"), split_axis=0, concat_axis=0, tiled=True)
    solution = pl.pallas_call(
        last_step_kernel,
        in_specs=[vmem()] * 4,
        out_specs=vmem(),
        out_shape=shape(1, SHARE),
        compiler_params=limit,
        name="last_step",
    )(ids, recv, state, blocks)
    return solution, reduced_rhs


def solution(mesh):
    in_specs = (
        P(("clu", "col"), None),
        P(("clu", "col")),
        P(("clu", "col"), None),
        P(None, None, ("clu", "col")),
        P(None, ("clu", "col")),
        P("clu", "col"),
        P("clu", "col"),
        P("clu", "col"),
        P("clu", None, None, "col"),
        P(),
        P(),
    )
    out_specs = (P("clu", "col"), P("clu", "col"))
    return jax.shard_map(
        per_device, mesh=mesh, in_specs=in_specs, out_specs=out_specs, check_vma=False
    )
```

```python
import functools

import jax
import jax.numpy as jnp
from jax import lax
from jax.experimental import pallas as pl
from jax.experimental.pallas import tpu as pltpu
from jax.sharding import PartitionSpec as P

CLUSTERS = 32
ROUNDS = 4
COLOURS = 4
COLS = 4
CAM = 576
SHARE = 144
WIDE = 640
SLOT = 256
SPARE = WIDE - CAM
TABLE = 2 * SHARE
GROUP = 8
TRK = 1024
NT = (((1,), (1,)), ((), ()))
NN = (((1,), (0,)), ((), ()))

MY_COLOUR, PARTNER, PARTNER_COLOUR = 0, 1, 5
LANES = 128

F32 = jnp.float32
BF16 = jnp.bfloat16


def smem():
    return pl.BlockSpec(memory_space=pltpu.SMEM)


def vmem():
    return pl.BlockSpec(memory_space=pltpu.VMEM)


def two_parts(v):
    high = v.astype(BF16)
    low = (v - high.astype(F32)).astype(BF16)
    return high, low


def widen(v, width=WIDE):
    return jnp.concatenate([v, jnp.zeros((v.shape[0], width - v.shape[1]), F32)], 1)


def place_share(share, col):
    total = jnp.zeros((1, WIDE), F32)
    for at in range(COLS):
        pieces = []
        if at:
            pieces.append(jnp.zeros((1, SHARE * at), F32))
        pieces.append(share)
        pieces.append(jnp.zeros((1, WIDE - SHARE * (at + 1)), F32))
        total = total + jnp.where(col == at, jnp.concatenate(pieces, 1), 0.0)
    return total


def take_share(vector, col):
    total = jnp.zeros((1, SHARE), F32)
    for at in range(COLS):
        total = total + jnp.where(col == at, vector[:, SHARE * at : SHARE * (at + 1)], 0.0)
    return total


def members(dest_ref):
    lanes = lax.broadcasted_iota(jnp.int32, (CLUSTERS, TRK), 0)
    return (lanes == dest_ref[...]).astype(F32)


def scatter_rows(onehot, row):
    high, low = two_parts(row)
    return jnp.concatenate(
        [onehot * high.astype(F32), onehot * low.astype(F32)], 0
    ).astype(BF16)


def fold(both):
    return both[:CLUSTERS] + both[CLUSTERS:]


def rhs_kernel(
    cc_hbm, rp_hbm, dest_hbm, obs_hbm, info_hbm, grad_hbm, cg_hbm, step_hbm, diag_hbm, jac_hbm,
    own_hbm, out_hbm, again_hbm,
    cc_ref, rp_ref, dest_ref, obs_ref, info_ref, grad_ref, cg_ref, step_ref, diag_ref, jac_ref,
    total, block_ref, out_ref, sems,
):
    sources = [dest_hbm, obs_hbm, info_hbm, grad_hbm, cg_hbm, step_hbm, diag_hbm, cc_hbm, rp_hbm]
    targets = [dest_ref, obs_ref, info_ref, grad_ref, cg_ref, step_ref, diag_ref, cc_ref, rp_ref]
    for a in range(3):
        sources.append(jac_hbm.at[CAM * a : CAM * (a + 1), :])
        targets.append(jac_ref.at[a])
    sources.append(own_hbm)
    targets.append(block_ref)
    copies = [
        pltpu.make_async_copy(source, target, sems.at[i])
        for i, (source, target) in enumerate(zip(sources, targets))
    ]
    for copy in copies:
        copy.start()
    me = lax.axis_index("clu")
    col = lax.axis_index("col")
    for copy in copies[:7]:
        copy.wait()
    onehot = members(dest_ref)
    obs = obs_ref[...].astype(F32)
    part = jnp.zeros((2 * CLUSTERS, CAM), F32)
    for a in range(3):
        q = jnp.zeros((1, TRK), F32)
        for b in range(3):
            q = q + obs * info_ref[a, b : b + 1, :] * grad_ref[b : b + 1, :]
        spread = scatter_rows(onehot, q)
        copies[9 + a].wait()
        part = part + lax.dot_general(spread, jac_ref[a], NT, preferred_element_type=F32)
    rows = lax.broadcasted_iota(jnp.int32, (CLUSTERS, WIDE), 0)
    total[...] = jnp.where(rows == me, place_share(cg_ref[...], col), 0.0) - widen(fold(part))
    copies[7].wait()
    copies[8].wait()
    copies[12].wait()
    back = pltpu.make_async_copy(block_ref, again_hbm, sems.at[13])
    back.start()
    spare = jnp.concatenate(
        [step_ref[...], diag_ref[...], jnp.zeros((1, 5 * SPARE - 2 * SHARE), F32)], 1
    )
    empty = jnp.zeros((1, CAM), F32)
    tails = [
        jnp.concatenate([empty, spare[:, SPARE * v : SPARE * (v + 1)]], 1) for v in range(5)
    ]
    lanes = lax.broadcasted_iota(jnp.int32, (1, WIDE), 1) - (CAM + TABLE % SPARE)
    outs = []
    for c in range(CLUSTERS):
        colour = cc_ref[c]
        sources = [c] + [rp_ref[colour, r, c] for r in range(ROUNDS)]
        last = jnp.where(lanes == MY_COLOUR, colour.astype(F32), tails[4])
        for r, p in enumerate(sources[1:]):
            last = jnp.where(lanes == PARTNER + r, p.astype(F32), last)
            last = jnp.where(lanes == PARTNER_COLOUR + r, cc_ref[p].astype(F32), last)
        for v, p in enumerate(sources):
            tail = last if v == 4 else tails[v]
            out_ref[c, :, WIDE * v : WIDE * (v + 1)] = total[pl.ds(p, 1), :] + tail
        if c % GROUP == GROUP - 1:
            rows = pl.ds(c + 1 - GROUP, GROUP)
            outs.append(
                pltpu.make_async_copy(
                    out_ref.at[rows], out_hbm.at[rows], sems.at[14 + c // GROUP]
                )
            )
            outs[-1].start()
    for copy in outs:
        copy.wait()
    back.wait()


def gather_kernel(recv_ref, ready_ref, out_ref, ids_ref):
    del ready_ref
    vectors = recv_ref[0]
    for c in range(1, CLUSTERS):
        vectors = vectors + recv_ref[c]
    out_ref[:, : WIDE * 5] = vectors

    def spare(c):
        return jnp.concatenate(
            [recv_ref[c, :, WIDE * (v + 1) - SPARE : WIDE * (v + 1)] for v in range(5)], 1
        )

    me = lax.axis_index("clu")
    mine = spare(me)
    table = mine[:, TABLE:].astype(jnp.int32)
    ids_ref[...] = jnp.concatenate(
        [table, jnp.zeros((1, LANES - table.shape[1]), jnp.int32)], 1
    )
    shares = [mine[:, :SHARE]]
    shares += [spare(ids_ref[0, PARTNER + r])[:, :SHARE] for r in range(ROUNDS)]
    shares.append(mine[:, SHARE:TABLE])
    for at, share in enumerate(shares):
        out_ref[:, WIDE * 5 + SLOT * at : WIDE * 5 + SLOT * (at + 1)] = widen(share, SLOT)


def three_parts(vectors):
    row = jnp.concatenate(vectors, 1)
    high = row.astype(BF16).astype(F32)
    middle = (row - high).astype(BF16).astype(F32)
    low = row - high - middle
    parts = [high, middle, low, jnp.zeros((13, ROUNDS * WIDE), F32)]
    return jnp.concatenate(parts, 0).astype(BF16)


def couple(vectors, blocks_ref, begin=0, end=CAM):
    blocks = blocks_ref[:, :, begin:end].reshape(ROUNDS * WIDE, end - begin)
    out = jnp.dot(three_parts(vectors), blocks, preferred_element_type=F32)
    return jnp.sum(out, 0, keepdims=True)


def lay_out_kernel(*refs):
    pieces, blocks_ref, sems = refs[:COLS], refs[COLS], refs[COLS + 1]
    col, core = lax.axis_index("col"), lax.rem(lax.axis_index("clu"), 2)
    copies = []
    for i, (piece, away) in enumerate(zip(pieces, (0, 1 + 2 * core, 2, 3 - 2 * core))):
        at = pl.multiple_of(jnp.bitwise_xor(col, away) * SHARE, 16)
        copies.append(
            pltpu.make_async_copy(piece, blocks_ref.at[:, pl.ds(at, SHARE), :], sems.at[i])
        )
        copies[i].start()
    blocks_ref[:, CAM:, :] = jnp.zeros((ROUNDS, WIDE - CAM, CAM), BF16)
    for copy in copies:
        copy.wait()


def first_step_kernel(
    ids_ref, v0, v1, v2, v3, blocks_ref, state_ref, out_ref, rhs_ref
):
    col = lax.axis_index("col")
    rows = [v[...] for v in (v0, v1, v2, v3)]
    vectors = (rows[0] + rows[1] + rows[2] + rows[3])[:, : WIDE * 5]
    shares = []
    for at in range(COLS):
        share = jnp.zeros((1, SLOT * 6), F32)
        for k in range(COLS):
            share = jnp.where(jnp.bitwise_xor(col, k) == at, rows[k][:, WIDE * 5 :], share)
        shares.append(share)

    def full(v):
        return widen(jnp.concatenate([s[:, SLOT * v : SLOT * v + SHARE] for s in shares], 1))

    rhs = vectors[:, :WIDE]
    step, diag = full(0), full(5)
    near = []
    for r in range(ROUNDS):
        x = full(r + 1) * vectors[:, WIDE * (r + 1) : WIDE * (r + 2)]
        near.append(jnp.where(ids_ref[0, PARTNER_COLOUR + r] == 0, x, 0.0))
    coupled = widen(couple(near, blocks_ref))
    mine = ids_ref[0, MY_COLOUR]
    x = jnp.where(mine == 0, step * rhs, jnp.where(mine == 1, step * (rhs - coupled), 0.0))
    state_ref[0:1, :] = x
    state_ref[1:2, :] = rhs
    state_ref[2:3, :] = step
    state_ref[3:4, :] = diag
    state_ref[4:8, :] = jnp.zeros((4, WIDE), F32)
    rhs_ref[...] = take_share(rhs, col)
    for c in range(CLUSTERS):
        out_ref[c] = x


def step_kernel(number, has_recv, *refs):
    ids_ref, recv_ref, state_ref, blocks_ref = refs[:4]
    tracks = refs[4:-2]
    new_ref, out_ref = refs[-2:]
    near = [recv_ref[ids_ref[0, PARTNER + r], :, :WIDE] for r in range(ROUNDS)]
    coupled = widen(couple(near, blocks_ref))
    x, rhs, step, diag, elim = (state_ref[i : i + 1, :] for i in range(5))
    mine = ids_ref[0, MY_COLOUR]
    if has_recv:
        total = recv_ref[0, :, WIDE:]
        for c in range(1, CLUSTERS):
            total = total + recv_ref[c, :, WIDE:]
        elim = jnp.where(mine >= (2 if number > COLOURS else 0), total, elim)
    if number == COLOURS:
        x, rhs, coupled = 0.25 * x, 0.25 * rhs, 0.25 * coupled
    resid = rhs - coupled
    if number >= COLOURS:
        resid = resid - diag * x + elim
    x = jnp.where(mine == number % COLOURS, x + step * resid, x)
    for i, v in enumerate((x, rhs, step, diag, elim)):
        new_ref[i : i + 1, :] = v
    if number == 2 * COLOURS - 2:
        x = jnp.where(mine == COLOURS - 1, x + step * (rhs - diag * x + elim), x)
    for c in range(out_ref.shape[0]):
        out_ref[c, :, :WIDE] = x
    if tracks:
        eliminate(recv_ref, out_ref, *tracks)


def last_step_kernel(ids_ref, recv_ref, state_ref, blocks_ref, out_ref):
    def total(c):
        v = recv_ref[COLS * c]
        for k in range(1, COLS):
            v = v + recv_ref[COLS * c + k]
        return v

    near = [total(ids_ref[0, PARTNER + r]) for r in range(ROUNDS)]
    x = total(lax.axis_index("clu"))
    col = lax.axis_index("col")
    for at in range(COLS):

        @pl.when(col == at)
        def _():
            begin = SHARE * at // LANES * LANES
            end = min(begin + 2 * LANES, CAM)
            coupled = couple(near, blocks_ref, begin, end)
            share = slice(SHARE * at - begin, SHARE * (at + 1) - begin)
            new = x[:, begin:end] - state_ref[2:3, begin:end] * coupled
            new = jnp.where(ids_ref[0, MY_COLOUR] == COLOURS - 1, new, x[:, begin:end])
            out_ref[...] = new[:, share]


def eliminate(recv_ref, out_ref, dest_ref, obs_ref, info_ref, jac_ref):
    onehot = members(dest_ref)
    obs = obs_ref[...].astype(F32)
    high, low = two_parts(recv_ref[:, 0, :CAM])
    both = jnp.concatenate([high, low], 0)

    def along(lanes):
        sums = []
        for b in range(3):
            rows = jac_ref[CAM * b : CAM * (b + 1), lanes]
            every = lax.dot_general(both, rows, NN, preferred_element_type=F32)
            sums.append(jnp.sum(fold(every) * onehot[:, lanes], 0, keepdims=True))
        return sums

    halves = [slice(0, TRK // 2), slice(TRK // 2, TRK)]
    sums = along(halves[0])
    total = jnp.zeros((2 * CLUSTERS, CAM), F32)
    for i, lanes in enumerate(halves):
        later = along(halves[1]) if i == 0 else None
        for a in range(3):
            u = jnp.zeros((1, TRK // 2), F32)
            for b in range(3):
                u = u + obs[:, lanes] * info_ref[a, b : b + 1, lanes] * sums[b]
            total = total + lax.dot_general(
                scatter_rows(onehot[:, lanes], u),
                jac_ref[CAM * a : CAM * (a + 1), lanes],
                NT,
                preferred_element_type=F32,
            )
        sums = later
    out_ref[:, 0, WIDE:] = widen(fold(total))


def shape(*dims, dtype=F32):
    return jax.ShapeDtypeStruct(dims, dtype)


def per_device(
    track_dest, obs_count, track_jac, point_info, point_grad, camera_grad, camera_diag,
    step_scale, covis_blocks, cluster_colour, round_partner,
):
    dest = jnp.transpose(track_dest)
    obs = obs_count[None, :]
    jac = jnp.transpose(track_jac)
    own = jnp.transpose(covis_blocks[0], (0, 2, 1))

    def over_col(v):
        return [v] + [lax.ppermute(v, "col", [(i, i ^ k) for i in range(COLS)]) for k in (1, 3, 2)]

    def swap(v, even, odd):
        pairs = []
        for c in range(CLUSTERS):
            for i in range(COLS):
                pairs.append((COLS * c + i, COLS * c + (i ^ (odd if c % 2 else even))))
        return lax.ppermute(v, ("clu", "col"), pairs)

    near = swap(own, 1, 3)
    limit = pltpu.CompilerParams(vmem_limit_bytes=24 << 20)
    large = pltpu.CompilerParams(vmem_limit_bytes=56 << 20)

    payload, again = pl.pallas_call(
        rhs_kernel,
        in_specs=[pl.BlockSpec(memory_space=pl.ANY)] * 11,
        out_specs=[pl.BlockSpec(memory_space=pl.ANY)] * 2,
        out_shape=[
            shape(CLUSTERS, 1, 5 * WIDE), shape(ROUNDS, SHARE, CAM, dtype=BF16),
        ],
        scratch_shapes=[
            pltpu.SMEM((CLUSTERS,), jnp.int32),
            pltpu.SMEM((COLOURS, ROUNDS, CLUSTERS), jnp.int32),
            pltpu.VMEM((1, TRK), jnp.int32),
            pltpu.VMEM((1, TRK), jnp.int32),
            pltpu.VMEM((3, 3, TRK), F32),
            pltpu.VMEM((3, TRK), F32),
            pltpu.VMEM((1, SHARE), F32),
            pltpu.VMEM((1, SHARE), F32),
            pltpu.VMEM((1, SHARE), F32),
            pltpu.VMEM((3, CAM, TRK), BF16),
            pltpu.VMEM((CLUSTERS, WIDE), F32),
            pltpu.VMEM((ROUNDS, SHARE, CAM), BF16),
            pltpu.VMEM((CLUSTERS, 1, 5 * WIDE), F32),
            pltpu.SemaphoreType.DMA((14 + CLUSTERS // GROUP,)),
        ],
        compiler_params=large,
        name="rhs",
    )(
        cluster_colour, round_partner, dest, obs, point_info, point_grad,
        camera_grad, step_scale, camera_diag, jac, own,
    )
    other = swap(again, 3, 1)
    pieces = [own, near, swap(near, 3, 1), other]

    def over_clu(v):
        return lax.all_to_all(v, "clu", split_axis=0, concat_axis=0, tiled=True)

    recv = over_clu(payload)
    row, ids = pl.pallas_call(
        gather_kernel,
        in_specs=[vmem(), pl.BlockSpec(memory_space=pl.ANY)],
        out_specs=[vmem()] * 2,
        out_shape=[shape(1, 5 * WIDE + 6 * SLOT), shape(1, LANES, dtype=jnp.int32)],
        compiler_params=limit,
        cost_estimate=pl.CostEstimate(
            flops=6 * 10**9, bytes_accessed=1 << 19, transcendentals=0
        ),
        name="gather",
    )(recv, other)
    row, first, third, second = over_col(row)
    blocks = pl.pallas_call(
        lay_out_kernel,
        in_specs=[pl.BlockSpec(memory_space=pl.ANY)] * COLS,
        out_specs=vmem(),
        out_shape=shape(ROUNDS, WIDE, CAM, dtype=BF16),
        scratch_shapes=[pltpu.SemaphoreType.DMA((COLS,))],
        compiler_params=limit,
        name="lay_out",
    )(*pieces)
    state, payload, reduced_rhs = pl.pallas_call(
        first_step_kernel,
        in_specs=[vmem()] * 6,
        out_specs=[vmem()] * 3,
        out_shape=[shape(8, WIDE), shape(CLUSTERS, 1, WIDE), shape(1, SHARE)],
        compiler_params=limit,
        name="first_step",
    )(ids, row, first, second, third, blocks)

    def update(number, recv, state, has_send=False, has_recv=False):
        rows = CLUSTERS * COLS if number == 2 * COLOURS - 2 else CLUSTERS
        extra = (dest, obs, point_info, jac) if has_send else ()
        return pl.pallas_call(
            functools.partial(step_kernel, number, has_recv),
            in_specs=[vmem()] * (4 + len(extra)),
            out_specs=[vmem()] * 2,
            out_shape=[shape(8, WIDE), shape(rows, 1, 2 * WIDE if has_send else WIDE)],
            compiler_params=limit,
            name="step",
        )(ids, recv, state, blocks, *extra)

    recv = over_clu(payload)
    state, payload = update(2, recv, state, has_send=True)
    recv = over_clu(payload)
    state, payload = update(3, recv, state, has_recv=True)
    recv = over_clu(payload)
    state, payload = update(4, recv, state, has_send=True)
    recv = over_clu(payload)
    state, payload = update(5, recv, state, has_recv=True)
    recv = over_clu(payload)
    state, payload = update(6, recv, state)
    recv = lax.all_to_all(payload, ("clu", "col"), split_axis=0, concat_axis=0, tiled=True)
    solution = pl.pallas_call(
        last_step_kernel,
        in_specs=[vmem()] * 4,
        out_specs=vmem(),
        out_shape=shape(1, SHARE),
        compiler_params=limit,
        name="last_step",
    )(ids, recv, state, blocks)
    return solution, reduced_rhs


def solution(mesh):
    in_specs = (
        P(("clu", "col"), None),
        P(("clu", "col")),
        P(("clu", "col"), None),
        P(None, None, ("clu", "col")),
        P(None, ("clu", "col")),
        P("clu", "col"),
        P("clu", "col"),
        P("clu", "col"),
        P("clu", None, None, "col"),
        P(),
        P(),
    )
    out_specs = (P("clu", "col"), P("clu", "col"))
    return jax.shard_map(
        per_device, mesh=mesh, in_specs=in_specs, out_specs=out_specs, check_vma=False
    )
```

```python
import functools

import jax
import jax.numpy as jnp
from jax import lax
from jax.experimental import pallas as pl
from jax.experimental.pallas import tpu as pltpu
from jax.sharding import PartitionSpec as P

CLUSTERS = 32
ROUNDS = 4
COLOURS = 4
COLS = 4
CAM = 576
SHARE = 144
WIDE = 640
SLOT = 256
SPARE = WIDE - CAM
TABLE = 2 * SHARE
GROUP = 8
TRK = 1024
NT = (((1,), (1,)), ((), ()))
NN = (((1,), (0,)), ((), ()))

MY_COLOUR, PARTNER, PARTNER_COLOUR = 0, 1, 5
LANES = 128

F32 = jnp.float32
BF16 = jnp.bfloat16


def smem():
    return pl.BlockSpec(memory_space=pltpu.SMEM)


def vmem():
    return pl.BlockSpec(memory_space=pltpu.VMEM)


def two_parts(v):
    high = v.astype(BF16)
    low = (v - high.astype(F32)).astype(BF16)
    return high, low


def widen(v, width=WIDE):
    return jnp.concatenate([v, jnp.zeros((v.shape[0], width - v.shape[1]), F32)], 1)


def place_share(share, col):
    total = jnp.zeros((1, WIDE), F32)
    for at in range(COLS):
        pieces = []
        if at:
            pieces.append(jnp.zeros((1, SHARE * at), F32))
        pieces.append(share)
        pieces.append(jnp.zeros((1, WIDE - SHARE * (at + 1)), F32))
        total = total + jnp.where(col == at, jnp.concatenate(pieces, 1), 0.0)
    return total


def take_share(vector, col):
    total = jnp.zeros((1, SHARE), F32)
    for at in range(COLS):
        total = total + jnp.where(col == at, vector[:, SHARE * at : SHARE * (at + 1)], 0.0)
    return total


def members(dest_ref):
    lanes = lax.broadcasted_iota(jnp.int32, (CLUSTERS, TRK), 0)
    return (lanes == dest_ref[...]).astype(F32)


def scatter_rows(onehot, row):
    high, low = two_parts(row)
    return jnp.concatenate(
        [onehot * high.astype(F32), onehot * low.astype(F32)], 0
    ).astype(BF16)


def fold(both):
    return both[:CLUSTERS] + both[CLUSTERS:]


def rhs_kernel(
    cc_hbm, rp_hbm, dest_hbm, obs_hbm, info_hbm, grad_hbm, cg_hbm, step_hbm, diag_hbm, jac_hbm,
    own_hbm, out_hbm, again_hbm,
    cc_ref, rp_ref, dest_ref, obs_ref, info_ref, grad_ref, cg_ref, step_ref, diag_ref, jac_ref,
    total, block_ref, out_ref, sems,
):
    sources = [dest_hbm, obs_hbm, info_hbm, grad_hbm, cg_hbm, step_hbm, diag_hbm, cc_hbm, rp_hbm]
    targets = [dest_ref, obs_ref, info_ref, grad_ref, cg_ref, step_ref, diag_ref, cc_ref, rp_ref]
    for a in range(3):
        sources.append(jac_hbm.at[CAM * a : CAM * (a + 1), :])
        targets.append(jac_ref.at[a])
    sources.append(own_hbm)
    targets.append(block_ref)
    copies = [
        pltpu.make_async_copy(source, target, sems.at[i])
        for i, (source, target) in enumerate(zip(sources, targets))
    ]
    for copy in copies:
        copy.start()
    me = lax.axis_index("clu")
    col = lax.axis_index("col")
    for copy in copies[:7]:
        copy.wait()
    onehot = members(dest_ref)
    obs = obs_ref[...].astype(F32)
    part = jnp.zeros((2 * CLUSTERS, CAM), F32)
    for a in range(3):
        q = jnp.zeros((1, TRK), F32)
        for b in range(3):
            q = q + obs * info_ref[a, b : b + 1, :] * grad_ref[b : b + 1, :]
        spread = scatter_rows(onehot, q)
        copies[9 + a].wait()
        part = part + lax.dot_general(spread, jac_ref[a], NT, preferred_element_type=F32)
    rows = lax.broadcasted_iota(jnp.int32, (CLUSTERS, WIDE), 0)
    total[...] = jnp.where(rows == me, place_share(cg_ref[...], col), 0.0) - widen(fold(part))
    copies[7].wait()
    copies[8].wait()
    copies[12].wait()
    back = pltpu.make_async_copy(block_ref, again_hbm, sems.at[13])
    back.start()
    spare = jnp.concatenate(
        [step_ref[...], diag_ref[...], jnp.zeros((1, 5 * SPARE - 2 * SHARE), F32)], 1
    )
    empty = jnp.zeros((1, CAM), F32)
    tails = [
        jnp.concatenate([empty, spare[:, SPARE * v : SPARE * (v + 1)]], 1) for v in range(5)
    ]
    lanes = lax.broadcasted_iota(jnp.int32, (1, WIDE), 1) - (CAM + TABLE % SPARE)
    outs = []
    for c in range(CLUSTERS):
        colour = cc_ref[c]
        sources = [c] + [rp_ref[colour, r, c] for r in range(ROUNDS)]
        last = jnp.where(lanes == MY_COLOUR, colour.astype(F32), tails[4])
        for r, p in enumerate(sources[1:]):
            last = jnp.where(lanes == PARTNER + r, p.astype(F32), last)
            last = jnp.where(lanes == PARTNER_COLOUR + r, cc_ref[p].astype(F32), last)
        for v, p in enumerate(sources):
            tail = last if v == 4 else tails[v]
            out_ref[c, :, WIDE * v : WIDE * (v + 1)] = total[pl.ds(p, 1), :] + tail
        if c % GROUP == GROUP - 1:
            rows = pl.ds(c + 1 - GROUP, GROUP)
            outs.append(
                pltpu.make_async_copy(
                    out_ref.at[rows], out_hbm.at[rows], sems.at[14 + c // GROUP]
                )
            )
            outs[-1].start()
    for copy in outs:
        copy.wait()
    back.wait()


def gather_kernel(recv_ref, ready_ref, out_ref, ids_ref):
    del ready_ref
    vectors = recv_ref[0]
    for c in range(1, CLUSTERS):
        vectors = vectors + recv_ref[c]
    out_ref[:, : WIDE * 5] = vectors

    def spare(c):
        return jnp.concatenate(
            [recv_ref[c, :, WIDE * (v + 1) - SPARE : WIDE * (v + 1)] for v in range(5)], 1
        )

    me = lax.axis_index("clu")
    mine = spare(me)
    table = mine[:, TABLE:].astype(jnp.int32)
    ids_ref[...] = jnp.concatenate(
        [table, jnp.zeros((1, LANES - table.shape[1]), jnp.int32)], 1
    )
    shares = [mine[:, :SHARE]]
    shares += [spare(ids_ref[0, PARTNER + r])[:, :SHARE] for r in range(ROUNDS)]
    shares.append(mine[:, SHARE:TABLE])
    for at, share in enumerate(shares):
        out_ref[:, WIDE * 5 + SLOT * at : WIDE * 5 + SLOT * (at + 1)] = widen(share, SLOT)


def three_parts(vectors):
    row = jnp.concatenate(vectors, 1)
    high = row.astype(BF16).astype(F32)
    middle = (row - high).astype(BF16).astype(F32)
    low = row - high - middle
    parts = [high, middle, low, jnp.zeros((13, ROUNDS * WIDE), F32)]
    return jnp.concatenate(parts, 0).astype(BF16)


def couple(vectors, blocks_ref, begin=0, end=CAM):
    blocks = blocks_ref[:, :, begin:end].reshape(ROUNDS * WIDE, end - begin)
    out = jnp.dot(three_parts(vectors), blocks, preferred_element_type=F32)
    return jnp.sum(out, 0, keepdims=True)


def lay_out_kernel(*refs):
    pieces, blocks_ref, sems = refs[:COLS], refs[COLS], refs[COLS + 1]
    col, core = lax.axis_index("col"), lax.rem(lax.axis_index("clu"), 2)
    copies = []
    for i, (piece, away) in enumerate(zip(pieces, (0, 1 + 2 * core, 2, 3 - 2 * core))):
        at = pl.multiple_of(jnp.bitwise_xor(col, away) * SHARE, 16)
        copies.append(
            pltpu.make_async_copy(piece, blocks_ref.at[:, pl.ds(at, SHARE), :], sems.at[i])
        )
        copies[i].start()
    blocks_ref[:, CAM:, :] = jnp.zeros((ROUNDS, WIDE - CAM, CAM), BF16)
    for copy in copies:
        copy.wait()


def first_step_kernel(
    ids_ref, v0, v1, v2, v3, blocks_ref, state_ref, out_ref, rhs_ref
):
    col = lax.axis_index("col")
    rows = [v[...] for v in (v0, v1, v2, v3)]
    vectors = (rows[0] + rows[1] + rows[2] + rows[3])[:, : WIDE * 5]
    shares = []
    for at in range(COLS):
        share = jnp.zeros((1, SLOT * 6), F32)
        for k in range(COLS):
            share = jnp.where(jnp.bitwise_xor(col, k) == at, rows[k][:, WIDE * 5 :], share)
        shares.append(share)

    def full(v):
        return widen(jnp.concatenate([s[:, SLOT * v : SLOT * v + SHARE] for s in shares], 1))

    rhs = vectors[:, :WIDE]
    step, diag = full(0), full(5)
    near = []
    for r in range(ROUNDS):
        x = full(r + 1) * vectors[:, WIDE * (r + 1) : WIDE * (r + 2)]
        near.append(jnp.where(ids_ref[0, PARTNER_COLOUR + r] == 0, x, 0.0))
    coupled = widen(couple(near, blocks_ref))
    mine = ids_ref[0, MY_COLOUR]
    x = jnp.where(mine == 0, step * rhs, jnp.where(mine == 1, step * (rhs - coupled), 0.0))
    state_ref[0:1, :] = x
    state_ref[1:2, :] = rhs
    state_ref[2:3, :] = step
    state_ref[3:4, :] = diag
    state_ref[4:8, :] = jnp.zeros((4, WIDE), F32)
    rhs_ref[...] = take_share(rhs, col)
    for c in range(CLUSTERS):
        out_ref[c] = x


def step_kernel(number, has_recv, *refs):
    ids_ref, recv_ref, state_ref, blocks_ref = refs[:4]
    tracks = refs[4:-2]
    new_ref, out_ref = refs[-2:]
    if tracks:
        eliminate(recv_ref, out_ref, *tracks)
    near = [recv_ref[ids_ref[0, PARTNER + r], :, :WIDE] for r in range(ROUNDS)]
    coupled = widen(couple(near, blocks_ref))
    x, rhs, step, diag, elim = (state_ref[i : i + 1, :] for i in range(5))
    mine = ids_ref[0, MY_COLOUR]
    if has_recv:
        total = recv_ref[0, :, WIDE:]
        for c in range(1, CLUSTERS):
            total = total + recv_ref[c, :, WIDE:]
        elim = jnp.where(mine >= (2 if number > COLOURS else 0), total, elim)
    if number == COLOURS:
        x, rhs, coupled = 0.25 * x, 0.25 * rhs, 0.25 * coupled
    resid = rhs - coupled
    if number >= COLOURS:
        resid = resid - diag * x + elim
    x = jnp.where(mine == number % COLOURS, x + step * resid, x)
    for i, v in enumerate((x, rhs, step, diag, elim)):
        new_ref[i : i + 1, :] = v
    if number == 2 * COLOURS - 2:
        x = jnp.where(mine == COLOURS - 1, x + step * (rhs - diag * x + elim), x)
    for c in range(out_ref.shape[0]):
        out_ref[c, :, :WIDE] = x


def last_step_kernel(ids_ref, recv_ref, state_ref, blocks_ref, out_ref):
    def total(c):
        v = recv_ref[COLS * c]
        for k in range(1, COLS):
            v = v + recv_ref[COLS * c + k]
        return v

    near = [total(ids_ref[0, PARTNER + r]) for r in range(ROUNDS)]
    x = total(lax.axis_index("clu"))
    col = lax.axis_index("col")
    for at in range(COLS):

        @pl.when(col == at)
        def _():
            begin = SHARE * at // LANES * LANES
            end = min(begin + 2 * LANES, CAM)
            coupled = couple(near, blocks_ref, begin, end)
            share = slice(SHARE * at - begin, SHARE * (at + 1) - begin)
            new = x[:, begin:end] - state_ref[2:3, begin:end] * coupled
            new = jnp.where(ids_ref[0, MY_COLOUR] == COLOURS - 1, new, x[:, begin:end])
            out_ref[...] = new[:, share]


def eliminate(recv_ref, out_ref, dest_ref, obs_ref, info_ref, jac_ref):
    onehot = members(dest_ref)
    obs = obs_ref[...].astype(F32)
    high, low = two_parts(recv_ref[:, 0, :CAM])
    both = jnp.concatenate([high, low], 0)

    def along(lanes):
        sums = []
        for b in range(3):
            rows = jac_ref[CAM * b : CAM * (b + 1), lanes]
            every = lax.dot_general(both, rows, NN, preferred_element_type=F32)
            sums.append(jnp.sum(fold(every) * onehot[:, lanes], 0, keepdims=True))
        return sums

    halves = [slice(0, TRK // 2), slice(TRK // 2, TRK)]
    sums = along(halves[0])
    total = jnp.zeros((2 * CLUSTERS, CAM), F32)
    for i, lanes in enumerate(halves):
        later = along(halves[1]) if i == 0 else None
        for a in range(3):
            u = jnp.zeros((1, TRK // 2), F32)
            for b in range(3):
                u = u + obs[:, lanes] * info_ref[a, b : b + 1, lanes] * sums[b]
            total = total + lax.dot_general(
                scatter_rows(onehot[:, lanes], u),
                jac_ref[CAM * a : CAM * (a + 1), lanes],
                NT,
                preferred_element_type=F32,
            )
        sums = later
    out_ref[:, 0, WIDE:] = widen(fold(total))


def shape(*dims, dtype=F32):
    return jax.ShapeDtypeStruct(dims, dtype)


def per_device(
    track_dest, obs_count, track_jac, point_info, point_grad, camera_grad, camera_diag,
    step_scale, covis_blocks, cluster_colour, round_partner,
):
    dest = jnp.transpose(track_dest)
    obs = obs_count[None, :]
    jac = jnp.transpose(track_jac)
    own = jnp.transpose(covis_blocks[0], (0, 2, 1))

    def over_col(v):
        return [v] + [lax.ppermute(v, "col", [(i, i ^ k) for i in range(COLS)]) for k in (1, 3, 2)]

    def swap(v, even, odd):
        pairs = []
        for c in range(CLUSTERS):
            for i in range(COLS):
                pairs.append((COLS * c + i, COLS * c + (i ^ (odd if c % 2 else even))))
        return lax.ppermute(v, ("clu", "col"), pairs)

    near = swap(own, 1, 3)
    limit = pltpu.CompilerParams(vmem_limit_bytes=24 << 20)
    large = pltpu.CompilerParams(vmem_limit_bytes=56 << 20)

    payload, again = pl.pallas_call(
        rhs_kernel,
        in_specs=[pl.BlockSpec(memory_space=pl.ANY)] * 11,
        out_specs=[pl.BlockSpec(memory_space=pl.ANY)] * 2,
        out_shape=[
            shape(CLUSTERS, 1, 5 * WIDE), shape(ROUNDS, SHARE, CAM, dtype=BF16),
        ],
        scratch_shapes=[
            pltpu.SMEM((CLUSTERS,), jnp.int32),
            pltpu.SMEM((COLOURS, ROUNDS, CLUSTERS), jnp.int32),
            pltpu.VMEM((1, TRK), jnp.int32),
            pltpu.VMEM((1, TRK), jnp.int32),
            pltpu.VMEM((3, 3, TRK), F32),
            pltpu.VMEM((3, TRK), F32),
            pltpu.VMEM((1, SHARE), F32),
            pltpu.VMEM((1, SHARE), F32),
            pltpu.VMEM((1, SHARE), F32),
            pltpu.VMEM((3, CAM, TRK), BF16),
            pltpu.VMEM((CLUSTERS, WIDE), F32),
            pltpu.VMEM((ROUNDS, SHARE, CAM), BF16),
            pltpu.VMEM((CLUSTERS, 1, 5 * WIDE), F32),
            pltpu.SemaphoreType.DMA((14 + CLUSTERS // GROUP,)),
        ],
        compiler_params=large,
        name="rhs",
    )(
        cluster_colour, round_partner, dest, obs, point_info, point_grad,
        camera_grad, step_scale, camera_diag, jac, own,
    )
    other = swap(again, 3, 1)
    pieces = [own, near, swap(near, 3, 1), other]

    def over_clu(v):
        return lax.all_to_all(v, "clu", split_axis=0, concat_axis=0, tiled=True)

    recv = over_clu(payload)
    row, ids = pl.pallas_call(
        gather_kernel,
        in_specs=[vmem(), pl.BlockSpec(memory_space=pl.ANY)],
        out_specs=[vmem()] * 2,
        out_shape=[shape(1, 5 * WIDE + 6 * SLOT), shape(1, LANES, dtype=jnp.int32)],
        compiler_params=limit,
        cost_estimate=pl.CostEstimate(
            flops=6 * 10**9, bytes_accessed=1 << 19, transcendentals=0
        ),
        name="gather",
    )(recv, other)
    row, first, third, second = over_col(row)
    blocks = pl.pallas_call(
        lay_out_kernel,
        in_specs=[pl.BlockSpec(memory_space=pl.ANY)] * COLS,
        out_specs=vmem(),
        out_shape=shape(ROUNDS, WIDE, CAM, dtype=BF16),
        scratch_shapes=[pltpu.SemaphoreType.DMA((COLS,))],
        compiler_params=limit,
        name="lay_out",
    )(*pieces)
    state, payload, reduced_rhs = pl.pallas_call(
        first_step_kernel,
        in_specs=[vmem()] * 6,
        out_specs=[vmem()] * 3,
        out_shape=[shape(8, WIDE), shape(CLUSTERS, 1, WIDE), shape(1, SHARE)],
        compiler_params=limit,
        name="first_step",
    )(ids, row, first, second, third, blocks)

    def update(number, recv, state, has_send=False, has_recv=False):
        rows = CLUSTERS * COLS if number == 2 * COLOURS - 2 else CLUSTERS
        extra = (dest, obs, point_info, jac) if has_send else ()
        return pl.pallas_call(
            functools.partial(step_kernel, number, has_recv),
            in_specs=[vmem()] * (4 + len(extra)),
            out_specs=[vmem()] * 2,
            out_shape=[shape(8, WIDE), shape(rows, 1, 2 * WIDE if has_send else WIDE)],
            compiler_params=limit,
            name="step",
        )(ids, recv, state, blocks, *extra)

    recv = over_clu(payload)
    state, payload = update(2, recv, state, has_send=True)
    recv = over_clu(payload)
    state, payload = update(3, recv, state, has_recv=True)
    recv = over_clu(payload)
    state, payload = update(4, recv, state, has_send=True)
    recv = over_clu(payload)
    state, payload = update(5, recv, state, has_recv=True)
    recv = over_clu(payload)
    state, payload = update(6, recv, state)
    recv = lax.all_to_all(payload, ("clu", "col"), split_axis=0, concat_axis=0, tiled=True)
    solution = pl.pallas_call(
        last_step_kernel,
        in_specs=[vmem()] * 4,
        out_specs=vmem(),
        out_shape=shape(1, SHARE),
        compiler_params=limit,
        name="last_step",
    )(ids, recv, state, blocks)
    return solution, reduced_rhs


def solution(mesh):
    in_specs = (
        P(("clu", "col"), None),
        P(("clu", "col")),
        P(("clu", "col"), None),
        P(None, None, ("clu", "col")),
        P(None, ("clu", "col")),
        P("clu", "col"),
        P("clu", "col"),
        P("clu", "col"),
        P("clu", None, None, "col"),
        P(),
        P(),
    )
    out_specs = (P("clu", "col"), P("clu", "col"))
    return jax.shard_map(
        per_device, mesh=mesh, in_specs=in_specs, out_specs=out_specs, check_vma=False
    )
```

```python
import functools

import jax
import jax.numpy as jnp
from jax import lax
from jax.experimental import pallas as pl
from jax.experimental.pallas import tpu as pltpu
from jax.sharding import PartitionSpec as P

CLUSTERS = 32
ROUNDS = 4
COLOURS = 4
COLS = 4
CAM = 576
SHARE = 144
WIDE = 640
SLOT = 256
SPARE = WIDE - CAM
TABLE = 2 * SHARE
GROUP = 8
TRK = 1024
NT = (((1,), (1,)), ((), ()))
NN = (((1,), (0,)), ((), ()))

MY_COLOUR, PARTNER, PARTNER_COLOUR = 0, 1, 5
LANES = 128

F32 = jnp.float32
BF16 = jnp.bfloat16


def smem():
    return pl.BlockSpec(memory_space=pltpu.SMEM)


def vmem():
    return pl.BlockSpec(memory_space=pltpu.VMEM)


def two_parts(v):
    high = v.astype(BF16)
    low = (v - high.astype(F32)).astype(BF16)
    return high, low


def widen(v, width=WIDE):
    return jnp.concatenate([v, jnp.zeros((v.shape[0], width - v.shape[1]), F32)], 1)


def place_share(share, col):
    total = jnp.zeros((1, WIDE), F32)
    for at in range(COLS):
        pieces = []
        if at:
            pieces.append(jnp.zeros((1, SHARE * at), F32))
        pieces.append(share)
        pieces.append(jnp.zeros((1, WIDE - SHARE * (at + 1)), F32))
        total = total + jnp.where(col == at, jnp.concatenate(pieces, 1), 0.0)
    return total


def take_share(vector, col):
    total = jnp.zeros((1, SHARE), F32)
    for at in range(COLS):
        total = total + jnp.where(col == at, vector[:, SHARE * at : SHARE * (at + 1)], 0.0)
    return total


def members(dest_ref):
    lanes = lax.broadcasted_iota(jnp.int32, (CLUSTERS, TRK), 0)
    return (lanes == dest_ref[...]).astype(F32)


def scatter_rows(onehot, row):
    high, low = two_parts(row)
    return jnp.concatenate(
        [onehot * high.astype(F32), onehot * low.astype(F32)], 0
    ).astype(BF16)


def fold(both):
    return both[:CLUSTERS] + both[CLUSTERS:]


def rhs_kernel(
    cc_hbm, rp_hbm, dest_hbm, obs_hbm, info_hbm, grad_hbm, cg_hbm, step_hbm, diag_hbm, jac_hbm,
    own_hbm, out_hbm, again_hbm,
    cc_ref, rp_ref, dest_ref, obs_ref, info_ref, grad_ref, cg_ref, step_ref, diag_ref, jac_ref,
    total, block_ref, out_ref, sems,
):
    sources = [dest_hbm, obs_hbm, info_hbm, grad_hbm, cg_hbm, step_hbm, diag_hbm, cc_hbm, rp_hbm]
    targets = [dest_ref, obs_ref, info_ref, grad_ref, cg_ref, step_ref, diag_ref, cc_ref, rp_ref]
    for a in range(3):
        sources.append(jac_hbm.at[CAM * a : CAM * (a + 1), :])
        targets.append(jac_ref.at[a])
    sources.append(own_hbm)
    targets.append(block_ref)
    copies = [
        pltpu.make_async_copy(source, target, sems.at[i])
        for i, (source, target) in enumerate(zip(sources, targets))
    ]
    for copy in copies:
        copy.start()
    me = lax.axis_index("clu")
    col = lax.axis_index("col")
    for copy in copies[:7]:
        copy.wait()
    onehot = members(dest_ref)
    obs = obs_ref[...].astype(F32)
    part = jnp.zeros((2 * CLUSTERS, CAM), F32)
    for a in range(3):
        q = jnp.zeros((1, TRK), F32)
        for b in range(3):
            q = q + obs * info_ref[a, b : b + 1, :] * grad_ref[b : b + 1, :]
        spread = scatter_rows(onehot, q)
        copies[9 + a].wait()
        part = part + lax.dot_general(spread, jac_ref[a], NT, preferred_element_type=F32)
    rows = lax.broadcasted_iota(jnp.int32, (CLUSTERS, WIDE), 0)
    total[...] = jnp.where(rows == me, place_share(cg_ref[...], col), 0.0) - widen(fold(part))
    copies[7].wait()
    copies[8].wait()
    copies[12].wait()
    back = pltpu.make_async_copy(block_ref, again_hbm, sems.at[13])
    back.start()
    spare = jnp.concatenate(
        [step_ref[...], diag_ref[...], jnp.zeros((1, 5 * SPARE - 2 * SHARE), F32)], 1
    )
    empty = jnp.zeros((1, CAM), F32)
    tails = [
        jnp.concatenate([empty, spare[:, SPARE * v : SPARE * (v + 1)]], 1) for v in range(5)
    ]
    lanes = lax.broadcasted_iota(jnp.int32, (1, WIDE), 1) - (CAM + TABLE % SPARE)
    outs = []
    for c in range(CLUSTERS):
        colour = cc_ref[c]
        sources = [c] + [rp_ref[colour, r, c] for r in range(ROUNDS)]
        last = jnp.where(lanes == MY_COLOUR, colour.astype(F32), tails[4])
        for r, p in enumerate(sources[1:]):
            last = jnp.where(lanes == PARTNER + r, p.astype(F32), last)
            last = jnp.where(lanes == PARTNER_COLOUR + r, cc_ref[p].astype(F32), last)
        for v, p in enumerate(sources):
            tail = last if v == 4 else tails[v]
            out_ref[c, :, WIDE * v : WIDE * (v + 1)] = total[pl.ds(p, 1), :] + tail
        if c % GROUP == GROUP - 1:
            rows = pl.ds(c + 1 - GROUP, GROUP)
            outs.append(
                pltpu.make_async_copy(
                    out_ref.at[rows], out_hbm.at[rows], sems.at[14 + c // GROUP]
                )
            )
            outs[-1].start()
    for copy in outs:
        copy.wait()
    back.wait()


def gather_kernel(recv_ref, ready_ref, out_ref, ids_ref):
    del ready_ref
    vectors = recv_ref[0]
    for c in range(1, CLUSTERS):
        vectors = vectors + recv_ref[c]
    out_ref[:, : WIDE * 5] = vectors

    def spare(c):
        return jnp.concatenate(
            [recv_ref[c, :, WIDE * (v + 1) - SPARE : WIDE * (v + 1)] for v in range(5)], 1
        )

    me = lax.axis_index("clu")
    mine = spare(me)
    table = mine[:, TABLE:].astype(jnp.int32)
    ids_ref[...] = jnp.concatenate(
        [table, jnp.zeros((1, LANES - table.shape[1]), jnp.int32)], 1
    )
    shares = [mine[:, :SHARE]]
    shares += [spare(ids_ref[0, PARTNER + r])[:, :SHARE] for r in range(ROUNDS)]
    shares.append(mine[:, SHARE:TABLE])
    for at, share in enumerate(shares):
        out_ref[:, WIDE * 5 + SLOT * at : WIDE * 5 + SLOT * (at + 1)] = widen(share, SLOT)


def three_parts(vectors):
    row = jnp.concatenate([v[:, :CAM] for v in vectors], 1)
    high = row.astype(BF16).astype(F32)
    middle = (row - high).astype(BF16).astype(F32)
    low = row - high - middle
    parts = [high, middle, low, jnp.zeros((13, ROUNDS * CAM), F32)]
    return jnp.concatenate(parts, 0).astype(BF16)


def couple(vectors, blocks_ref, begin=0, end=CAM):
    blocks = blocks_ref[:, :, begin:end].reshape(ROUNDS * CAM, end - begin)
    out = jnp.dot(three_parts(vectors), blocks, preferred_element_type=F32)
    return jnp.sum(out, 0, keepdims=True)


def lay_out_kernel(*refs):
    pieces, blocks_ref, sems = refs[:COLS], refs[COLS], refs[COLS + 1]
    col, core = lax.axis_index("col"), lax.rem(lax.axis_index("clu"), 2)
    copies = []
    for i, (piece, away) in enumerate(zip(pieces, (0, 1 + 2 * core, 2, 3 - 2 * core))):
        at = pl.multiple_of(jnp.bitwise_xor(col, away) * SHARE, 16)
        copies.append(
            pltpu.make_async_copy(piece, blocks_ref.at[:, pl.ds(at, SHARE), :], sems.at[i])
        )
        copies[i].start()
    for copy in copies:
        copy.wait()


def first_step_kernel(
    ids_ref, v0, v1, v2, v3, blocks_ref, state_ref, out_ref, rhs_ref
):
    col = lax.axis_index("col")
    rows = [v[...] for v in (v0, v1, v2, v3)]
    vectors = (rows[0] + rows[1] + rows[2] + rows[3])[:, : WIDE * 5]
    shares = []
    for at in range(COLS):
        share = jnp.zeros((1, SLOT * 6), F32)
        for k in range(COLS):
            share = jnp.where(jnp.bitwise_xor(col, k) == at, rows[k][:, WIDE * 5 :], share)
        shares.append(share)

    def full(v):
        return widen(jnp.concatenate([s[:, SLOT * v : SLOT * v + SHARE] for s in shares], 1))

    rhs = vectors[:, :WIDE]
    step, diag = full(0), full(5)
    near = []
    for r in range(ROUNDS):
        x = full(r + 1) * vectors[:, WIDE * (r + 1) : WIDE * (r + 2)]
        near.append(jnp.where(ids_ref[0, PARTNER_COLOUR + r] == 0, x, 0.0))
    coupled = widen(couple(near, blocks_ref))
    mine = ids_ref[0, MY_COLOUR]
    x = jnp.where(mine == 0, step * rhs, jnp.where(mine == 1, step * (rhs - coupled), 0.0))
    state_ref[0:1, :] = x
    state_ref[1:2, :] = rhs
    state_ref[2:3, :] = step
    state_ref[3:4, :] = diag
    state_ref[4:8, :] = jnp.zeros((4, WIDE), F32)
    rhs_ref[...] = take_share(rhs, col)
    for c in range(CLUSTERS):
        out_ref[c] = x


def step_kernel(number, has_recv, *refs):
    ids_ref, recv_ref, state_ref, blocks_ref = refs[:4]
    tracks = refs[4:-2]
    new_ref, out_ref = refs[-2:]
    if tracks:
        eliminate(recv_ref, out_ref, *tracks)
    near = [recv_ref[ids_ref[0, PARTNER + r], :, :WIDE] for r in range(ROUNDS)]
    coupled = widen(couple(near, blocks_ref))
    x, rhs, step, diag, elim = (state_ref[i : i + 1, :] for i in range(5))
    mine = ids_ref[0, MY_COLOUR]
    if has_recv:
        total = recv_ref[0, :, WIDE:]
        for c in range(1, CLUSTERS):
            total = total + recv_ref[c, :, WIDE:]
        elim = jnp.where(mine >= (2 if number > COLOURS else 0), total, elim)
    if number == COLOURS:
        x, rhs, coupled = 0.25 * x, 0.25 * rhs, 0.25 * coupled
    resid = rhs - coupled
    if number >= COLOURS:
        resid = resid - diag * x + elim
    x = jnp.where(mine == number % COLOURS, x + step * resid, x)
    for i, v in enumerate((x, rhs, step, diag, elim)):
        new_ref[i : i + 1, :] = v
    if number == 2 * COLOURS - 2:
        x = jnp.where(mine == COLOURS - 1, x + step * (rhs - diag * x + elim), x)
    for c in range(out_ref.shape[0]):
        out_ref[c, :, :WIDE] = x


def last_step_kernel(ids_ref, recv_ref, state_ref, blocks_ref, out_ref):
    def total(c):
        v = recv_ref[COLS * c]
        for k in range(1, COLS):
            v = v + recv_ref[COLS * c + k]
        return v

    near = [total(ids_ref[0, PARTNER + r]) for r in range(ROUNDS)]
    x = total(lax.axis_index("clu"))
    col = lax.axis_index("col")
    for at in range(COLS):

        @pl.when(col == at)
        def _():
            begin = SHARE * at // LANES * LANES
            end = min(begin + 2 * LANES, CAM)
            coupled = couple(near, blocks_ref, begin, end)
            share = slice(SHARE * at - begin, SHARE * (at + 1) - begin)
            new = x[:, begin:end] - state_ref[2:3, begin:end] * coupled
            new = jnp.where(ids_ref[0, MY_COLOUR] == COLOURS - 1, new, x[:, begin:end])
            out_ref[...] = new[:, share]


def eliminate(recv_ref, out_ref, dest_ref, obs_ref, info_ref, jac_ref):
    onehot = members(dest_ref)
    obs = obs_ref[...].astype(F32)
    high, low = two_parts(recv_ref[:, 0, :CAM])
    both = jnp.concatenate([high, low], 0)

    def along(lanes):
        sums = []
        for b in range(3):
            rows = jac_ref[CAM * b : CAM * (b + 1), lanes]
            every = lax.dot_general(both, rows, NN, preferred_element_type=F32)
            sums.append(jnp.sum(fold(every) * onehot[:, lanes], 0, keepdims=True))
        return sums

    halves = [slice(0, TRK // 2), slice(TRK // 2, TRK)]
    sums = along(halves[0])
    total = jnp.zeros((2 * CLUSTERS, CAM), F32)
    for i, lanes in enumerate(halves):
        later = along(halves[1]) if i == 0 else None
        for a in range(3):
            u = jnp.zeros((1, TRK // 2), F32)
            for b in range(3):
                u = u + obs[:, lanes] * info_ref[a, b : b + 1, lanes] * sums[b]
            total = total + lax.dot_general(
                scatter_rows(onehot[:, lanes], u),
                jac_ref[CAM * a : CAM * (a + 1), lanes],
                NT,
                preferred_element_type=F32,
            )
        sums = later
    out_ref[:, 0, WIDE:] = widen(fold(total))


def shape(*dims, dtype=F32):
    return jax.ShapeDtypeStruct(dims, dtype)


def per_device(
    track_dest, obs_count, track_jac, point_info, point_grad, camera_grad, camera_diag,
    step_scale, covis_blocks, cluster_colour, round_partner,
):
    dest = jnp.transpose(track_dest)
    obs = obs_count[None, :]
    jac = jnp.transpose(track_jac)
    own = jnp.transpose(covis_blocks[0], (0, 2, 1))

    def over_col(v):
        return [v] + [lax.ppermute(v, "col", [(i, i ^ k) for i in range(COLS)]) for k in (1, 3, 2)]

    def swap(v, even, odd):
        pairs = []
        for c in range(CLUSTERS):
            for i in range(COLS):
                pairs.append((COLS * c + i, COLS * c + (i ^ (odd if c % 2 else even))))
        return lax.ppermute(v, ("clu", "col"), pairs)

    near = swap(own, 1, 3)
    limit = pltpu.CompilerParams(vmem_limit_bytes=24 << 20)
    large = pltpu.CompilerParams(vmem_limit_bytes=56 << 20)

    payload, again = pl.pallas_call(
        rhs_kernel,
        in_specs=[pl.BlockSpec(memory_space=pl.ANY)] * 11,
        out_specs=[pl.BlockSpec(memory_space=pl.ANY)] * 2,
        out_shape=[
            shape(CLUSTERS, 1, 5 * WIDE), shape(ROUNDS, SHARE, CAM, dtype=BF16),
        ],
        scratch_shapes=[
            pltpu.SMEM((CLUSTERS,), jnp.int32),
            pltpu.SMEM((COLOURS, ROUNDS, CLUSTERS), jnp.int32),
            pltpu.VMEM((1, TRK), jnp.int32),
            pltpu.VMEM((1, TRK), jnp.int32),
            pltpu.VMEM((3, 3, TRK), F32),
            pltpu.VMEM((3, TRK), F32),
            pltpu.VMEM((1, SHARE), F32),
            pltpu.VMEM((1, SHARE), F32),
            pltpu.VMEM((1, SHARE), F32),
            pltpu.VMEM((3, CAM, TRK), BF16),
            pltpu.VMEM((CLUSTERS, WIDE), F32),
            pltpu.VMEM((ROUNDS, SHARE, CAM), BF16),
            pltpu.VMEM((CLUSTERS, 1, 5 * WIDE), F32),
            pltpu.SemaphoreType.DMA((14 + CLUSTERS // GROUP,)),
        ],
        compiler_params=large,
        name="rhs",
    )(
        cluster_colour, round_partner, dest, obs, point_info, point_grad,
        camera_grad, step_scale, camera_diag, jac, own,
    )
    other = swap(again, 3, 1)
    pieces = [own, near, swap(near, 3, 1), other]

    def over_clu(v):
        return lax.all_to_all(v, "clu", split_axis=0, concat_axis=0, tiled=True)

    recv = over_clu(payload)
    row, ids = pl.pallas_call(
        gather_kernel,
        in_specs=[vmem(), pl.BlockSpec(memory_space=pl.ANY)],
        out_specs=[vmem()] * 2,
        out_shape=[shape(1, 5 * WIDE + 6 * SLOT), shape(1, LANES, dtype=jnp.int32)],
        compiler_params=limit,
        cost_estimate=pl.CostEstimate(
            flops=6 * 10**9, bytes_accessed=1 << 19, transcendentals=0
        ),
        name="gather",
    )(recv, other)
    row, first, third, second = over_col(row)
    blocks = pl.pallas_call(
        lay_out_kernel,
        in_specs=[pl.BlockSpec(memory_space=pl.ANY)] * COLS,
        out_specs=vmem(),
        out_shape=shape(ROUNDS, CAM, CAM, dtype=BF16),
        scratch_shapes=[pltpu.SemaphoreType.DMA((COLS,))],
        compiler_params=limit,
        name="lay_out",
    )(*pieces)
    state, payload, reduced_rhs = pl.pallas_call(
        first_step_kernel,
        in_specs=[vmem()] * 6,
        out_specs=[vmem()] * 3,
        out_shape=[shape(8, WIDE), shape(CLUSTERS, 1, WIDE), shape(1, SHARE)],
        compiler_params=limit,
        name="first_step",
    )(ids, row, first, second, third, blocks)

    def update(number, recv, state, has_send=False, has_recv=False):
        rows = CLUSTERS * COLS if number == 2 * COLOURS - 2 else CLUSTERS
        extra = (dest, obs, point_info, jac) if has_send else ()
        return pl.pallas_call(
            functools.partial(step_kernel, number, has_recv),
            in_specs=[vmem()] * (4 + len(extra)),
            out_specs=[vmem()] * 2,
            out_shape=[shape(8, WIDE), shape(rows, 1, 2 * WIDE if has_send else WIDE)],
            compiler_params=limit,
            name="step",
        )(ids, recv, state, blocks, *extra)

    recv = over_clu(payload)
    state, payload = update(2, recv, state, has_send=True)
    recv = over_clu(payload)
    state, payload = update(3, recv, state, has_recv=True)
    recv = over_clu(payload)
    state, payload = update(4, recv, state, has_send=True)
    recv = over_clu(payload)
    state, payload = update(5, recv, state, has_recv=True)
    recv = over_clu(payload)
    state, payload = update(6, recv, state)
    recv = lax.all_to_all(payload, ("clu", "col"), split_axis=0, concat_axis=0, tiled=True)
    solution = pl.pallas_call(
        last_step_kernel,
        in_specs=[vmem()] * 4,
        out_specs=vmem(),
        out_shape=shape(1, SHARE),
        compiler_params=limit,
        name="last_step",
    )(ids, recv, state, blocks)
    return solution, reduced_rhs


def solution(mesh):
    in_specs = (
        P(("clu", "col"), None),
        P(("clu", "col")),
        P(("clu", "col"), None),
        P(None, None, ("clu", "col")),
        P(None, ("clu", "col")),
        P("clu", "col"),
        P("clu", "col"),
        P("clu", "col"),
        P("clu", None, None, "col"),
        P(),
        P(),
    )
    out_specs = (P("clu", "col"), P("clu", "col"))
    return jax.shard_map(
        per_device, mesh=mesh, in_specs=in_specs, out_specs=out_specs, check_vma=False
    )
```
